32 devices in a mesh: seq: 4 (over x, core), shard: 8 (over z, y).
Axes of the slice: x: 2, y: 2, z: 4, core: 2. Of those that a mesh axis runs over, the one named last changes fastest.
Arguments:
- inputs: bfloat16 [16, 584, 1024], P('shard', 'seq'), may hold values from -6 to 6
- key_mask: int32 [16, 584], P('shard'), may hold values from 0 to 1, as said below
- cotangent: bfloat16 [16, 584, 1024], P('shard', 'seq'), may hold values from -6 to 6
- attn_gain: bfloat16 [1024], P('shard'), may hold values from 0.5 to 1.5
- attn_shift: bfloat16 [1024], P('shard'), may hold values from -1.796875 to 1.796875
- qkv_weight: bfloat16 [1024, 3072], P('shard'), may hold values from -0.1875 to 0.1875
- query_bias: bfloat16 [1024], P('shard'), may hold values from -1.796875 to 1.796875
- value_bias: bfloat16 [1024], P('shard'), may hold values from -1.796875 to 1.796875
- out_weight: bfloat16 [1024, 1024], P('shard'), may hold values from -2 to 2
- out_bias: bfloat16 [1024], P('shard'), may hold values from -1.796875 to 1.796875
- mlp_gain: bfloat16 [1024], P('shard'), may hold values from 0.5 to 1.5
- mlp_shift: bfloat16 [1024], P('shard'), may hold values from -1.796875 to 1.796875
- up_weight: bfloat16 [1024, 4096], P('shard'), may hold values from -0.1875 to 0.1875
- up_bias: bfloat16 [4096], P('shard'), may hold values from -1.796875 to 1.796875
- down_weight: bfloat16 [4096, 1024], P('shard'), may hold values from -0.125 to 0.125
- down_bias: bfloat16 [1024], P('shard'), may hold values from -1.796875 to 1.796875
Outputs:
- output: bfloat16 [16, 584, 1024], P('shard', 'seq')
- input_grad: bfloat16 [16, 584, 1024], P('shard', 'seq')
- grad_attn_gain: float32 [1024], P('shard')
- grad_attn_shift: float32 [1024], P('shard')
- grad_qkv_weight: float32 [1024, 3072], P('shard')
- grad_query_bias: float32 [1024], P('shard')
- grad_value_bias: float32 [1024], P('shard')
- grad_out_weight: float32 [1024, 1024], P('shard')
- grad_out_bias: float32 [1024], P('shard')
- grad_mlp_gain: float32 [1024], P('shard')
- grad_mlp_shift: float32 [1024], P('shard')
- grad_up_weight: float32 [1024, 4096], P('shard')
- grad_up_bias: float32 [4096], P('shard')
- grad_down_weight: float32 [4096, 1024], P('shard')
- grad_down_bias: float32 [1024], P('shard')
The draws below stay inside these ranges and needn't reach their ends.
Inputs may be any that keep to these rules, and one draw needn't show every extreme that they name: `key_mask`: each image has exactly 577 ones, at positions that differ from image to image.
All inputs are finite; a program needn't handle non-finite values.
Results may differ from the reference program's by a relative error of at most 0.02.
Values may be sent and summed in bfloat16 or wider, within the bound.
A program may use at most 192 MiB of HBM per device.

```python
import jax
import jax.numpy as jnp
from jax import lax

D = 1024
HEADS = 16
HEAD_DIM = 64
FF = 4096
SEQLEN = 584
VALID = 577
IMG_DEV = 2
IMAGES = 16
N_SHARD = 8


def draw_key_mask(key, part):
    row_keys = jax.random.split(key, IMAGES)

    def one_order(row_key):
        return jax.random.permutation(row_key, SEQLEN)
    orders = jax.vmap(one_order)(row_keys)
    places = jnp.argsort(orders, axis=-1, stable=True)
    return (places < VALID).astype(jnp.int32)


def block_scale(key, shape, cuts, least, largest):
    level = 1.0
    for axis_at, parts in cuts:
        steps = jax.random.uniform(jax.random.fold_in(jax.random.fold_in(key, 6), axis_at), (parts,), jnp.float32, least / len(cuts), largest / len(cuts))
        level = level * jnp.repeat(jnp.exp(steps), shape[axis_at] // parts).reshape((-1,) + (1,) * (len(shape) - 1 - axis_at))
    return level


def gaussian(own_key, dims, scale, most, shards=(), dtype=jnp.bfloat16):
    loudness = block_scale(own_key, dims, shards, -0.22, 0.18) if shards else 1.0
    values = jax.random.normal(own_key, dims, jnp.float32) * scale * loudness
    return jnp.minimum(jnp.maximum(values, -most), most).astype(dtype)


def setup_inputs(seed: int = 0) -> dict:
    keys = jax.random.split(jax.random.key(seed), 17)
    return {
        "inputs": gaussian(keys[0], (IMAGES, SEQLEN, D), 1.0, 6.0, ((0, 8), (1, 4))),
        "key_mask": draw_key_mask(jax.random.fold_in(keys[16], 71), 0),
        "cotangent": gaussian(keys[2], (IMAGES, SEQLEN, D), 1.0, 6.0, ((0, 8), (1, 4))),
        "attn_gain": jnp.clip(1.0 + 0.1 * jax.random.normal(keys[3], (D,), jnp.float32), 0.5, 1.5).astype(jnp.bfloat16),
        "attn_shift": gaussian(keys[4], (D,), 0.3, 1.796875, ((0, 8),)),
        "qkv_weight": gaussian(keys[5], (D, 3 * D), D ** -0.5, 0.1875, ((0, 8),)),
        "query_bias": gaussian(keys[6], (D,), 0.3, 1.796875, ((0, 8),)),
        "value_bias": gaussian(keys[7], (D,), 0.3, 1.796875, ((0, 8),)),
        "out_weight": gaussian(keys[8], (D, D), (D // 128) ** -0.5, 2.0, ((0, 8),)),
        "out_bias": gaussian(keys[9], (D,), 0.3, 1.796875, ((0, 8),)),
        "mlp_gain": jnp.clip(1.0 + 0.1 * jax.random.normal(keys[10], (D,), jnp.float32), 0.5, 1.5).astype(jnp.bfloat16),
        "mlp_shift": gaussian(keys[11], (D,), 0.3, 1.796875, ((0, 8),)),
        "up_weight": gaussian(keys[12], (D, FF), D ** -0.5, 0.1875, ((0, 8),)),
        "up_bias": gaussian(keys[13], (FF,), 0.3, 1.796875, ((0, 8),)),
        "down_weight": gaussian(keys[14], (FF, D), (FF // 2) ** -0.5, 0.125, ((0, 8),)),
        "down_bias": gaussian(keys[15], (D,), 0.3, 1.796875, ((0, 8),)),
    }


@jax.custom_vjp
def low(v):
    return lax.optimization_barrier(v.astype(jnp.bfloat16)).astype(jnp.float32)

@jax.custom_vjp
def low_back(v):
    return v

def low_keep(v):
    return (low(v), None)

def low_pass(kept, grad):
    return (grad,)

def back_keep(v):
    return (v, None)

def back_low(kept, grad):
    return (low(grad),)
low.defvjp(low_keep, low_pass)
low_back.defvjp(back_keep, back_low)
EPSILON = 1e-05
PRECISE = lax.Precision.HIGHEST

def norm_rows(current, gain, shift):
    centre = lax.optimization_barrier(jnp.mean(current, axis=-1, keepdims=True))
    centred = current - centre
    spread = lax.optimization_barrier(jnp.mean(centred * centred, axis=-1, keepdims=True))
    return centred * lax.rsqrt(spread + EPSILON) * gain + shift

def matmul(left, right):
    return jnp.matmul(left, right, precision=PRECISE)

def one_layer(current, keep_mask, params):
    attn_gain, attn_shift, qkv_weight, query_bias, value_bias, out_weight, out_bias, mlp_gain, mlp_shift, up_weight, up_bias, down_weight, down_bias = params
    images, length, width = current.shape
    packed_bias = jnp.concatenate([query_bias, jnp.zeros((width,), jnp.float32), value_bias])
    normed = low(norm_rows(current, attn_gain, attn_shift))
    packed = low_back(low(matmul(normed, qkv_weight) + packed_bias))
    packed = packed.reshape(images, length, 3, HEADS, HEAD_DIM)
    query = packed[:, :, 0]
    keyed = packed[:, :, 1]
    valued = packed[:, :, 2]
    scores = low_back(jnp.einsum('iqhd,ikhd->ihqk', query, keyed, precision=PRECISE) * HEAD_DIM ** (-0.5))
    scores = jnp.where(keep_mask[:, None, None, :] > 0, scores, -1e+30)
    probs = low(jax.nn.softmax(scores, axis=-1))
    mixed = jnp.einsum('ihqk,ikhd->iqhd', probs, valued, precision=PRECISE).reshape(images, length, width)
    mixed = low_back(low(mixed))
    branch = low_back(matmul(mixed, out_weight) + out_bias)
    middle = current + branch
    second = low(norm_rows(middle, mlp_gain, mlp_shift))
    hidden = low_back(matmul(second, up_weight) + up_bias)
    active = low(hidden * jax.nn.sigmoid(1.702 * hidden))
    return middle + low_back(matmul(active, down_weight) + down_bias)

def reference(inputs, key_mask, cotangent, attn_gain, attn_shift, qkv_weight, query_bias, value_bias, out_weight, out_bias, mlp_gain, mlp_shift, up_weight, up_bias, down_weight, down_bias):
    listed = (attn_gain, attn_shift, qkv_weight, query_bias, value_bias, out_weight, out_bias, mlp_gain, mlp_shift, up_weight, up_bias, down_weight, down_bias)
    params = [entry.astype(jnp.float32) for entry in listed]
    groups = N_SHARD
    starts = inputs.astype(jnp.float32).reshape(groups, IMG_DEV, SEQLEN, D)
    masks = key_mask.reshape(groups, IMG_DEV, SEQLEN)
    upstreams = cotangent.astype(jnp.float32).reshape(groups, IMG_DEV, SEQLEN, D) * masks[..., None].astype(jnp.float32)

    def step(totals, item):
        current, keep_mask, incoming = item
        result, pull = jax.vjp(lambda start, weights: one_layer(start, keep_mask, weights), current, params)
        d_current, d_weights = pull(incoming)
        totals = [left + right for left, right in zip(totals, d_weights)]
        return (totals, (result.astype(jnp.bfloat16), d_current.astype(jnp.bfloat16)))
    zeros = [jnp.zeros_like(entry) for entry in params]
    totals, (results, d_inputs) = lax.scan(step, zeros, (starts, masks, upstreams))
    output = results.reshape(IMAGES, SEQLEN, D)
    input_grad = d_inputs.reshape(IMAGES, SEQLEN, D)
    return (output, input_grad, totals[0], totals[1], totals[2], totals[3], totals[4], totals[5], totals[6], totals[7], totals[8], totals[9], totals[10], totals[11], totals[12])
```

```python
import jax
import jax.numpy as jnp
from jax import lax
from jax.experimental import pallas as pl
from jax.experimental.pallas import tpu as pltpu
from jax.sharding import PartitionSpec as P

D = 1024
HEAD_DIM = 64


EPSILON = 1e-05


def product(left, right):
    return jnp.dot(left, right, preferred_element_type=jnp.float32)


def product_tn(left, right):
    return lax.dot_general(
        left, right, (((0,), (0,)), ((), ())), preferred_element_type=jnp.float32
    )


def product_nt(left, right):
    return lax.dot_general(
        left, right, (((1,), (1,)), ((), ())), preferred_element_type=jnp.float32
    )


def norm_rows(current, gain, shift):
    centre = jnp.mean(current, axis=-1, keepdims=True)
    centred = current - centre
    inverse = lax.rsqrt(jnp.mean(centred * centred, axis=-1, keepdims=True) + EPSILON)
    scaled = centred * inverse
    return (scaled * gain + shift, scaled, inverse)


def norm_back(incoming, scaled, inverse, gain):
    inner = incoming * gain
    d_current = inverse * (
        inner
        - jnp.mean(inner, axis=-1, keepdims=True)
        - scaled * jnp.mean(inner * scaled, axis=-1, keepdims=True)
    )
    return (d_current, jnp.sum(incoming * scaled, axis=0), jnp.sum(incoming, axis=0))


def split_heads(block):
    images, length, width = block.shape
    return block.reshape(images, length, width // HEAD_DIM, HEAD_DIM)


def masked_scores(query_h, keyed_h, key_mask):
    scores = jnp.einsum("iqhd,ikhd->ihqk", query_h, keyed_h, preferred_element_type=jnp.float32)
    scores = scores * HEAD_DIM ** (-0.5)
    return jnp.where(key_mask[:, None, None, :] > 0, scores, -1e30)


def layer_forward(current, key_mask, weights, images):
    (
        attn_gain,
        attn_shift,
        qkv_weight,
        query_bias,
        value_bias,
        out_weight,
        out_bias,
        mlp_gain,
        mlp_shift,
        up_weight,
        up_bias,
        down_weight,
        down_bias,
    ) = weights
    row_count = current.shape[0]
    tok_local = row_count // images
    normed, scaled_a, inverse_a = norm_rows(
        current, attn_gain.astype(jnp.float32), attn_shift.astype(jnp.float32)
    )
    normed_low = normed.astype(jnp.bfloat16)
    packed_bias = jnp.concatenate(
        [
            query_bias.astype(jnp.float32),
            jnp.zeros((D,), jnp.float32),
            value_bias.astype(jnp.float32),
        ]
    )
    packed = (product(normed_low, qkv_weight) + packed_bias).astype(jnp.bfloat16)
    packed = packed.reshape(images, tok_local, 3, D)
    head_view = lax.all_to_all(packed, "seq", split_axis=3, concat_axis=1, tiled=True)
    query_h = split_heads(head_view[:, :, 0])
    keyed_h = split_heads(head_view[:, :, 1])
    value_h = split_heads(head_view[:, :, 2])
    scores = masked_scores(query_h, keyed_h, key_mask)
    row_max = jnp.max(scores, axis=-1, keepdims=True)
    raised = jnp.exp(scores - row_max)
    row_sum = jnp.sum(raised, axis=-1, keepdims=True)
    attn_probs = raised / row_sum
    log_total = row_max + jnp.log(row_sum)
    mixed = jnp.einsum(
        "ihqk,ikhd->iqhd",
        attn_probs.astype(jnp.bfloat16),
        value_h,
        preferred_element_type=jnp.float32,
    )
    seq_len = head_view.shape[1]
    mixed = mixed.reshape(images, seq_len, head_view.shape[3]).astype(jnp.bfloat16)
    merged = lax.all_to_all(mixed, "seq", split_axis=1, concat_axis=2, tiled=True)
    merged_rows = merged.reshape(row_count, D)
    middle = current + product(merged_rows, out_weight) + out_bias.astype(jnp.float32)
    second, scaled_b, inverse_b = norm_rows(
        middle, mlp_gain.astype(jnp.float32), mlp_shift.astype(jnp.float32)
    )
    second_low = second.astype(jnp.bfloat16)
    hidden = product(second_low, up_weight) + up_bias.astype(jnp.float32)
    active = (hidden * jax.nn.sigmoid(1.702 * hidden)).astype(jnp.bfloat16)
    result = middle + product(active, down_weight) + down_bias.astype(jnp.float32)
    stored = (
        scaled_a,
        inverse_a,
        normed_low,
        head_view,
        log_total,
        merged_rows,
        scaled_b,
        inverse_b,
        second_low,
        hidden,
        active,
    )
    return (result, stored)


def layer_backward(upstream, key_mask, weights, stored, images):
    (
        attn_gain,
        attn_shift,
        qkv_weight,
        query_bias,
        value_bias,
        out_weight,
        out_bias,
        mlp_gain,
        mlp_shift,
        up_weight,
        up_bias,
        down_weight,
        down_bias,
    ) = weights
    (
        scaled_a,
        inverse_a,
        normed_low,
        head_view,
        log_total,
        merged_rows,
        scaled_b,
        inverse_b,
        second_low,
        hidden,
        active,
    ) = stored
    row_count = upstream.shape[0]
    tok_local = row_count // images
    branch_low = upstream.astype(jnp.bfloat16)
    grad_down_bias = jnp.sum(branch_low, axis=0, dtype=jnp.float32)
    grad_down_weight = product_tn(active, branch_low)
    d_active = product_nt(branch_low, down_weight)
    gate_sig = jax.nn.sigmoid(1.702 * hidden)
    d_hidden = (d_active * (gate_sig + 1.702 * hidden * gate_sig * (1.0 - gate_sig))).astype(
        jnp.bfloat16
    )
    grad_up_bias = jnp.sum(d_hidden, axis=0, dtype=jnp.float32)
    grad_up_weight = product_tn(second_low, d_hidden)
    d_second = product_nt(d_hidden, up_weight)
    d_norm_b, grad_mlp_gain, grad_mlp_shift = norm_back(
        d_second, scaled_b, inverse_b, mlp_gain.astype(jnp.float32)
    )
    d_middle = upstream + d_norm_b
    d_branch = d_middle.astype(jnp.bfloat16)
    grad_out_bias = jnp.sum(d_branch, axis=0, dtype=jnp.float32)
    grad_out_weight = product_tn(merged_rows, d_branch)
    d_merged = product_nt(d_branch, out_weight).astype(jnp.bfloat16).reshape(images, tok_local, D)
    d_heads = lax.all_to_all(d_merged, "seq", split_axis=2, concat_axis=1, tiled=True)
    query_h = split_heads(head_view[:, :, 0])
    keyed_h = split_heads(head_view[:, :, 1])
    value_h = split_heads(head_view[:, :, 2])
    d_out_h = split_heads(d_heads)
    scores = masked_scores(query_h, keyed_h, key_mask)
    attn_probs = jnp.exp(scores - log_total)
    d_value = jnp.einsum(
        "ihqk,iqhd->ikhd",
        attn_probs.astype(jnp.bfloat16),
        d_out_h,
        preferred_element_type=jnp.float32,
    )
    d_probs = jnp.einsum("iqhd,ikhd->ihqk", d_out_h, value_h, preferred_element_type=jnp.float32)
    d_scores = attn_probs * (d_probs - jnp.sum(attn_probs * d_probs, axis=-1, keepdims=True))
    d_scores = d_scores.astype(jnp.bfloat16)
    d_query = jnp.einsum(
        "ihqk,ikhd->iqhd", d_scores, keyed_h, preferred_element_type=jnp.float32
    ) * HEAD_DIM ** (-0.5)
    d_key = jnp.einsum(
        "ihqk,iqhd->ikhd", d_scores, query_h, preferred_element_type=jnp.float32
    ) * HEAD_DIM ** (-0.5)
    seq_len = head_view.shape[1]
    d_packed = jnp.stack((d_query, d_key, d_value), axis=2).astype(jnp.bfloat16)
    d_packed = d_packed.reshape(images, seq_len, 3, head_view.shape[3])
    d_tokens = lax.all_to_all(d_packed, "seq", split_axis=1, concat_axis=3, tiled=True).reshape(
        row_count, 3 * D
    )
    grad_query_bias = jnp.sum(d_tokens[:, :D], axis=0, dtype=jnp.float32)
    grad_value_bias = jnp.sum(d_tokens[:, 2 * D :], axis=0, dtype=jnp.float32)
    grad_qkv_weight = product_tn(normed_low, d_tokens)
    d_normed = product_nt(d_tokens, qkv_weight)
    d_norm_a, grad_attn_gain, grad_attn_shift = norm_back(
        d_normed, scaled_a, inverse_a, attn_gain.astype(jnp.float32)
    )
    grads = (
        grad_attn_gain,
        grad_attn_shift,
        grad_qkv_weight,
        grad_query_bias,
        grad_value_bias,
        grad_out_weight,
        grad_out_bias,
        grad_mlp_gain,
        grad_mlp_shift,
        grad_up_weight,
        grad_up_bias,
        grad_down_weight,
        grad_down_bias,
    )
    return (d_middle + d_norm_a, grads)


def reduce_grads(grads):
    shares = (
        lax.psum_scatter(
            grads[0].astype(jnp.bfloat16), "shard", scatter_dimension=0, tiled=True
        ).astype(jnp.float32),
        lax.psum_scatter(
            grads[1].astype(jnp.bfloat16), "shard", scatter_dimension=0, tiled=True
        ).astype(jnp.float32),
        lax.psum_scatter(
            grads[2].astype(jnp.bfloat16), "shard", scatter_dimension=0, tiled=True
        ).astype(jnp.float32),
        lax.psum_scatter(
            grads[3].astype(jnp.bfloat16), "shard", scatter_dimension=0, tiled=True
        ).astype(jnp.float32),
        lax.psum_scatter(
            grads[4].astype(jnp.bfloat16), "shard", scatter_dimension=0, tiled=True
        ).astype(jnp.float32),
        lax.psum_scatter(
            grads[5].astype(jnp.bfloat16), "shard", scatter_dimension=0, tiled=True
        ).astype(jnp.float32),
        lax.psum_scatter(
            grads[6].astype(jnp.bfloat16), "shard", scatter_dimension=0, tiled=True
        ).astype(jnp.float32),
        lax.psum_scatter(
            grads[7].astype(jnp.bfloat16), "shard", scatter_dimension=0, tiled=True
        ).astype(jnp.float32),
        lax.psum_scatter(
            grads[8].astype(jnp.bfloat16), "shard", scatter_dimension=0, tiled=True
        ).astype(jnp.float32),
        lax.psum_scatter(
            grads[9].astype(jnp.bfloat16), "shard", scatter_dimension=0, tiled=True
        ).astype(jnp.float32),
        lax.psum_scatter(
            grads[10].astype(jnp.bfloat16), "shard", scatter_dimension=0, tiled=True
        ).astype(jnp.float32),
        lax.psum_scatter(
            grads[11].astype(jnp.bfloat16), "shard", scatter_dimension=0, tiled=True
        ).astype(jnp.float32),
        lax.psum_scatter(
            grads[12].astype(jnp.bfloat16), "shard", scatter_dimension=0, tiled=True
        ).astype(jnp.float32),
    )
    return (
        lax.psum(shares[0].astype(jnp.bfloat16), "seq").astype(jnp.float32),
        lax.psum(shares[1].astype(jnp.bfloat16), "seq").astype(jnp.float32),
        lax.psum(shares[2].astype(jnp.bfloat16), "seq").astype(jnp.float32),
        lax.psum(shares[3].astype(jnp.bfloat16), "seq").astype(jnp.float32),
        lax.psum(shares[4].astype(jnp.bfloat16), "seq").astype(jnp.float32),
        lax.psum(shares[5].astype(jnp.bfloat16), "seq").astype(jnp.float32),
        lax.psum(shares[6].astype(jnp.bfloat16), "seq").astype(jnp.float32),
        lax.psum(shares[7].astype(jnp.bfloat16), "seq").astype(jnp.float32),
        lax.psum(shares[8].astype(jnp.bfloat16), "seq").astype(jnp.float32),
        lax.psum(shares[9].astype(jnp.bfloat16), "seq").astype(jnp.float32),
        lax.psum(shares[10].astype(jnp.bfloat16), "seq").astype(jnp.float32),
        lax.psum(shares[11].astype(jnp.bfloat16), "seq").astype(jnp.float32),
        lax.psum(shares[12].astype(jnp.bfloat16), "seq").astype(jnp.float32),
    )


def per_device(
    inputs,
    key_mask,
    cotangent,
    attn_gain,
    attn_shift,
    qkv_weight,
    query_bias,
    value_bias,
    out_weight,
    out_bias,
    mlp_gain,
    mlp_shift,
    up_weight,
    up_bias,
    down_weight,
    down_bias,
):
    shard_set = (
        attn_gain,
        attn_shift,
        qkv_weight,
        query_bias,
        value_bias,
        out_weight,
        out_bias,
        mlp_gain,
        mlp_shift,
        up_weight,
        up_bias,
        down_weight,
        down_bias,
    )
    images = inputs.shape[0]
    tok_local = inputs.shape[1]
    row_count = images * tok_local
    current = inputs.astype(jnp.float32).reshape(row_count, D)
    gathered = (
        lax.all_gather(shard_set[0], "shard", axis=0, tiled=True),
        lax.all_gather(shard_set[1], "shard", axis=0, tiled=True),
        lax.all_gather(shard_set[2], "shard", axis=0, tiled=True),
        lax.all_gather(shard_set[3], "shard", axis=0, tiled=True),
        lax.all_gather(shard_set[4], "shard", axis=0, tiled=True),
        lax.all_gather(shard_set[5], "shard", axis=0, tiled=True),
        lax.all_gather(shard_set[6], "shard", axis=0, tiled=True),
        lax.all_gather(shard_set[7], "shard", axis=0, tiled=True),
        lax.all_gather(shard_set[8], "shard", axis=0, tiled=True),
        lax.all_gather(shard_set[9], "shard", axis=0, tiled=True),
        lax.all_gather(shard_set[10], "shard", axis=0, tiled=True),
        lax.all_gather(shard_set[11], "shard", axis=0, tiled=True),
        lax.all_gather(shard_set[12], "shard", axis=0, tiled=True),
    )
    result, stored = layer_forward(current, key_mask, gathered, images)
    output = result.astype(jnp.bfloat16).reshape(images, tok_local, D)
    start_row = lax.axis_index("seq") * tok_local
    own_mask = lax.dynamic_slice_in_dim(key_mask, start_row, tok_local, 1).astype(jnp.float32)
    upstream = (cotangent.astype(jnp.float32) * own_mask[:, :, None]).reshape(row_count, D)
    again = (
        lax.all_gather(shard_set[0], "shard", axis=0, tiled=True),
        lax.all_gather(shard_set[1], "shard", axis=0, tiled=True),
        lax.all_gather(shard_set[2], "shard", axis=0, tiled=True),
        lax.all_gather(shard_set[3], "shard", axis=0, tiled=True),
        lax.all_gather(shard_set[4], "shard", axis=0, tiled=True),
        lax.all_gather(shard_set[5], "shard", axis=0, tiled=True),
        lax.all_gather(shard_set[6], "shard", axis=0, tiled=True),
        lax.all_gather(shard_set[7], "shard", axis=0, tiled=True),
        lax.all_gather(shard_set[8], "shard", axis=0, tiled=True),
        lax.all_gather(shard_set[9], "shard", axis=0, tiled=True),
        lax.all_gather(shard_set[10], "shard", axis=0, tiled=True),
        lax.all_gather(shard_set[11], "shard", axis=0, tiled=True),
        lax.all_gather(shard_set[12], "shard", axis=0, tiled=True),
    )
    d_input, grads = layer_backward(upstream, key_mask, again, stored, images)
    reduced = reduce_grads(grads)
    input_grad = d_input.astype(jnp.bfloat16).reshape(images, tok_local, D)
    return (
        output,
        input_grad,
        reduced[0],
        reduced[1],
        reduced[2],
        reduced[3],
        reduced[4],
        reduced[5],
        reduced[6],
        reduced[7],
        reduced[8],
        reduced[9],
        reduced[10],
        reduced[11],
        reduced[12],
    )


NSEQ = 4
NSH = 8
TOK = 160
ROWS = NSEQ * TOK
HEADS_DEV = 4
MASKED = -1e30
VMEM_LIMIT = 64 * 1024 * 1024 - 1024 * 1024
MESH_ID = pl.DeviceIdType.MESH
BF = jnp.bfloat16
F32 = jnp.float32
GATE = 1.702


def dot_nn(left, right):
    return lax.dot_general(left, right, (((1,), (0,)), ((), ())), preferred_element_type=F32)


def dot_nt(left, right):
    return lax.dot_general(left, right, (((1,), (1,)), ((), ())), preferred_element_type=F32)


def dot_tn(left, right):
    return lax.dot_general(left, right, (((0,), (0,)), ((), ())), preferred_element_type=F32)


def layer_kernel(
    xin, dmin, bias, pack, wq_h, wo_h, wu_h, wd_h,
    out_o, dx_o, gq_o, go_o, gu_o, gd_o, sg_o,
    xg, wq, wo, wu, wd, pg, qkv, dqkv, probs, mixt, mixed, part, rc, rx, rc2, rx2,
    hid, cg, act, gate, dmg, dhid, dmix,
    gq, go, gu, gd, ryq, ryo, ryu, ryd, rzq, rzo, rzu, rzd, sgs, sg1, sg2,
    ssem, rsem, lsem,
):
    s = lax.axis_index("seq")
    j = lax.axis_index("shard")
    x, k = s // 2, s % 2
    z, y = j // 2, j % 2
    s_core = x * 2 + (1 - k)
    s_x = (1 - x) * 2 + k
    s_diag = (1 - x) * 2 + (1 - k)
    j_y = z * 2 + (1 - y)
    core = (s_core, j)
    xdev = (s_x, j)
    ydev = (s, j_y)

    def zj(d):
        return lax.rem(z + d, 4) * 2 + y

    ids = {}

    def ix(*key):
        return ids.setdefault(key, len(ids))

    pending = {}

    def send(tag, key, src, dst, dev):
        n = ix(*key)
        copy = pltpu.make_async_remote_copy(
            src_ref=src, dst_ref=dst, send_sem=ssem.at[n], recv_sem=rsem.at[n],
            device_id=dev, device_id_type=MESH_ID)
        copy.start()
        pending.setdefault(tag, []).append(copy)

    def sent(tag):
        for copy in pending.pop(tag, []):
            copy.wait_send()

    def arrived(key, dst, dev):
        n = ix(*key)
        pltpu.make_async_remote_copy(
            src_ref=dst, dst_ref=dst, send_sem=ssem.at[n], recv_sem=rsem.at[n],
            device_id=dev, device_id_type=MESH_ID).wait_recv()

    local = {}

    def load(key, src, dst):
        copy = pltpu.make_async_copy(src, dst, lsem.at[local.setdefault(key, len(local))])
        copy.start()
        return copy

    def rows(block):
        return pl.ds(pl.multiple_of(block * TOK, TOK), TOK)

    def tiles(count, step, body, init=None):
        def inner(t, carry):
            return body(pl.multiple_of(t * step, step), carry)
        return lax.fori_loop(0, count // step, inner, init)

    barrier = pltpu.get_barrier_semaphore()
    for d in range(1, NSEQ):
        pl.semaphore_signal(barrier, inc=1, device_id=(lax.rem(s + d, NSEQ), j), device_id_type=MESH_ID)
    for d in range(1, NSH):
        pl.semaphore_signal(barrier, inc=1, device_id=(s, lax.rem(j + d, NSH)), device_id_type=MESH_ID)
    loads_q = [load(("wq", c), wq_h.at[:, pl.ds(pl.multiple_of(1024 * c + 256 * s, 256), 256)],
                    wq.at[j, :, pl.ds(256 * c, 256)]) for c in range(3)]
    loads_u = [load(("wu", c), wu_h.at[:, pl.ds(pl.multiple_of(512 * c + 128 * s, 128), 128)],
                    wu.at[j, :, pl.ds(128 * c, 128)]) for c in range(8)]
    load_d = load(("wd",), wd_h.at[pl.ds(pl.multiple_of(128 * s, 128), 128)], wd.at[j])
    pg[j] = pack[...]
    pl.semaphore_wait(barrier, NSEQ - 1 + NSH - 1)

    def ag4_start(key, buf, i, src):
        send(key, (key, "c", i), src, buf.at[i, rows(s)], core)
        send(key, (key, "x", i), src, buf.at[i, rows(s)], xdev)

    def ag4_forward(key, buf, i):
        arrived((key, "x", i), buf.at[i, rows(s_x)], xdev)
        send(key + "f", (key, "d", i), buf.at[i, rows(s_x)], buf.at[i, rows(s_x)], core)

    def ag4_end(key, buf, i):
        arrived((key, "c", i), buf.at[i, rows(s_core)], core)
        arrived((key, "d", i), buf.at[i, rows(s_diag)], core)

    def agw_start(key, buf):
        send(key, (key, "y", 0), buf.at[j], buf.at[j], ydev)
        for d in (1, 2, 3):
            send(key, (key, "z", d), buf.at[j], buf.at[j], (s, zj(d)))

    def agw_forward(key, buf, d):
        jf = zj(4 - d)
        arrived((key, "z", d), buf.at[jf], (s, jf))
        send(key, (key, "y", d), buf.at[jf], buf.at[jf], ydev)

    def agw_end(key, buf):
        for d in (0, 1, 2, 3):
            jf = lax.rem(z + 4 - d, 4) * 2 + (1 - y)
            arrived((key, "y", d), buf.at[jf], ydev)

    def rs4_a(key, i, rcb):
        send(key, (key, "c0", i), part.at[i, rows(s_core)], rcb.at[i, 0], core)
        send(key, (key, "c1", i), part.at[i, rows(s_diag)], rcb.at[i, 1], core)

    def rs4_b(key, i, rcb, rxb):
        arrived((key, "c1", i), rcb.at[i, 1], core)

        def add(r, _):
            here = pl.ds(pl.multiple_of(s_x * TOK + r, 32), 32)
            total = part[i, here, :].astype(F32) + rcb[i, 1, pl.ds(r, 32), :].astype(F32)
            part[i, here, :] = total.astype(BF)
        tiles(TOK, 32, add)
        send(key, (key, "x", i), part.at[i, rows(s_x)], rxb.at[i], xdev)

    def rs4_wait(key, i, rcb, rxb):
        arrived((key, "c0", i), rcb.at[i, 0], core)
        arrived((key, "x", i), rxb.at[i], xdev)

    def rs4_sum(i, r, rcb, rxb):
        here = pl.ds(pl.multiple_of(s * TOK + r, 32), 32)
        return (part[i, here, :].astype(F32) + rcb[i, 0, pl.ds(r, 32), :].astype(F32)
                + rxb[i, pl.ds(r, 32), :].astype(F32))

    def add_into(g, row, others):
        def add(r, _):
            total = g[row, pl.ds(r, 32), :].astype(F32)
            for ref, at in others:
                total = total + ref[at, pl.ds(r, 32), :].astype(F32)
            g[row, pl.ds(r, 32), :] = total.astype(BF)
        tiles(128, 32, add)

    def rsw_start(key, g, ry):
        for d in (1, 2, 3, 0):
            send(key, (key, "gy", d), g.at[lax.rem(z + d, 4) * 2 + (1 - y)], ry.at[d], ydev)

    def rsw_mid(key, g, ry, rz):
        for d in (1, 2, 3, 0):
            arrived((key, "gy", d), ry.at[d], ydev)
            add_into(g, zj(d), [(ry, d)])
            if d:
                send(key, (key, "gz", d), g.at[zj(d)], rz.at[d - 1], (s, zj(d)))

    def rsw_end(key, g, rz, g_o):
        for d in (1, 2, 3):
            arrived((key, "gz", d), rz.at[d - 1], (s, zj(4 - d)))
        add_into(g, j, [(rz, 0), (rz, 1), (rz, 2)])
        copy = load((key, "go"), g.at[j], g_o.at[s])
        send(key, (key, "gc"), g.at[j], g_o.at[s], core)
        send(key, (key, "gx"), g.at[j], g_o.at[s], xdev)
        return copy

    def rsw_forward(key, g_o):
        arrived((key, "gx"), g_o.at[s_x], xdev)
        send(key, (key, "gd"), g_o.at[s_x], g_o.at[s_x], core)

    def rsw_done(key, g_o):
        arrived((key, "gc"), g_o.at[s_core], core)
        arrived((key, "gd"), g_o.at[s_diag], core)

    def param(p):
        return jnp.concatenate([pg[b, pl.ds(p, 1), :] for b in range(NSH)], axis=1)

    def head_param(p):
        return jnp.concatenate([pg[2 * s, pl.ds(p, 1), :], pg[2 * s + 1, pl.ds(p, 1), :]], axis=1)

    def normal(value):
        centre = jnp.mean(value, axis=-1, keepdims=True)
        centred = value - centre
        inverse = lax.rsqrt(jnp.mean(centred * centred, axis=-1, keepdims=True) + EPSILON)
        return centred * inverse, inverse

    def normal_back(incoming, scaled, inverse, gain):
        inner = incoming * gain
        return inverse * (inner - jnp.mean(inner, axis=-1, keepdims=True)
                          - scaled * jnp.mean(inner * scaled, axis=-1, keepdims=True))

    def fold(value):
        return value[0:8] + value[8:16] + value[16:24] + value[24:32]

    for i in range(2):
        ag4_start("xg", xg, i, xin.at[i])
    for d in range(1, NSH):
        send("pk", ("pk", d), pack, pg.at[j], (s, lax.rem(j + d, NSH)))
    for copy in loads_q:
        copy.wait()
    agw_start("wq", wq)
    for i in range(2):
        xg[i, rows(s), :] = xin[i]
        dmg[i, rows(s), :] = dmin[i]
    for d in range(1, NSH):
        jf = lax.rem(j + NSH - d, NSH)
        arrived(("pk", d), pg.at[jf], (s, jf))

    attn_gain, attn_shift = param(0), param(1)

    def norm_block(i, block):
        def body(r, _):
            here = pl.ds(pl.multiple_of(block * TOK + r, 32), 32)
            scaled, _inverse = normal(xg[i, here, :].astype(F32))
            xg[i, here, :] = (scaled * attn_gain + attn_shift).astype(BF)
        tiles(TOK, 32, body)

    norm_block(0, s)
    norm_block(1, s)
    ag4_forward("xg", xg, 0)
    agw_forward("wq", wq, 1)
    agw_forward("wq", wq, 2)
    ag4_forward("xg", xg, 1)
    agw_forward("wq", wq, 3)
    for copy in loads_u:
        copy.wait()
    load_d.wait()

    n_oz = [ix("woz", d) for d in (1, 2, 3)]

    def out_copy(d):
        return pltpu.make_async_remote_copy(
            src_ref=wo.at[y], dst_ref=wo.at[y], send_sem=ssem.at[n_oz[d - 1]], recv_sem=rsem.at[n_oz[0]],
            device_id=(s, zj(d)), device_id_type=MESH_ID)

    @pl.when(z == s)
    def _():
        copy = pltpu.make_async_copy(wo_h, wo.at[y], lsem.at[local.setdefault("wo", len(local))])
        copy.start()
        copy.wait()
        for d in (1, 2, 3):
            out_copy(d).start()

    agw_start("wu", wu)

    for i in range(2):
        ag4_end("xg", xg, i)
        sent("xgf")
        norm_block(i, s_core)
        norm_block(i, s_x)
        norm_block(i, s_diag)
    for i in range(2):
        ag4_start("dm", dmg, i, dmin.at[i])
    agw_end("wq", wq)

    @pl.when(z != s)
    def _():
        pltpu.make_async_remote_copy(
            src_ref=wo.at[y], dst_ref=wo.at[y], send_sem=ssem.at[n_oz[0]], recv_sem=rsem.at[n_oz[0]],
            device_id=(s, zj(1)), device_id_type=MESH_ID).wait_recv()
    send("wo", ("wo", "y"), wo.at[y], wo.at[y], ydev)

    packed_bias = jnp.concatenate([head_param(2), jnp.zeros((1, 256), F32), head_param(3)], axis=1)

    def attend(i):
        def project(r, _):
            here = pl.ds(r, 320)
            value = dot_nn(xg[i, here, :], wq[...].reshape(D, 768)) + packed_bias
            qkv[i, here, :] = value.astype(BF)
        tiles(ROWS, 320, project)
        value_t = qkv[i, :, 512:768].astype(F32).T.astype(BF)
        mixt[...] = value_t
        lane = lax.broadcasted_iota(jnp.int32, (1, 256), 1) // HEAD_DIM

        def one_head(h, _):
            keyed = jnp.where(lane == h, qkv[i, :, 256:512], jnp.zeros((), BF))
            query = qkv[i, :, 0:256] * jnp.asarray(HEAD_DIM ** -0.5, BF)
            scores = dot_nt(keyed, query) + bias[i, :, 0:1]
            raised = jnp.exp(scores - jnp.max(scores, axis=0, keepdims=True))
            chances = (raised * (1.0 / jnp.sum(raised, axis=0, keepdims=True))).astype(BF)
            probs[i, h] = chances
            here = pl.ds(pl.multiple_of(h * HEAD_DIM, HEAD_DIM), HEAD_DIM)
            mixt[here, :] = dot_nn(mixt[here, :], chances).astype(BF)
        lax.fori_loop(0, HEADS_DEV, one_head, None)
        mixed[i] = mixt[...].astype(F32).T.astype(BF)

    def project_out(i):
        def body(r, _):
            here = pl.ds(r, 320)
            part[i, here, :] = dot_nn(mixed[i, here, :], wo[...].reshape(256, D)).astype(BF)
        tiles(ROWS, 320, body)

    attend(0)
    agw_forward("wu", wu, 1)
    arrived(("wo", "y"), wo.at[1 - y], ydev)
    project_out(0)
    rs4_a("o", 0, rc)
    agw_forward("wu", wu, 2)
    agw_forward("wu", wu, 3)
    agw_start("wd", wd)
    rs4_b("o", 0, rc, rx)
    attend(1)
    project_out(1)
    rs4_a("o", 1, rc)
    rs4_b("o", 1, rc, rx)
    for i in range(2):
        ag4_forward("dm", dmg, i)

    out_bias, mlp_gain, mlp_shift, down_bias = param(4), param(5), param(6), param(7)
    up_bias = param(8)

    for i in range(2):
        rs4_wait("o", i, rc, rx)

        def middle(r, _, i=i):
            value = xin[i, pl.ds(r, 32), :].astype(F32) + (rs4_sum(i, r, rc, rx) + out_bias)
            hid[i, pl.ds(r, 32), :] = value
            scaled, _inverse = normal(value)
            here = pl.ds(pl.multiple_of(s * TOK + r, 32), 32)
            cg[i, here, :] = (scaled * mlp_gain + mlp_shift).astype(BF)
        tiles(TOK, 32, middle)
        ag4_start("c", cg, i, cg.at[i, rows(s)])
    agw_forward("wd", wd, 1)
    agw_forward("wd", wd, 2)
    agw_forward("wd", wd, 3)
    agw_end("wu", wu)
    for i in range(2):
        ag4_forward("c", cg, i)
        if i == 0:
            for n in range(2):
                ag4_end("dm", dmg, n)
        ag4_end("c", cg, i)

        def up(r, _, i=i):
            here = pl.ds(r, 320)
            value = dot_nn(cg[i, here, :], wu[...].reshape(D, D)) + up_bias
            sig = jax.nn.sigmoid(GATE * value)
            act[i, here, :] = (value * sig).astype(BF)
            gate[i, here, :] = (sig + GATE * value * sig * (1.0 - sig)).astype(BF)
        tiles(ROWS, 320, up)
    agw_end("wd", wd)
    sent("o")

    du_sum = jnp.zeros((8, D), F32)
    for i in range(2):
        def d_up(r, carry, i=i):
            here = pl.ds(r, 320)
            value = dot_nt(dmg[i, here, :], wd[...].reshape(D, D)) * gate[i, here, :].astype(F32)
            value = value.astype(BF)
            gate[i, here, :] = value
            return carry + jnp.sum(value.astype(F32).reshape(40, 8, D), axis=0)
        du_sum = tiles(ROWS, 320, d_up, du_sum)

    def weight_grad(left, right, g):
        def body(t, _):
            cols = pl.ds(pl.multiple_of(t * 256, 256), 256)
            value = dot_tn(left[:, :, cols].reshape(2 * ROWS, 256), right[...].reshape(2 * ROWS, right.shape[2]))
            g[pl.ds(2 * t, 2)] = value.astype(BF).reshape(2, 128, right.shape[2])
        lax.fori_loop(0, left.shape[2] // 256, body, None)

    sent("dmf")
    sent("dm")
    weight_grad(act, dmg, gd)
    rsw_start("d", gd, ryd)

    def d_second(i):
        def body(r, _):
            here = pl.ds(r, 320)
            part[i, here, :] = dot_nt(gate[i, here, :], wu[...].reshape(D, D)).astype(BF)
        tiles(ROWS, 320, body)
    for i in range(2):
        d_second(i)
        rs4_a("dc", i, rc)
    rs4_b("dc", 0, rc, rx)
    rs4_b("dc", 1, rc, rx)
    weight_grad(cg, gate, gu)
    rsw_start("u", gu, ryu)

    zero8 = jnp.zeros((8, D), F32)
    sums = (zero8, zero8, zero8, zero8)
    for i in range(2):
        rs4_wait("dc", i, rc, rx)

        def d_middle(r, carry, i=i):
            mine = pl.ds(r, 32)
            incoming = rs4_sum(i, r, rc, rx)
            scaled, inverse = normal(hid[i, mine, :])
            upstream = dmin[i, mine, :].astype(F32)
            value = upstream + normal_back(incoming, scaled, inverse, mlp_gain)
            dhid[i, mine, :] = value
            low = value.astype(BF)
            dmg[i, pl.ds(pl.multiple_of(s * TOK + r, 32), 32), :] = low
            return (carry[0] + fold(incoming * scaled), carry[1] + fold(incoming),
                    carry[2] + fold(low.astype(F32)), carry[3] + fold(upstream))
        sums = tiles(TOK, 32, d_middle, sums)
        ag4_start("db", dmg, i, dmg.at[i, rows(s)])
    sent("dc")

    for i in range(2):
        def down(r, _, i=i):
            here = pl.ds(r, 320)
            part[i, here, :] = dot_nn(act[i, here, :], wd[...].reshape(D, D)).astype(BF)
        tiles(ROWS, 320, down)
    rsw_mid("d", gd, ryd, rzd)
    for i in range(2):
        ag4_forward("db", dmg, i)
    for i in range(2):
        ag4_end("db", dmg, i)
    for i in range(2):
        rs4_a("y", i, rc2)

    for i in range(2):
        def d_mixed(r, _, i=i):
            here = pl.ds(r, 320)
            dmix[i, here, :] = dot_nt(dmg[i, here, :], wo[...].reshape(256, D)).astype(BF)
        tiles(ROWS, 320, d_mixed)
    value = dot_tn(mixed[...].reshape(2 * ROWS, 256), dmg[...].reshape(2 * ROWS, D))
    go[...] = value.astype(BF).reshape(2, 128, D)
    send("go", ("go", "y"), go.at[1 - y], ryo, ydev)
    rs4_b("y", 0, rc2, rx2)
    rs4_b("y", 1, rc2, rx2)

    def attend_back(i):
        lane = lax.broadcasted_iota(jnp.int32, (1, 256), 1) // HEAD_DIM
        mixt[...] = qkv[i, :, 256:512].astype(F32).T.astype(BF)

        def one_head(h, _):
            own = lane == h
            chances = probs[i, h]
            d_value = dot_nn(chances, dmix[i])
            dqkv[i, :, 512:768] = jnp.where(own, d_value.astype(BF), dqkv[i, :, 512:768])
            valued = jnp.where(own, qkv[i, :, 512:768], jnp.zeros((), BF))
            d_chances = dot_nt(valued, dmix[i])
            wide = chances.astype(F32)
            d_scores = wide * (d_chances - jnp.sum(wide * d_chances, axis=0, keepdims=True))
            d_scores = d_scores.astype(BF)
            d_key = dot_nn(d_scores, qkv[i, :, 0:256]) * HEAD_DIM ** -0.5
            dqkv[i, :, 256:512] = jnp.where(own, d_key.astype(BF), dqkv[i, :, 256:512])
            here = pl.ds(pl.multiple_of(h * HEAD_DIM, HEAD_DIM), HEAD_DIM)
            mixt[here, :] = (dot_nn(mixt[here, :], d_scores) * HEAD_DIM ** -0.5).astype(BF)
        lax.fori_loop(0, HEADS_DEV, one_head, None)
        dqkv[i, :, 0:256] = mixt[...].astype(F32).T.astype(BF)

    attend_back(0)
    rsw_mid("u", gu, ryu, rzu)
    copy_d = rsw_end("d", gd, rzd, gd_o)
    arrived(("go", "y"), ryo, ydev)

    def add_out(r, _):
        total = go[y, pl.ds(r, 32), :].astype(F32) + ryo[pl.ds(r, 32), :].astype(F32)
        go[y, pl.ds(r, 32), :] = total.astype(BF)
    tiles(128, 32, add_out)
    n_gz = [ix("goz", d) for d in range(3)]
    n_gs = ix("gozs")

    def out_grad_copy(slot):
        return pltpu.make_async_remote_copy(
            src_ref=go.at[y], dst_ref=rzo.at[slot], send_sem=ssem.at[n_gs], recv_sem=rsem.at[n_gz[0] + slot],
            device_id=(s, s * 2 + y), device_id_type=MESH_ID)

    @pl.when(z != s)
    def _():
        out_grad_copy(lax.rem(z + 3 - s, 4)).start()

    attend_back(1)
    sent("y")
    for i in range(2):
        rs4_wait("y", i, rc2, rx2)

        def last(r, _, i=i):
            mine = pl.ds(r, 32)
            value = hid[i, mine, :] + (rs4_sum(i, r, rc2, rx2) + down_bias)
            out_o[i, mine, :] = value.astype(BF)
        tiles(TOK, 32, last)
    for i in range(2):
        def d_normed(r, _, i=i):
            here = pl.ds(r, 320)
            part[i, here, :] = dot_nt(dqkv[i, here, :], wq[...].reshape(D, 768)).astype(BF)
        tiles(ROWS, 320, d_normed)
        rs4_a("da", i, rc)
    rs4_b("da", 0, rc, rx)
    rs4_b("da", 1, rc, rx)
    weight_grad(xg, dqkv, gq)
    rsw_start("q", gq, ryq)

    copy_u = rsw_end("u", gu, rzu, gu_o)

    n_gb = [ix("gob", d) for d in range(3)]

    def out_final_copy(d):
        return pltpu.make_async_remote_copy(
            src_ref=go.at[y], dst_ref=go_o, send_sem=ssem.at[n_gb[d - 1]], recv_sem=rsem.at[n_gb[0]],
            device_id=(lax.rem(s + d, 4), j), device_id_type=MESH_ID)
    n_ol = local.setdefault("go", len(local))

    @pl.when(z == s)
    def _():
        for slot in range(3):
            pltpu.make_async_remote_copy(
                src_ref=go.at[y], dst_ref=rzo.at[slot], send_sem=ssem.at[n_gs], recv_sem=rsem.at[n_gz[slot]],
                device_id=(s, zj(1)), device_id_type=MESH_ID).wait_recv()

        def add(r, _):
            total = go[y, pl.ds(r, 32), :].astype(F32)
            for slot in range(3):
                total = total + rzo[slot, pl.ds(r, 32), :].astype(F32)
            go[y, pl.ds(r, 32), :] = total.astype(BF)
        tiles(128, 32, add)
        pltpu.make_async_copy(go.at[y], go_o, lsem.at[n_ol]).start()
        for d in (1, 2, 3):
            out_final_copy(d).start()
    rsw_forward("d", gd_o)

    sums_a = (zero8, zero8)
    for i in range(2):
        rs4_wait("da", i, rc, rx)

        def d_input(r, carry, i=i):
            mine = pl.ds(r, 32)
            incoming = rs4_sum(i, r, rc, rx)
            scaled, inverse = normal(xin[i, mine, :].astype(F32))
            value = dhid[i, mine, :] + normal_back(incoming, scaled, inverse, attn_gain)
            dx_o[i, mine, :] = value.astype(BF)
            return carry[0] + fold(incoming * scaled), carry[1] + fold(incoming)
        sums_a = tiles(TOK, 32, d_input, sums_a)

    sgs[...] = jnp.zeros_like(sgs)

    def place(row, total):
        for b in range(NSH):
            sgs[b, pl.ds(row, 1), :] = total[:, 128 * b:128 * b + 128]

    def flat(value):
        return jnp.sum(value, axis=0, keepdims=True)
    place(0, flat(sums_a[0]))
    place(1, flat(sums_a[1]))
    place(4, flat(sums[2]))
    place(5, flat(sums[0]))
    place(6, flat(sums[1]))
    place(7, flat(sums[3]))
    d_query_sum = jnp.sum(dqkv[0, :, 0:256].astype(F32) + dqkv[1, :, 0:256].astype(F32), axis=0, keepdims=True)
    d_value_sum = jnp.sum(dqkv[0, :, 512:768].astype(F32) + dqkv[1, :, 512:768].astype(F32), axis=0, keepdims=True)
    for b in range(2):
        sgs[2 * s + b, pl.ds(2, 1), :] = d_query_sum[:, 128 * b:128 * b + 128]
        sgs[2 * s + b, pl.ds(3, 1), :] = d_value_sum[:, 128 * b:128 * b + 128]
    up_sum = flat(du_sum)
    row_at = lax.broadcasted_iota(jnp.int32, (8, 128), 0)
    for b in range(NSH):
        wide = jnp.broadcast_to(up_sum[:, 128 * b:128 * b + 128], (8, 128))
        sgs[b, 8:16, :] = jnp.where(row_at == s, wide, 0.0)
    for d in range(1, NSH):
        send("sg", ("sg", d), sgs.at[lax.rem(j + d, NSH)], sg1.at[d - 1], (s, lax.rem(j + d, NSH)))

    rsw_mid("q", gq, ryq, rzq)

    for d in range(1, NSH):
        jf = lax.rem(j + NSH - d, NSH)
        arrived(("sg", d), sg1.at[d - 1], (s, jf))
    total = sgs[j]
    for d in range(1, NSH):
        total = total + sg1[d - 1]
    sg2[0] = total
    for d in range(1, NSEQ):
        send("sg", ("sh", d), sg2.at[0], sg2.at[d], (lax.rem(s + d, NSEQ), j))
    rsw_forward("u", gu_o)
    copy_q = rsw_end("q", gq, rzq, gq_o)
    for d in range(1, NSEQ):
        arrived(("sh", d), sg2.at[d], (lax.rem(s + NSEQ - d, NSEQ), j))
    sg_o[...] = sg2[0] + sg2[1] + sg2[2] + sg2[3]
    rsw_forward("q", gq_o)
    rsw_done("d", gd_o)
    rsw_done("u", gu_o)
    rsw_done("q", gq_o)

    @pl.when(z == s)
    def _():
        for d in (1, 2, 3):
            out_final_copy(d).wait_send()
            out_copy(d).wait_send()
        pltpu.make_async_copy(go.at[y], go_o, lsem.at[n_ol]).wait()

    @pl.when(z != s)
    def _():
        out_final_copy(1).wait_recv()
        out_grad_copy(0).wait_send()
    for copy in (copy_d, copy_u, copy_q):
        copy.wait()
    for tag in list(pending):
        sent(tag)

def fused_device(
    inputs, key_mask, cotangent, attn_gain, attn_shift, qkv_weight, query_bias, value_bias,
    out_weight, out_bias, mlp_gain, mlp_shift, up_weight, up_bias, down_weight, down_bias,
):
    tok = inputs.shape[1]
    s = lax.axis_index("seq")
    own_mask = lax.dynamic_slice_in_dim(key_mask, s * tok, tok, 1)
    gap = ((0, 0), (0, TOK - tok), (0, 0))
    xin = jnp.pad(inputs, gap)
    dmin = jnp.pad(jnp.where(own_mask[:, :, None] > 0, cotangent, jnp.zeros((), BF)), gap)
    slots = jnp.pad(key_mask.reshape(2, NSEQ, tok), ((0, 0), (0, 0), (0, TOK - tok)))
    bias = jnp.where(slots.reshape(2, ROWS, 1) > 0, 0.0, MASKED)
    bias = jnp.broadcast_to(bias, (2, ROWS, 128)).astype(F32)
    own_up = lax.dynamic_slice_in_dim(up_bias, s * 128, 128, 0)
    pack = jnp.stack(
        (attn_gain, attn_shift, query_bias, value_bias, out_bias, mlp_gain, mlp_shift, down_bias, own_up)
    ).astype(F32)
    pack = jnp.pad(pack, ((0, 7), (0, 0)))
    vm = pl.BlockSpec(memory_space=pltpu.VMEM)
    hbm = pl.BlockSpec(memory_space=pl.ANY)

    def shape(dims, dtype=BF):
        return jax.ShapeDtypeStruct(dims, dtype)

    outs = pl.pallas_call(
        layer_kernel,
        out_shape=(
            shape((2, TOK, D)), shape((2, TOK, D)), shape((4, 128, 768)), shape((128, D)),
            shape((4, 128, D)), shape((4, 128, D)), shape((16, 128), F32),
        ),
        in_specs=[vm, vm, vm, vm, hbm, hbm, hbm, hbm],
        out_specs=(vm, vm, hbm, hbm, hbm, hbm, vm),
        scratch_shapes=[
            pltpu.VMEM((2, ROWS, D), BF),
            pltpu.VMEM((8, 128, 768), BF),
            pltpu.VMEM((2, 128, D), BF),
            pltpu.VMEM((8, 128, D), BF),
            pltpu.VMEM((8, 128, D), BF),
            pltpu.VMEM((8, 16, 128), F32),
            pltpu.VMEM((2, ROWS, 768), BF),
            pltpu.VMEM((2, ROWS, 768), BF),
            pltpu.VMEM((2, HEADS_DEV, ROWS, ROWS), BF),
            pltpu.VMEM((256, ROWS), BF),
            pltpu.VMEM((2, ROWS, 256), BF),
            pltpu.VMEM((2, ROWS, D), BF),
            pltpu.VMEM((2, 2, TOK, D), BF),
            pltpu.VMEM((2, TOK, D), BF),
            pltpu.VMEM((2, 2, TOK, D), BF),
            pltpu.VMEM((2, TOK, D), BF),
            pltpu.VMEM((2, TOK, D), F32),
            pltpu.VMEM((2, ROWS, D), BF),
            pltpu.VMEM((2, ROWS, D), BF),
            pltpu.VMEM((2, ROWS, D), BF),
            pltpu.VMEM((2, ROWS, D), BF),
            pltpu.VMEM((2, TOK, D), F32),
            pltpu.VMEM((2, ROWS, 256), BF),
            pltpu.VMEM((8, 128, 768), BF),
            pltpu.VMEM((2, 128, D), BF),
            pltpu.VMEM((8, 128, D), BF),
            pltpu.VMEM((8, 128, D), BF),
            pltpu.VMEM((4, 128, 768), BF),
            pltpu.VMEM((128, D), BF),
            pltpu.VMEM((4, 128, D), BF),
            pltpu.VMEM((4, 128, D), BF),
            pltpu.VMEM((3, 128, 768), BF),
            pltpu.VMEM((3, 128, D), BF),
            pltpu.VMEM((3, 128, D), BF),
            pltpu.VMEM((3, 128, D), BF),
            pltpu.VMEM((8, 16, 128), F32),
            pltpu.VMEM((7, 16, 128), F32),
            pltpu.VMEM((4, 16, 128), F32),
            pltpu.SemaphoreType.DMA((160,)),
            pltpu.SemaphoreType.DMA((160,)),
            pltpu.SemaphoreType.DMA((24,)),
        ],
        compiler_params=pltpu.CompilerParams(
            collective_id=0, has_side_effects=True, vmem_limit_bytes=VMEM_LIMIT
        ),
        cost_estimate=pl.CostEstimate(flops=26_000_000_000, bytes_accessed=30_000_000, transcendentals=8_000_000),
    )(xin, dmin, bias, pack, qkv_weight, out_weight, up_weight, down_weight)
    out, d_input, gq, go, gu, gd, small = outs
    grad_qkv = gq.reshape(4, 128, 3, 256).transpose(1, 2, 0, 3).reshape(128, 3072).astype(F32)
    grad_up = gu.reshape(4, 128, 8, 128).transpose(1, 2, 0, 3).reshape(128, 4096).astype(F32)
    grad_down = gd.reshape(512, D).astype(F32)
    return (
        out[:, :tok], d_input[:, :tok], small[0], small[1], grad_qkv, small[2], small[3],
        go.astype(F32), small[4], small[5], small[6], grad_up, small[8:12].reshape(512), grad_down, small[7],
    )


def solution(mesh):
    in_specs = (
        P("shard", "seq", None),
        P("shard", None),
        P("shard", "seq", None),
        P("shard"),
        P("shard"),
        P("shard", None),
        P("shard"),
        P("shard"),
        P("shard", None),
        P("shard"),
        P("shard"),
        P("shard"),
        P("shard", None),
        P("shard"),
        P("shard", None),
        P("shard"),
    )
    out_specs = (
        P("shard", "seq", None),
        P("shard", "seq", None),
        P("shard"),
        P("shard"),
        P("shard", None),
        P("shard"),
        P("shard"),
        P("shard", None),
        P("shard"),
        P("shard"),
        P("shard"),
        P("shard", None),
        P("shard"),
        P("shard", None),
        P("shard"),
    )
    fits = dict(mesh.shape) == {"seq": NSEQ, "shard": NSH}
    return jax.shard_map(
        fused_device if fits else per_device, mesh=mesh, in_specs=in_specs, out_specs=out_specs, check_vma=False
    )
```

```python
import jax
import jax.numpy as jnp
from jax import lax
from jax.experimental import pallas as pl
from jax.experimental.pallas import tpu as pltpu
from jax.sharding import PartitionSpec as P

D = 1024
HEAD_DIM = 64


EPSILON = 1e-05


def product(left, right):
    return jnp.dot(left, right, preferred_element_type=jnp.float32)


def product_tn(left, right):
    return lax.dot_general(
        left, right, (((0,), (0,)), ((), ())), preferred_element_type=jnp.float32
    )


def product_nt(left, right):
    return lax.dot_general(
        left, right, (((1,), (1,)), ((), ())), preferred_element_type=jnp.float32
    )


def norm_rows(current, gain, shift):
    centre = jnp.mean(current, axis=-1, keepdims=True)
    centred = current - centre
    inverse = lax.rsqrt(jnp.mean(centred * centred, axis=-1, keepdims=True) + EPSILON)
    scaled = centred * inverse
    return (scaled * gain + shift, scaled, inverse)


def norm_back(incoming, scaled, inverse, gain):
    inner = incoming * gain
    d_current = inverse * (
        inner
        - jnp.mean(inner, axis=-1, keepdims=True)
        - scaled * jnp.mean(inner * scaled, axis=-1, keepdims=True)
    )
    return (d_current, jnp.sum(incoming * scaled, axis=0), jnp.sum(incoming, axis=0))


def split_heads(block):
    images, length, width = block.shape
    return block.reshape(images, length, width // HEAD_DIM, HEAD_DIM)


def masked_scores(query_h, keyed_h, key_mask):
    scores = jnp.einsum("iqhd,ikhd->ihqk", query_h, keyed_h, preferred_element_type=jnp.float32)
    scores = scores * HEAD_DIM ** (-0.5)
    return jnp.where(key_mask[:, None, None, :] > 0, scores, -1e30)


def layer_forward(current, key_mask, weights, images):
    (
        attn_gain,
        attn_shift,
        qkv_weight,
        query_bias,
        value_bias,
        out_weight,
        out_bias,
        mlp_gain,
        mlp_shift,
        up_weight,
        up_bias,
        down_weight,
        down_bias,
    ) = weights
    row_count = current.shape[0]
    tok_local = row_count // images
    normed, scaled_a, inverse_a = norm_rows(
        current, attn_gain.astype(jnp.float32), attn_shift.astype(jnp.float32)
    )
    normed_low = normed.astype(jnp.bfloat16)
    packed_bias = jnp.concatenate(
        [
            query_bias.astype(jnp.float32),
            jnp.zeros((D,), jnp.float32),
            value_bias.astype(jnp.float32),
        ]
    )
    packed = (product(normed_low, qkv_weight) + packed_bias).astype(jnp.bfloat16)
    packed = packed.reshape(images, tok_local, 3, D)
    head_view = lax.all_to_all(packed, "seq", split_axis=3, concat_axis=1, tiled=True)
    query_h = split_heads(head_view[:, :, 0])
    keyed_h = split_heads(head_view[:, :, 1])
    value_h = split_heads(head_view[:, :, 2])
    scores = masked_scores(query_h, keyed_h, key_mask)
    row_max = jnp.max(scores, axis=-1, keepdims=True)
    raised = jnp.exp(scores - row_max)
    row_sum = jnp.sum(raised, axis=-1, keepdims=True)
    attn_probs = raised / row_sum
    log_total = row_max + jnp.log(row_sum)
    mixed = jnp.einsum(
        "ihqk,ikhd->iqhd",
        attn_probs.astype(jnp.bfloat16),
        value_h,
        preferred_element_type=jnp.float32,
    )
    seq_len = head_view.shape[1]
    mixed = mixed.reshape(images, seq_len, head_view.shape[3]).astype(jnp.bfloat16)
    merged = lax.all_to_all(mixed, "seq", split_axis=1, concat_axis=2, tiled=True)
    merged_rows = merged.reshape(row_count, D)
    middle = current + product(merged_rows, out_weight) + out_bias.astype(jnp.float32)
    second, scaled_b, inverse_b = norm_rows(
        middle, mlp_gain.astype(jnp.float32), mlp_shift.astype(jnp.float32)
    )
    second_low = second.astype(jnp.bfloat16)
    hidden = product(second_low, up_weight) + up_bias.astype(jnp.float32)
    active = (hidden * jax.nn.sigmoid(1.702 * hidden)).astype(jnp.bfloat16)
    result = middle + product(active, down_weight) + down_bias.astype(jnp.float32)
    stored = (
        scaled_a,
        inverse_a,
        normed_low,
        head_view,
        log_total,
        merged_rows,
        scaled_b,
        inverse_b,
        second_low,
        hidden,
        active,
    )
    return (result, stored)


def layer_backward(upstream, key_mask, weights, stored, images):
    (
        attn_gain,
        attn_shift,
        qkv_weight,
        query_bias,
        value_bias,
        out_weight,
        out_bias,
        mlp_gain,
        mlp_shift,
        up_weight,
        up_bias,
        down_weight,
        down_bias,
    ) = weights
    (
        scaled_a,
        inverse_a,
        normed_low,
        head_view,
        log_total,
        merged_rows,
        scaled_b,
        inverse_b,
        second_low,
        hidden,
        active,
    ) = stored
    row_count = upstream.shape[0]
    tok_local = row_count // images
    branch_low = upstream.astype(jnp.bfloat16)
    grad_down_bias = jnp.sum(branch_low, axis=0, dtype=jnp.float32)
    grad_down_weight = product_tn(active, branch_low)
    d_active = product_nt(branch_low, down_weight)
    gate_sig = jax.nn.sigmoid(1.702 * hidden)
    d_hidden = (d_active * (gate_sig + 1.702 * hidden * gate_sig * (1.0 - gate_sig))).astype(
        jnp.bfloat16
    )
    grad_up_bias = jnp.sum(d_hidden, axis=0, dtype=jnp.float32)
    grad_up_weight = product_tn(second_low, d_hidden)
    d_second = product_nt(d_hidden, up_weight)
    d_norm_b, grad_mlp_gain, grad_mlp_shift = norm_back(
        d_second, scaled_b, inverse_b, mlp_gain.astype(jnp.float32)
    )
    d_middle = upstream + d_norm_b
    d_branch = d_middle.astype(jnp.bfloat16)
    grad_out_bias = jnp.sum(d_branch, axis=0, dtype=jnp.float32)
    grad_out_weight = product_tn(merged_rows, d_branch)
    d_merged = product_nt(d_branch, out_weight).astype(jnp.bfloat16).reshape(images, tok_local, D)
    d_heads = lax.all_to_all(d_merged, "seq", split_axis=2, concat_axis=1, tiled=True)
    query_h = split_heads(head_view[:, :, 0])
    keyed_h = split_heads(head_view[:, :, 1])
    value_h = split_heads(head_view[:, :, 2])
    d_out_h = split_heads(d_heads)
    scores = masked_scores(query_h, keyed_h, key_mask)
    attn_probs = jnp.exp(scores - log_total)
    d_value = jnp.einsum(
        "ihqk,iqhd->ikhd",
        attn_probs.astype(jnp.bfloat16),
        d_out_h,
        preferred_element_type=jnp.float32,
    )
    d_probs = jnp.einsum("iqhd,ikhd->ihqk", d_out_h, value_h, preferred_element_type=jnp.float32)
    d_scores = attn_probs * (d_probs - jnp.sum(attn_probs * d_probs, axis=-1, keepdims=True))
    d_scores = d_scores.astype(jnp.bfloat16)
    d_query = jnp.einsum(
        "ihqk,ikhd->iqhd", d_scores, keyed_h, preferred_element_type=jnp.float32
    ) * HEAD_DIM ** (-0.5)
    d_key = jnp.einsum(
        "ihqk,iqhd->ikhd", d_scores, query_h, preferred_element_type=jnp.float32
    ) * HEAD_DIM ** (-0.5)
    seq_len = head_view.shape[1]
    d_packed = jnp.stack((d_query, d_key, d_value), axis=2).astype(jnp.bfloat16)
    d_packed = d_packed.reshape(images, seq_len, 3, head_view.shape[3])
    d_tokens = lax.all_to_all(d_packed, "seq", split_axis=1, concat_axis=3, tiled=True).reshape(
        row_count, 3 * D
    )
    grad_query_bias = jnp.sum(d_tokens[:, :D], axis=0, dtype=jnp.float32)
    grad_value_bias = jnp.sum(d_tokens[:, 2 * D :], axis=0, dtype=jnp.float32)
    grad_qkv_weight = product_tn(normed_low, d_tokens)
    d_normed = product_nt(d_tokens, qkv_weight)
    d_norm_a, grad_attn_gain, grad_attn_shift = norm_back(
        d_normed, scaled_a, inverse_a, attn_gain.astype(jnp.float32)
    )
    grads = (
        grad_attn_gain,
        grad_attn_shift,
        grad_qkv_weight,
        grad_query_bias,
        grad_value_bias,
        grad_out_weight,
        grad_out_bias,
        grad_mlp_gain,
        grad_mlp_shift,
        grad_up_weight,
        grad_up_bias,
        grad_down_weight,
        grad_down_bias,
    )
    return (d_middle + d_norm_a, grads)


def reduce_grads(grads):
    shares = (
        lax.psum_scatter(
            grads[0].astype(jnp.bfloat16), "shard", scatter_dimension=0, tiled=True
        ).astype(jnp.float32),
        lax.psum_scatter(
            grads[1].astype(jnp.bfloat16), "shard", scatter_dimension=0, tiled=True
        ).astype(jnp.float32),
        lax.psum_scatter(
            grads[2].astype(jnp.bfloat16), "shard", scatter_dimension=0, tiled=True
        ).astype(jnp.float32),
        lax.psum_scatter(
            grads[3].astype(jnp.bfloat16), "shard", scatter_dimension=0, tiled=True
        ).astype(jnp.float32),
        lax.psum_scatter(
            grads[4].astype(jnp.bfloat16), "shard", scatter_dimension=0, tiled=True
        ).astype(jnp.float32),
        lax.psum_scatter(
            grads[5].astype(jnp.bfloat16), "shard", scatter_dimension=0, tiled=True
        ).astype(jnp.float32),
        lax.psum_scatter(
            grads[6].astype(jnp.bfloat16), "shard", scatter_dimension=0, tiled=True
        ).astype(jnp.float32),
        lax.psum_scatter(
            grads[7].astype(jnp.bfloat16), "shard", scatter_dimension=0, tiled=True
        ).astype(jnp.float32),
        lax.psum_scatter(
            grads[8].astype(jnp.bfloat16), "shard", scatter_dimension=0, tiled=True
        ).astype(jnp.float32),
        lax.psum_scatter(
            grads[9].astype(jnp.bfloat16), "shard", scatter_dimension=0, tiled=True
        ).astype(jnp.float32),
        lax.psum_scatter(
            grads[10].astype(jnp.bfloat16), "shard", scatter_dimension=0, tiled=True
        ).astype(jnp.float32),
        lax.psum_scatter(
            grads[11].astype(jnp.bfloat16), "shard", scatter_dimension=0, tiled=True
        ).astype(jnp.float32),
        lax.psum_scatter(
            grads[12].astype(jnp.bfloat16), "shard", scatter_dimension=0, tiled=True
        ).astype(jnp.float32),
    )
    return (
        lax.psum(shares[0].astype(jnp.bfloat16), "seq").astype(jnp.float32),
        lax.psum(shares[1].astype(jnp.bfloat16), "seq").astype(jnp.float32),
        lax.psum(shares[2].astype(jnp.bfloat16), "seq").astype(jnp.float32),
        lax.psum(shares[3].astype(jnp.bfloat16), "seq").astype(jnp.float32),
        lax.psum(shares[4].astype(jnp.bfloat16), "seq").astype(jnp.float32),
        lax.psum(shares[5].astype(jnp.bfloat16), "seq").astype(jnp.float32),
        lax.psum(shares[6].astype(jnp.bfloat16), "seq").astype(jnp.float32),
        lax.psum(shares[7].astype(jnp.bfloat16), "seq").astype(jnp.float32),
        lax.psum(shares[8].astype(jnp.bfloat16), "seq").astype(jnp.float32),
        lax.psum(shares[9].astype(jnp.bfloat16), "seq").astype(jnp.float32),
        lax.psum(shares[10].astype(jnp.bfloat16), "seq").astype(jnp.float32),
        lax.psum(shares[11].astype(jnp.bfloat16), "seq").astype(jnp.float32),
        lax.psum(shares[12].astype(jnp.bfloat16), "seq").astype(jnp.float32),
    )


def per_device(
    inputs,
    key_mask,
    cotangent,
    attn_gain,
    attn_shift,
    qkv_weight,
    query_bias,
    value_bias,
    out_weight,
    out_bias,
    mlp_gain,
    mlp_shift,
    up_weight,
    up_bias,
    down_weight,
    down_bias,
):
    shard_set = (
        attn_gain,
        attn_shift,
        qkv_weight,
        query_bias,
        value_bias,
        out_weight,
        out_bias,
        mlp_gain,
        mlp_shift,
        up_weight,
        up_bias,
        down_weight,
        down_bias,
    )
    images = inputs.shape[0]
    tok_local = inputs.shape[1]
    row_count = images * tok_local
    current = inputs.astype(jnp.float32).reshape(row_count, D)
    gathered = (
        lax.all_gather(shard_set[0], "shard", axis=0, tiled=True),
        lax.all_gather(shard_set[1], "shard", axis=0, tiled=True),
        lax.all_gather(shard_set[2], "shard", axis=0, tiled=True),
        lax.all_gather(shard_set[3], "shard", axis=0, tiled=True),
        lax.all_gather(shard_set[4], "shard", axis=0, tiled=True),
        lax.all_gather(shard_set[5], "shard", axis=0, tiled=True),
        lax.all_gather(shard_set[6], "shard", axis=0, tiled=True),
        lax.all_gather(shard_set[7], "shard", axis=0, tiled=True),
        lax.all_gather(shard_set[8], "shard", axis=0, tiled=True),
        lax.all_gather(shard_set[9], "shard", axis=0, tiled=True),
        lax.all_gather(shard_set[10], "shard", axis=0, tiled=True),
        lax.all_gather(shard_set[11], "shard", axis=0, tiled=True),
        lax.all_gather(shard_set[12], "shard", axis=0, tiled=True),
    )
    result, stored = layer_forward(current, key_mask, gathered, images)
    output = result.astype(jnp.bfloat16).reshape(images, tok_local, D)
    start_row = lax.axis_index("seq") * tok_local
    own_mask = lax.dynamic_slice_in_dim(key_mask, start_row, tok_local, 1).astype(jnp.float32)
    upstream = (cotangent.astype(jnp.float32) * own_mask[:, :, None]).reshape(row_count, D)
    again = (
        lax.all_gather(shard_set[0], "shard", axis=0, tiled=True),
        lax.all_gather(shard_set[1], "shard", axis=0, tiled=True),
        lax.all_gather(shard_set[2], "shard", axis=0, tiled=True),
        lax.all_gather(shard_set[3], "shard", axis=0, tiled=True),
        lax.all_gather(shard_set[4], "shard", axis=0, tiled=True),
        lax.all_gather(shard_set[5], "shard", axis=0, tiled=True),
        lax.all_gather(shard_set[6], "shard", axis=0, tiled=True),
        lax.all_gather(shard_set[7], "shard", axis=0, tiled=True),
        lax.all_gather(shard_set[8], "shard", axis=0, tiled=True),
        lax.all_gather(shard_set[9], "shard", axis=0, tiled=True),
        lax.all_gather(shard_set[10], "shard", axis=0, tiled=True),
        lax.all_gather(shard_set[11], "shard", axis=0, tiled=True),
        lax.all_gather(shard_set[12], "shard", axis=0, tiled=True),
    )
    d_input, grads = layer_backward(upstream, key_mask, again, stored, images)
    reduced = reduce_grads(grads)
    input_grad = d_input.astype(jnp.bfloat16).reshape(images, tok_local, D)
    return (
        output,
        input_grad,
        reduced[0],
        reduced[1],
        reduced[2],
        reduced[3],
        reduced[4],
        reduced[5],
        reduced[6],
        reduced[7],
        reduced[8],
        reduced[9],
        reduced[10],
        reduced[11],
        reduced[12],
    )


LIMITS = (3, 4, 4, 6, 7, 8, 9, 10, 10, 10)
NSEQ = 4
NSH = 8
TOK = 160
ROWS = NSEQ * TOK
HEADS_DEV = 4
MASKED = -1e30
VMEM_LIMIT = 64 * 1024 * 1024 - 1024 * 1024
WIDEN_LIMIT = 32 * 1024 * 1024
MESH_ID = pl.DeviceIdType.MESH
BF = jnp.bfloat16
F32 = jnp.float32
GATE = 1.702


def dot_nn(left, right):
    return lax.dot_general(left, right, (((1,), (0,)), ((), ())), preferred_element_type=F32)


def dot_nt(left, right):
    return lax.dot_general(left, right, (((1,), (1,)), ((), ())), preferred_element_type=F32)


def dot_tn(left, right):
    return lax.dot_general(left, right, (((0,), (0,)), ((), ())), preferred_element_type=F32)


def layer_kernel(
    xin, dmin, bias, pack, wq_h, wo_h, wu_h, wd_h,
    out_o, dx_o, gq_o, go_o, gu_o, gd_o, sg_o,
    bias_t, xg, wq, wo, wu, wd, pg, qkv, dqkv, probs, mixt, mixed, part, rc, rx, rc2, rx2,
    hid, cg, act, gate, dmg, dhid, dmix,
    gq, go, gu, gd, ryq, ryo, ryu, ryd, rzq, rzo, rzu, rzd, sgs, sg1, sg2,
    ssem, rsem, lsem,
):
    s = lax.axis_index("seq")
    j = lax.axis_index("shard")
    x, k = s // 2, s % 2
    z, y = j // 2, j % 2
    s_core = x * 2 + (1 - k)
    s_x = (1 - x) * 2 + k
    s_diag = (1 - x) * 2 + (1 - k)
    j_y = z * 2 + (1 - y)
    core = (s_core, j)
    xdev = (s_x, j)
    ydev = (s, j_y)

    def zj(d):
        return lax.rem(z + d, 4) * 2 + y

    ids = {}

    def ix(*key):
        return ids.setdefault(key, len(ids))

    pending = {}

    def send(tag, key, src, dst, dev):
        n = ix(*key)
        copy = pltpu.make_async_remote_copy(
            src_ref=src, dst_ref=dst, send_sem=ssem.at[n], recv_sem=rsem.at[n],
            device_id=dev, device_id_type=MESH_ID)
        copy.start()
        pending.setdefault(tag, []).append(copy)

    def sent(tag):
        for copy in pending.pop(tag, []):
            copy.wait_send()

    def arrived(key, dst, dev):
        n = ix(*key)
        pltpu.make_async_remote_copy(
            src_ref=dst, dst_ref=dst, send_sem=ssem.at[n], recv_sem=rsem.at[n],
            device_id=dev, device_id_type=MESH_ID).wait_recv()

    local = {}

    def load(key, src, dst):
        copy = pltpu.make_async_copy(src, dst, lsem.at[local.setdefault(key, len(local))])
        copy.start()
        return copy

    def rows(block):
        return pl.ds(pl.multiple_of(block * TOK, TOK), TOK)

    def tiles(count, step, body, init=None, unroll=False):
        def inner(t, carry):
            return body(pl.multiple_of(t * step, step), carry)
        return lax.fori_loop(0, count // step, inner, init, unroll=unroll)

    barrier = pltpu.get_barrier_semaphore()
    for d in range(1, NSEQ):
        pl.semaphore_signal(barrier, inc=1, device_id=(lax.rem(s + d, NSEQ), j), device_id_type=MESH_ID)
    for d in range(1, NSH):
        pl.semaphore_signal(barrier, inc=1, device_id=(s, lax.rem(j + d, NSH)), device_id_type=MESH_ID)
    loads_q = [load(("wq", c), wq_h.at[:, pl.ds(pl.multiple_of(1024 * c + 256 * s, 256), 256)],
                    wq.at[j, :, pl.ds(256 * c, 256)]) for c in range(3)]
    loads_u = [load(("wu", c), wu_h.at[:, pl.ds(pl.multiple_of(512 * c + 128 * s, 128), 128)],
                    wu.at[j, :, pl.ds(128 * c, 128)]) for c in range(8)]
    load_d = load(("wd",), wd_h.at[pl.ds(pl.multiple_of(128 * s, 128), 128)], wd.at[j])
    pg[j] = pack[...]
    n_wo = local.setdefault("wo", len(local))

    @pl.when(z == s)
    def _():
        pltpu.make_async_copy(wo_h, wo.at[y], lsem.at[n_wo]).start()
    pl.semaphore_wait(barrier, NSEQ - 1 + NSH - 1)

    def ag4_start(key, buf, i, src):
        send(key, (key, "c", i), src, buf.at[i, rows(s)], core)
        send(key, (key, "x", i), src, buf.at[i, rows(s)], xdev)

    def ag4_forward(key, buf, i):
        arrived((key, "x", i), buf.at[i, rows(s_x)], xdev)
        send(key + "f", (key, "d", i), buf.at[i, rows(s_x)], buf.at[i, rows(s_x)], core)

    def ag4_end(key, buf, i):
        arrived((key, "c", i), buf.at[i, rows(s_core)], core)
        arrived((key, "d", i), buf.at[i, rows(s_diag)], core)

    weights = {"wq": wq, "wu": wu, "wd": wd}
    n_up, n_down = ix("wo", "up"), ix("wo", "down")

    def out_hop(step):
        n = n_up if step == 1 else n_down
        return pltpu.make_async_remote_copy(
            src_ref=wo.at[y], dst_ref=wo.at[y], send_sem=ssem.at[n], recv_sem=rsem.at[n_up],
            device_id=(s, (z + step) * 2 + y), device_id_type=MESH_ID)

    def out_hops(act_on):
        @pl.when((z >= s) & (z < 3))
        def _():
            act_on(out_hop(1))

        @pl.when((z <= s) & (z > 0))
        def _():
            act_on(out_hop(-1))

    def gather_start(key, d):
        if key == "wo":
            @pl.when(z == s)
            def _():
                pltpu.make_async_copy(wo_h, wo.at[y], lsem.at[n_wo]).wait()

            @pl.when((z == s) & (z < 3))
            def _():
                out_hop(1).start()

            @pl.when((z == s) & (z > 0))
            def _():
                out_hop(-1).start()
            return
        buf = weights[key]
        if d == 1:
            send(key, (key, "y", 0), buf.at[j], buf.at[j], ydev)
        send(key, (key, "z", d), buf.at[j], buf.at[j], (s, zj(d)))

    def gather_forward(key, d):
        if key == "wo":
            @pl.when(z > s)
            def _():
                pltpu.make_async_remote_copy(
                    src_ref=wo.at[y], dst_ref=wo.at[y], send_sem=ssem.at[n_up], recv_sem=rsem.at[n_up],
                    device_id=(s, (z - 1) * 2 + y), device_id_type=MESH_ID).wait_recv()

            @pl.when(z < s)
            def _():
                pltpu.make_async_remote_copy(
                    src_ref=wo.at[y], dst_ref=wo.at[y], send_sem=ssem.at[n_up], recv_sem=rsem.at[n_up],
                    device_id=(s, (z + 1) * 2 + y), device_id_type=MESH_ID).wait_recv()

            @pl.when((z > s) & (z < 3))
            def _():
                out_hop(1).start()

            @pl.when((z < s) & (z > 0))
            def _():
                out_hop(-1).start()
            send("wo", ("wo", "y"), wo.at[y], wo.at[y], ydev)
            return
        buf = weights[key]
        jf = zj(4 - d)
        arrived((key, "z", d), buf.at[jf], (s, jf))
        send(key, (key, "y", d), buf.at[jf], buf.at[jf], ydev)

    rounds = [("wq", 1), ("wq", 3), ("wq", 2), ("wo", 0), ("wu", 1), ("wu", 3), ("wu", 2), ("wd", 1), ("wd", 3), ("wd", 2)]
    at_round, issued = [0], [0]

    def gather_issue(upto):
        while issued[0] < min(upto, len(rounds)):
            gather_start(*rounds[issued[0]])
            issued[0] += 1

    def pump(count=1):
        for _step in range(count):
            n = at_round[0]
            gather_forward(*rounds[n])
            at_round[0] = n + 1
            gather_issue(LIMITS[n])

    def agw_end(key, buf):
        for d in (0, 1, 3, 2):
            jf = lax.rem(z + 4 - d, 4) * 2 + (1 - y)
            arrived((key, "y", d), buf.at[jf], ydev)

    def rs4_a(key, i, rcb):
        send(key, (key, "c0", i), part.at[i, rows(s_core)], rcb.at[i, 0], core)
        send(key, (key, "c1", i), part.at[i, rows(s_diag)], rcb.at[i, 1], core)

    def rs4_b(key, i, rcb, rxb):
        arrived((key, "c1", i), rcb.at[i, 1], core)

        def add(r, _):
            here = pl.ds(pl.multiple_of(s_x * TOK + r, 32), 32)
            total = part[i, here, :].astype(F32) + rcb[i, 1, pl.ds(r, 32), :].astype(F32)
            part[i, here, :] = total.astype(BF)
        tiles(TOK, 32, add, unroll=True)
        send(key, (key, "x", i), part.at[i, rows(s_x)], rxb.at[i], xdev)

    def rs4_wait(key, i, rcb, rxb):
        arrived((key, "c0", i), rcb.at[i, 0], core)
        arrived((key, "x", i), rxb.at[i], xdev)

    def rs4_sum(i, r, rcb, rxb):
        here = pl.ds(pl.multiple_of(s * TOK + r, 32), 32)
        return (part[i, here, :].astype(F32) + rcb[i, 0, pl.ds(r, 32), :].astype(F32)
                + rxb[i, pl.ds(r, 32), :].astype(F32))

    def add_into(g, row, others):
        def add(r, _):
            total = g[row, pl.ds(r, 32), :].astype(F32)
            for ref, at in others:
                total = total + ref[at, pl.ds(r, 32), :].astype(F32)
            g[row, pl.ds(r, 32), :] = total.astype(BF)
        tiles(128, 32, add, unroll=True)

    waiting, flying = [], []

    def reduce_fill():
        while waiting and len(flying) < 3:
            piece = waiting.pop(0)
            key, d, g, ry, rz = piece
            if key == "o":
                send("go", ("go", "y"), g.at[1 - y], ry, ydev)
            else:
                send(key, (key, "gy", d), g.at[lax.rem(z + d, 4) * 2 + (1 - y)], ry.at[d], ydev)
            flying.append(piece)

    def reduce_add(key, g, ry, rz):
        for d in ((0,) if key == "o" else (2, 1, 3, 0)):
            waiting.append((key, d, g, ry, rz))
        reduce_fill()

    def reduce_step(count=1):
        for _step in range(count):
            key, d, g, ry, rz = flying.pop(0)
            if key == "o":
                arrived(("go", "y"), ry, ydev)
                reduce_fill()
                add_out_block()
                continue
            arrived((key, "gy", d), ry.at[d], ydev)
            reduce_fill()
            add_into(g, zj(d), [(ry, d)])
            if d:
                send(key, (key, "gz", d), g.at[zj(d)], rz.at[d - 1], (s, zj(d)))

    n_gz = [ix("goz", d) for d in range(3)]
    n_gs = ix("gozs")

    def out_grad_copy(slot):
        return pltpu.make_async_remote_copy(
            src_ref=go.at[y], dst_ref=rzo.at[slot], send_sem=ssem.at[n_gs], recv_sem=rsem.at[n_gz[0] + slot],
            device_id=(s, s * 2 + y), device_id_type=MESH_ID)

    def add_out_block():
        def add_out(r, _):
            total = go[y, pl.ds(r, 32), :].astype(F32) + ryo[pl.ds(r, 32), :].astype(F32)
            go[y, pl.ds(r, 32), :] = total.astype(BF)
        tiles(128, 32, add_out, unroll=True)

        @pl.when(z != s)
        def _():
            out_grad_copy(lax.rem(z + 3 - s, 4)).start()

    def rsw_end(key, g, rz, g_o):
        for d in (2, 1, 3):
            arrived((key, "gz", d), rz.at[d - 1], (s, zj(4 - d)))
        add_into(g, j, [(rz, 0), (rz, 1), (rz, 2)])
        copy = load((key, "go"), g.at[j], g_o.at[s])
        send(key, (key, "gc"), g.at[j], g_o.at[s], core)
        send(key, (key, "gx"), g.at[j], g_o.at[s], xdev)
        return copy

    def rsw_forward(key, g_o):
        arrived((key, "gx"), g_o.at[s_x], xdev)
        send(key, (key, "gd"), g_o.at[s_x], g_o.at[s_x], core)

    def rsw_done(key, g_o):
        arrived((key, "gc"), g_o.at[s_core], core)
        arrived((key, "gd"), g_o.at[s_diag], core)

    def param(p):
        return jnp.concatenate([pg[b, pl.ds(p, 1), :] for b in range(NSH)], axis=1)

    def head_param(p):
        return jnp.concatenate([pg[2 * s, pl.ds(p, 1), :], pg[2 * s + 1, pl.ds(p, 1), :]], axis=1)

    def normal(value):
        centre = jnp.mean(value, axis=-1, keepdims=True)
        centred = value - centre
        inverse = lax.rsqrt(jnp.mean(centred * centred, axis=-1, keepdims=True) + EPSILON)
        return centred * inverse, inverse

    def normal_back(incoming, scaled, inverse, gain):
        inner = incoming * gain
        return inverse * (inner - jnp.mean(inner, axis=-1, keepdims=True)
                          - scaled * jnp.mean(inner * scaled, axis=-1, keepdims=True))

    def fold(value):
        return value[0:8] + value[8:16] + value[16:24] + value[24:32]

    for d in range(1, NSH):
        send("pk", ("pk", d), pack, pg.at[j], (s, lax.rem(j + d, NSH)))
    for i in range(2):
        ag4_start("xg", xg, i, xin.at[i])
    bias_t[...] = bias[...].T
    for copy in loads_q:
        copy.wait()
    gather_issue(2)
    for i in range(2):
        xg[i, rows(s), :] = xin[i]
        dmg[i, rows(s), :] = dmin[i]
    for copy in loads_u:
        copy.wait()
    load_d.wait()
    pump()
    ag4_forward("xg", xg, 0)

    for d in range(1, NSH):
        jf = lax.rem(j + NSH - d, NSH)
        arrived(("pk", d), pg.at[jf], (s, jf))
    attn_gain, attn_shift = param(0), param(1)

    def norm_block(i, block):
        def body(r, _):
            here = pl.ds(pl.multiple_of(block * TOK + r, 32), 32)
            scaled, _inverse = normal(xg[i, here, :].astype(F32))
            xg[i, here, :] = (scaled * attn_gain + attn_shift).astype(BF)
        tiles(TOK, 32, body, unroll=True)

    norm_block(0, s)
    norm_block(1, s)
    pump()
    for i in range(2):
        arrived(("xg", "c", i), xg.at[i, rows(s_core)], core)
        norm_block(i, s_core)
    ag4_forward("xg", xg, 1)
    for i in range(2):
        ag4_start("dm", dmg, i, dmin.at[i])
    arrived(("xg", "d", 0), xg.at[0, rows(s_diag)], core)
    norm_block(0, s_diag)
    sent("xgf")
    pump()
    norm_block(0, s_x)
    norm_block(1, s_x)
    arrived(("xg", "d", 1), xg.at[1, rows(s_diag)], core)
    norm_block(1, s_diag)
    pump()
    agw_end("wq", wq)

    packed_bias = jnp.concatenate([head_param(2), jnp.zeros((1, 256), F32), head_param(3)], axis=1)

    def project_in(i):
        def project(r, _):
            here = pl.ds(r, 320)
            value = dot_nn(xg[i, here, :], wq[...].reshape(D, 768)) + packed_bias
            qkv[i, here, :] = value.astype(BF)
        tiles(ROWS, 320, project)

    def attend(i):
        value_t = qkv[i, :, 512:768].astype(F32).T.astype(BF)
        mixt[...] = value_t
        lane = lax.broadcasted_iota(jnp.int32, (1, 256), 1) // HEAD_DIM

        def one_head(h, _):
            keyed = jnp.where(lane == h, qkv[i, :, 256:512], jnp.zeros((), BF))
            query = qkv[i, :, 0:256] * jnp.asarray(HEAD_DIM ** -0.5, BF)
            scores = dot_nt(keyed, query) + bias_t[:, i:i + 1]
            raised = jnp.exp(scores - jnp.max(scores, axis=0, keepdims=True))
            chances = (raised * (1.0 / jnp.sum(raised, axis=0, keepdims=True))).astype(BF)
            probs[i, h] = chances
            here = pl.ds(pl.multiple_of(h * HEAD_DIM, HEAD_DIM), HEAD_DIM)
            mixt[here, :] = dot_nn(mixt[here, :], chances).astype(BF)
        lax.fori_loop(0, HEADS_DEV, one_head, None)
        mixed[i] = mixt[...].astype(F32).T.astype(BF)

    def project_out(i):
        def body(r, _):
            here = pl.ds(r, 320)
            part[i, here, :] = dot_nn(mixed[i, here, :], wo[...].reshape(256, D)).astype(BF)
        tiles(ROWS, 320, body)

    project_in(0)
    attend(0)
    project_in(1)
    arrived(("wo", "y"), wo.at[1 - y], ydev)
    project_out(0)
    rs4_a("o", 0, rc)
    attend(1)
    rs4_b("o", 0, rc, rx)
    project_out(1)
    rs4_a("o", 1, rc)
    pump()
    rs4_b("o", 1, rc, rx)
    for i in range(2):
        ag4_forward("dm", dmg, i)
    pump()

    out_bias, mlp_gain, mlp_shift, down_bias = param(4), param(5), param(6), param(7)
    up_bias = param(8)

    for i in range(2):
        rs4_wait("o", i, rc, rx)

        def middle(r, _, i=i):
            value = xin[i, pl.ds(r, 32), :].astype(F32) + (rs4_sum(i, r, rc, rx) + out_bias)
            hid[i, pl.ds(r, 32), :] = value
            scaled, _inverse = normal(value)
            here = pl.ds(pl.multiple_of(s * TOK + r, 32), 32)
            cg[i, here, :] = (scaled * mlp_gain + mlp_shift).astype(BF)
        tiles(TOK, 32, middle, unroll=True)
        ag4_start("c", cg, i, cg.at[i, rows(s)])
        pump()
    for n in range(2):
        ag4_end("dm", dmg, n)
    agw_end("wu", wu)
    for i in range(2):
        ag4_forward("c", cg, i)
        ag4_end("c", cg, i)

        def up(r, _, i=i):
            here = pl.ds(r, 320)
            value = dot_nn(cg[i, here, :], wu[...].reshape(D, D)) + up_bias
            sig = jax.nn.sigmoid(GATE * value)
            act[i, here, :] = (value * sig).astype(BF)
            gate[i, here, :] = (sig + GATE * value * sig * (1.0 - sig)).astype(BF)
        tiles(ROWS, 320, up)
        pump()
    sent("o")

    def weight_grad(left, right, g):
        def body(t, _):
            cols = pl.ds(pl.multiple_of(t * 256, 256), 256)
            value = dot_tn(left[:, :, cols].reshape(2 * ROWS, 256), right[...].reshape(2 * ROWS, right.shape[2]))
            g[pl.ds(2 * t, 2)] = value.astype(BF).reshape(2, 128, right.shape[2])
        lax.fori_loop(0, left.shape[2] // 256, body, None)

    weight_grad(act, dmg, gd)
    reduce_add("d", gd, ryd, rzd)
    agw_end("wd", wd)

    def d_up(i, total):
        def body(r, carry):
            here = pl.ds(r, 320)
            value = dot_nt(dmg[i, here, :], wd[...].reshape(D, D)) * gate[i, here, :].astype(F32)
            value = value.astype(BF)
            gate[i, here, :] = value
            return carry + jnp.sum(value.astype(F32).reshape(40, 8, D), axis=0)
        return tiles(ROWS, 320, body, total)

    def d_second(i):
        def body(r, _):
            here = pl.ds(r, 320)
            part[i, here, :] = dot_nt(gate[i, here, :], wu[...].reshape(D, D)).astype(BF)
        tiles(ROWS, 320, body)

    sent("dmf")
    sent("dm")
    du_sum = d_up(0, jnp.zeros((8, D), F32))
    d_second(0)
    rs4_a("dc", 0, rc)
    du_sum = d_up(1, du_sum)
    rs4_b("dc", 0, rc, rx)
    d_second(1)
    rs4_a("dc", 1, rc)
    reduce_step()
    rs4_b("dc", 1, rc, rx)
    weight_grad(cg, gate, gu)
    reduce_add("u", gu, ryu, rzu)
    reduce_step()

    zero8 = jnp.zeros((8, D), F32)
    sums = (zero8, zero8, zero8, zero8)
    for i in range(2):
        rs4_wait("dc", i, rc, rx)

        def d_middle(r, carry, i=i):
            mine = pl.ds(r, 32)
            incoming = rs4_sum(i, r, rc, rx)
            scaled, inverse = normal(hid[i, mine, :])
            upstream = dmin[i, mine, :].astype(F32)
            value = upstream + normal_back(incoming, scaled, inverse, mlp_gain)
            dhid[i, mine, :] = value
            low = value.astype(BF)
            dmg[i, pl.ds(pl.multiple_of(s * TOK + r, 32), 32), :] = low
            return (carry[0] + fold(incoming * scaled), carry[1] + fold(incoming),
                    carry[2] + fold(low.astype(F32)), carry[3] + fold(upstream))
        sums = tiles(TOK, 32, d_middle, sums, unroll=True)
        ag4_start("db", dmg, i, dmg.at[i, rows(s)])
        reduce_step()
    sent("dc")

    for i in range(2):
        def down(r, _, i=i):
            here = pl.ds(r, 320)
            part[i, here, :] = dot_nn(act[i, here, :], wd[...].reshape(D, D)).astype(BF)
        tiles(ROWS, 320, down)

    def attend_back(i):
        def d_mixed(r, _):
            here = pl.ds(r, 320)
            dmix[i, here, :] = dot_nt(dmg[i, here, :], wo[...].reshape(256, D)).astype(BF)
        tiles(ROWS, 320, d_mixed)
        lane = lax.broadcasted_iota(jnp.int32, (1, 256), 1) // HEAD_DIM
        mixt[...] = qkv[i, :, 256:512].astype(F32).T.astype(BF)

        def one_head(h, _):
            own = lane == h
            chances = probs[i, h]
            d_value = dot_nn(chances, dmix[i])
            dqkv[i, :, 512:768] = jnp.where(own, d_value.astype(BF), dqkv[i, :, 512:768])
            valued = jnp.where(own, qkv[i, :, 512:768], jnp.zeros((), BF))
            d_chances = dot_nt(valued, dmix[i])
            wide = chances.astype(F32)
            d_scores = wide * (d_chances - jnp.sum(wide * d_chances, axis=0, keepdims=True))
            d_scores = d_scores.astype(BF)
            d_key = dot_nn(d_scores, qkv[i, :, 0:256]) * HEAD_DIM ** -0.5
            dqkv[i, :, 256:512] = jnp.where(own, d_key.astype(BF), dqkv[i, :, 256:512])
            here = pl.ds(pl.multiple_of(h * HEAD_DIM, HEAD_DIM), HEAD_DIM)
            mixt[here, :] = (dot_nn(mixt[here, :], d_scores) * HEAD_DIM ** -0.5).astype(BF)
        lax.fori_loop(0, HEADS_DEV, one_head, None)
        dqkv[i, :, 0:256] = mixt[...].astype(F32).T.astype(BF)

    def out_presum(i):
        arrived(("y", "c0", i), rc2.at[i, 0], core)
        arrived(("y", "c1", i), rc2.at[i, 1], core)

        def body(r, _):
            mine = pl.ds(r, 32)
            here = pl.ds(pl.multiple_of(s * TOK + r, 32), 32)
            there = pl.ds(pl.multiple_of(s_x * TOK + r, 32), 32)
            total = part[i, here, :].astype(F32) + rc2[i, 0, mine, :].astype(F32)
            hid[i, mine, :] = hid[i, mine, :] + (total + down_bias)
            total = part[i, there, :].astype(F32) + rc2[i, 1, mine, :].astype(F32)
            rc2[i, 1, mine, :] = total.astype(BF)
        tiles(TOK, 32, body, unroll=True)

    def d_normed(i):
        def body(r, _):
            here = pl.ds(r, 320)
            part[i, here, :] = dot_nt(dqkv[i, here, :], wq[...].reshape(D, 768)).astype(BF)
        tiles(ROWS, 320, body)
        rs4_a("da", i, rc)

    ag4_forward("db", dmg, 0)
    ag4_end("db", dmg, 0)
    for i in range(2):
        rs4_a("y", i, rc2)
    attend_back(0)
    reduce_step()
    ag4_forward("db", dmg, 1)
    for i in range(2):
        out_presum(i)
    sent("y")
    d_normed(0)
    ag4_end("db", dmg, 1)
    copy_d = rsw_end("d", gd, rzd, gd_o)
    rs4_b("da", 0, rc, rx)
    attend_back(1)
    reduce_step()
    d_normed(1)
    weight_grad(xg, dqkv, gq)
    rs4_b("da", 1, rc, rx)
    value = dot_tn(mixed[...].reshape(2 * ROWS, 256), dmg[...].reshape(2 * ROWS, D))
    go[...] = value.astype(BF).reshape(2, 128, D)
    reduce_add("o", go, ryo, rzo)
    reduce_add("q", gq, ryq, rzq)
    reduce_step()
    for i in range(2):
        send("y", ("y", "x", i), rc2.at[i, 1], rx2.at[i], xdev)
    reduce_step()

    n_gb = [ix("gob", d) for d in range(3)]

    def out_final_copy(d):
        return pltpu.make_async_remote_copy(
            src_ref=go.at[y], dst_ref=go_o, send_sem=ssem.at[n_gb[d - 1]], recv_sem=rsem.at[n_gb[0]],
            device_id=(lax.rem(s + d, 4), j), device_id_type=MESH_ID)
    n_ol = local.setdefault("go", len(local))

    sums_a = (zero8, zero8)
    for i in range(2):
        rs4_wait("da", i, rc, rx)

        def d_input(r, carry, i=i):
            mine = pl.ds(r, 32)
            incoming = rs4_sum(i, r, rc, rx)
            scaled, inverse = normal(xin[i, mine, :].astype(F32))
            value = dhid[i, mine, :] + normal_back(incoming, scaled, inverse, attn_gain)
            dx_o[i, mine, :] = value.astype(BF)
            return carry[0] + fold(incoming * scaled), carry[1] + fold(incoming)
        sums_a = tiles(TOK, 32, d_input, sums_a, unroll=True)
        if i == 0:
            rsw_forward("d", gd_o)
            reduce_step()

    sgs[...] = jnp.zeros_like(sgs)

    def place(row, total):
        for b in range(NSH):
            sgs[b, pl.ds(row, 1), :] = total[:, 128 * b:128 * b + 128]

    def flat(value):
        return jnp.sum(value, axis=0, keepdims=True)
    place(0, flat(sums_a[0]))
    place(1, flat(sums_a[1]))
    place(4, flat(sums[2]))
    place(5, flat(sums[0]))
    place(6, flat(sums[1]))
    place(7, flat(sums[3]))
    d_query_sum = jnp.sum(dqkv[0, :, 0:256].astype(F32) + dqkv[1, :, 0:256].astype(F32), axis=0, keepdims=True)
    d_value_sum = jnp.sum(dqkv[0, :, 512:768].astype(F32) + dqkv[1, :, 512:768].astype(F32), axis=0, keepdims=True)
    for b in range(2):
        sgs[2 * s + b, pl.ds(2, 1), :] = d_query_sum[:, 128 * b:128 * b + 128]
        sgs[2 * s + b, pl.ds(3, 1), :] = d_value_sum[:, 128 * b:128 * b + 128]
    up_sum = flat(du_sum)
    row_at = lax.broadcasted_iota(jnp.int32, (8, 128), 0)
    for b in range(NSH):
        wide = jnp.broadcast_to(up_sum[:, 128 * b:128 * b + 128], (8, 128))
        sgs[b, 8:16, :] = jnp.where(row_at == s, wide, 0.0)
    for d in range(1, NSH):
        send("sg", ("sg", d), sgs.at[lax.rem(j + d, NSH)], sg1.at[d - 1], (s, lax.rem(j + d, NSH)))

    copy_u = rsw_end("u", gu, rzu, gu_o)
    reduce_step(2)

    @pl.when(z == s)
    def _():
        for slot in range(3):
            pltpu.make_async_remote_copy(
                src_ref=go.at[y], dst_ref=rzo.at[slot], send_sem=ssem.at[n_gs], recv_sem=rsem.at[n_gz[slot]],
                device_id=(s, zj(1)), device_id_type=MESH_ID).wait_recv()

        def add(r, _):
            total = go[y, pl.ds(r, 32), :].astype(F32)
            for slot in range(3):
                total = total + rzo[slot, pl.ds(r, 32), :].astype(F32)
            go[y, pl.ds(r, 32), :] = total.astype(BF)
        tiles(128, 32, add, unroll=True)
        pltpu.make_async_copy(go.at[y], go_o, lsem.at[n_ol]).start()
        for d in (1, 2, 3):
            out_final_copy(d).start()

    for d in range(1, NSH):
        jf = lax.rem(j + NSH - d, NSH)
        arrived(("sg", d), sg1.at[d - 1], (s, jf))
    total = sgs[j]
    for d in range(1, NSH):
        total = total + sg1[d - 1]
    sg2[0] = total
    for d in range(1, NSEQ):
        send("sg", ("sh", d), sg2.at[0], sg2.at[d], (lax.rem(s + d, NSEQ), j))
    for i in range(2):
        arrived(("y", "x", i), rx2.at[i], xdev)

        def last(r, _, i=i):
            mine = pl.ds(r, 32)
            out_o[i, mine, :] = (hid[i, mine, :] + rx2[i, mine, :].astype(F32)).astype(BF)
        tiles(TOK, 32, last, unroll=True)
    reduce_step(len(flying) + len(waiting))
    assert not waiting and not flying
    rsw_forward("u", gu_o)
    copy_q = rsw_end("q", gq, rzq, gq_o)
    for d in range(1, NSEQ):
        arrived(("sh", d), sg2.at[d], (lax.rem(s + NSEQ - d, NSEQ), j))
    sg_o[...] = sg2[0] + sg2[1] + sg2[2] + sg2[3]
    rsw_forward("q", gq_o)
    rsw_done("d", gd_o)
    rsw_done("u", gu_o)
    rsw_done("q", gq_o)

    @pl.when(z == s)
    def _():
        for d in (1, 2, 3):
            out_final_copy(d).wait_send()
        pltpu.make_async_copy(go.at[y], go_o, lsem.at[n_ol]).wait()

    @pl.when(z != s)
    def _():
        out_final_copy(1).wait_recv()
        out_grad_copy(0).wait_send()
    for copy in (copy_d, copy_u, copy_q):
        copy.wait()
    out_hops(lambda hop: hop.wait_send())
    for tag in list(pending):
        sent(tag)

def widen_kernel(
    gq, go, gu, gd, small,
    attn_gain, attn_shift, qkv, query, value, out, out_b, mlp_gain, mlp_shift, up, up_b, down, down_b,
):
    for at, ref in enumerate((attn_gain, attn_shift, query, value, out_b, mlp_gain, mlp_shift, down_b)):
        ref[...] = small[at]
    for b in range(NSEQ):
        up_b[128 * b:128 * b + 128] = small[8 + b]
        for c in range(3):
            qkv[:, 1024 * c + 256 * b:1024 * c + 256 * b + 256] = gq[b, :, 256 * c:256 * c + 256].astype(F32)
        for c in range(8):
            up[:, 512 * c + 128 * b:512 * c + 128 * b + 128] = gu[b, :, 128 * c:128 * c + 128].astype(F32)
        down[128 * b:128 * b + 128, :] = gd[b].astype(F32)
    out[...] = go[...].astype(F32)


def fused_device(
    inputs, key_mask, cotangent, attn_gain, attn_shift, qkv_weight, query_bias, value_bias,
    out_weight, out_bias, mlp_gain, mlp_shift, up_weight, up_bias, down_weight, down_bias,
):
    tok = inputs.shape[1]
    s = lax.axis_index("seq")
    gap = ((0, 0), (0, TOK - tok))
    slots = jnp.pad(key_mask.reshape(2, NSEQ, tok), ((0, 0),) + gap)
    own_mask = lax.dynamic_slice_in_dim(slots, s, 1, 1).reshape(2, TOK, 1)
    held = lax.broadcasted_iota(jnp.int32, (1, TOK, 1), 1) < tok
    none = jnp.zeros((), BF)
    xin = jnp.where(held, jnp.pad(inputs, gap + ((0, 0),)), none)
    dmin = jnp.where(own_mask > 0, jnp.pad(cotangent, gap + ((0, 0),)), none)
    bias = jnp.where(slots.reshape(2, ROWS) > 0, 0.0, MASKED).astype(F32)
    bias = jnp.pad(bias, ((0, 6), (0, 0)))
    own_up = lax.dynamic_slice_in_dim(up_bias, s * 128, 128, 0)
    pack = jnp.stack(
        (attn_gain, attn_shift, query_bias, value_bias, out_bias, mlp_gain, mlp_shift, down_bias, own_up)
    ).astype(F32)
    pack = jnp.pad(pack, ((0, 7), (0, 0)))
    vm = pl.BlockSpec(memory_space=pltpu.VMEM)
    hbm = pl.BlockSpec(memory_space=pl.ANY)

    def shape(dims, dtype=BF):
        return jax.ShapeDtypeStruct(dims, dtype)

    outs = pl.pallas_call(
        layer_kernel,
        out_shape=(
            shape((2, TOK, D)), shape((2, TOK, D)), shape((4, 128, 768)), shape((128, D)),
            shape((4, 128, D)), shape((4, 128, D)), shape((16, 128), F32),
        ),
        in_specs=[vm, vm, vm, vm, hbm, hbm, hbm, hbm],
        out_specs=(vm, vm, hbm, hbm, hbm, hbm, vm),
        scratch_shapes=[
            pltpu.VMEM((ROWS, 8), F32),
            pltpu.VMEM((2, ROWS, D), BF),
            pltpu.VMEM((8, 128, 768), BF),
            pltpu.VMEM((2, 128, D), BF),
            pltpu.VMEM((8, 128, D), BF),
            pltpu.VMEM((8, 128, D), BF),
            pltpu.VMEM((8, 16, 128), F32),
            pltpu.VMEM((2, ROWS, 768), BF),
            pltpu.VMEM((2, ROWS, 768), BF),
            pltpu.VMEM((2, HEADS_DEV, ROWS, ROWS), BF),
            pltpu.VMEM((256, ROWS), BF),
            pltpu.VMEM((2, ROWS, 256), BF),
            pltpu.VMEM((2, ROWS, D), BF),
            pltpu.VMEM((2, 2, TOK, D), BF),
            pltpu.VMEM((2, TOK, D), BF),
            pltpu.VMEM((2, 2, TOK, D), BF),
            pltpu.VMEM((2, TOK, D), BF),
            pltpu.VMEM((2, TOK, D), F32),
            pltpu.VMEM((2, ROWS, D), BF),
            pltpu.VMEM((2, ROWS, D), BF),
            pltpu.VMEM((2, ROWS, D), BF),
            pltpu.VMEM((2, ROWS, D), BF),
            pltpu.VMEM((2, TOK, D), F32),
            pltpu.VMEM((2, ROWS, 256), BF),
            pltpu.VMEM((8, 128, 768), BF),
            pltpu.VMEM((2, 128, D), BF),
            pltpu.VMEM((8, 128, D), BF),
            pltpu.VMEM((8, 128, D), BF),
            pltpu.VMEM((4, 128, 768), BF),
            pltpu.VMEM((128, D), BF),
            pltpu.VMEM((4, 128, D), BF),
            pltpu.VMEM((4, 128, D), BF),
            pltpu.VMEM((3, 128, 768), BF),
            pltpu.VMEM((3, 128, D), BF),
            pltpu.VMEM((3, 128, D), BF),
            pltpu.VMEM((3, 128, D), BF),
            pltpu.VMEM((8, 16, 128), F32),
            pltpu.VMEM((7, 16, 128), F32),
            pltpu.VMEM((4, 16, 128), F32),
            pltpu.SemaphoreType.DMA((160,)),
            pltpu.SemaphoreType.DMA((160,)),
            pltpu.SemaphoreType.DMA((24,)),
        ],
        compiler_params=pltpu.CompilerParams(
            collective_id=0, has_side_effects=True, vmem_limit_bytes=VMEM_LIMIT
        ),
        cost_estimate=pl.CostEstimate(flops=26_000_000_000, bytes_accessed=30_000_000, transcendentals=8_000_000),
    )(xin, dmin, bias, pack, qkv_weight, out_weight, up_weight, down_weight)
    out, d_input, gq, go, gu, gd, small = outs
    line = shape((128,), F32)
    grads = pl.pallas_call(
        widen_kernel,
        out_shape=(
            line, line, shape((128, 3 * D), F32), line, line, shape((128, D), F32), line, line, line,
            shape((128, 4 * D), F32), shape((512,), F32), shape((512, D), F32), line,
        ),
        in_specs=[vm] * 5,
        out_specs=(vm,) * 13,
        compiler_params=pltpu.CompilerParams(vmem_limit_bytes=WIDEN_LIMIT),
    )(gq, go, gu, gd, small)
    return (out[:, :tok], d_input[:, :tok]) + tuple(grads)


def solution(mesh):
    in_specs = (
        P("shard", "seq", None),
        P("shard", None),
        P("shard", "seq", None),
        P("shard"),
        P("shard"),
        P("shard", None),
        P("shard"),
        P("shard"),
        P("shard", None),
        P("shard"),
        P("shard"),
        P("shard"),
        P("shard", None),
        P("shard"),
        P("shard", None),
        P("shard"),
    )
    out_specs = (
        P("shard", "seq", None),
        P("shard", "seq", None),
        P("shard"),
        P("shard"),
        P("shard", None),
        P("shard"),
        P("shard"),
        P("shard", None),
        P("shard"),
        P("shard"),
        P("shard"),
        P("shard", None),
        P("shard"),
        P("shard", None),
        P("shard"),
    )
    fits = dict(mesh.shape) == {"seq": NSEQ, "shard": NSH}
    return jax.shard_map(
        fused_device if fits else per_device, mesh=mesh, in_specs=in_specs, out_specs=out_specs, check_vma=False
    )
```

```python
import jax
import jax.numpy as jnp
from jax import lax
from jax.experimental import pallas as pl
from jax.experimental.pallas import tpu as pltpu
from jax.sharding import PartitionSpec as P

D = 1024
HEAD_DIM = 64


EPSILON = 1e-05


def product(left, right):
    return jnp.dot(left, right, preferred_element_type=jnp.float32)


def product_tn(left, right):
    return lax.dot_general(
        left, right, (((0,), (0,)), ((), ())), preferred_element_type=jnp.float32
    )


def product_nt(left, right):
    return lax.dot_general(
        left, right, (((1,), (1,)), ((), ())), preferred_element_type=jnp.float32
    )


def norm_rows(current, gain, shift):
    centre = jnp.mean(current, axis=-1, keepdims=True)
    centred = current - centre
    inverse = lax.rsqrt(jnp.mean(centred * centred, axis=-1, keepdims=True) + EPSILON)
    scaled = centred * inverse
    return (scaled * gain + shift, scaled, inverse)


def norm_back(incoming, scaled, inverse, gain):
    inner = incoming * gain
    d_current = inverse * (
        inner
        - jnp.mean(inner, axis=-1, keepdims=True)
        - scaled * jnp.mean(inner * scaled, axis=-1, keepdims=True)
    )
    return (d_current, jnp.sum(incoming * scaled, axis=0), jnp.sum(incoming, axis=0))


def split_heads(block):
    images, length, width = block.shape
    return block.reshape(images, length, width // HEAD_DIM, HEAD_DIM)


def masked_scores(query_h, keyed_h, key_mask):
    scores = jnp.einsum("iqhd,ikhd->ihqk", query_h, keyed_h, preferred_element_type=jnp.float32)
    scores = scores * HEAD_DIM ** (-0.5)
    return jnp.where(key_mask[:, None, None, :] > 0, scores, -1e30)


def layer_forward(current, key_mask, weights, images):
    (
        attn_gain,
        attn_shift,
        qkv_weight,
        query_bias,
        value_bias,
        out_weight,
        out_bias,
        mlp_gain,
        mlp_shift,
        up_weight,
        up_bias,
        down_weight,
        down_bias,
    ) = weights
    row_count = current.shape[0]
    tok_local = row_count // images
    normed, scaled_a, inverse_a = norm_rows(
        current, attn_gain.astype(jnp.float32), attn_shift.astype(jnp.float32)
    )
    normed_low = normed.astype(jnp.bfloat16)
    packed_bias = jnp.concatenate(
        [
            query_bias.astype(jnp.float32),
            jnp.zeros((D,), jnp.float32),
            value_bias.astype(jnp.float32),
        ]
    )
    packed = (product(normed_low, qkv_weight) + packed_bias).astype(jnp.bfloat16)
    packed = packed.reshape(images, tok_local, 3, D)
    head_view = lax.all_to_all(packed, "seq", split_axis=3, concat_axis=1, tiled=True)
    query_h = split_heads(head_view[:, :, 0])
    keyed_h = split_heads(head_view[:, :, 1])
    value_h = split_heads(head_view[:, :, 2])
    scores = masked_scores(query_h, keyed_h, key_mask)
    row_max = jnp.max(scores, axis=-1, keepdims=True)
    raised = jnp.exp(scores - row_max)
    row_sum = jnp.sum(raised, axis=-1, keepdims=True)
    attn_probs = raised / row_sum
    log_total = row_max + jnp.log(row_sum)
    mixed = jnp.einsum(
        "ihqk,ikhd->iqhd",
        attn_probs.astype(jnp.bfloat16),
        value_h,
        preferred_element_type=jnp.float32,
    )
    seq_len = head_view.shape[1]
    mixed = mixed.reshape(images, seq_len, head_view.shape[3]).astype(jnp.bfloat16)
    merged = lax.all_to_all(mixed, "seq", split_axis=1, concat_axis=2, tiled=True)
    merged_rows = merged.reshape(row_count, D)
    middle = current + product(merged_rows, out_weight) + out_bias.astype(jnp.float32)
    second, scaled_b, inverse_b = norm_rows(
        middle, mlp_gain.astype(jnp.float32), mlp_shift.astype(jnp.float32)
    )
    second_low = second.astype(jnp.bfloat16)
    hidden = product(second_low, up_weight) + up_bias.astype(jnp.float32)
    active = (hidden * jax.nn.sigmoid(1.702 * hidden)).astype(jnp.bfloat16)
    result = middle + product(active, down_weight) + down_bias.astype(jnp.float32)
    stored = (
        scaled_a,
        inverse_a,
        normed_low,
        head_view,
        log_total,
        merged_rows,
        scaled_b,
        inverse_b,
        second_low,
        hidden,
        active,
    )
    return (result, stored)


def layer_backward(upstream, key_mask, weights, stored, images):
    (
        attn_gain,
        attn_shift,
        qkv_weight,
        query_bias,
        value_bias,
        out_weight,
        out_bias,
        mlp_gain,
        mlp_shift,
        up_weight,
        up_bias,
        down_weight,
        down_bias,
    ) = weights
    (
        scaled_a,
        inverse_a,
        normed_low,
        head_view,
        log_total,
        merged_rows,
        scaled_b,
        inverse_b,
        second_low,
        hidden,
        active,
    ) = stored
    row_count = upstream.shape[0]
    tok_local = row_count // images
    branch_low = upstream.astype(jnp.bfloat16)
    grad_down_bias = jnp.sum(branch_low, axis=0, dtype=jnp.float32)
    grad_down_weight = product_tn(active, branch_low)
    d_active = product_nt(branch_low, down_weight)
    gate_sig = jax.nn.sigmoid(1.702 * hidden)
    d_hidden = (d_active * (gate_sig + 1.702 * hidden * gate_sig * (1.0 - gate_sig))).astype(
        jnp.bfloat16
    )
    grad_up_bias = jnp.sum(d_hidden, axis=0, dtype=jnp.float32)
    grad_up_weight = product_tn(second_low, d_hidden)
    d_second = product_nt(d_hidden, up_weight)
    d_norm_b, grad_mlp_gain, grad_mlp_shift = norm_back(
        d_second, scaled_b, inverse_b, mlp_gain.astype(jnp.float32)
    )
    d_middle = upstream + d_norm_b
    d_branch = d_middle.astype(jnp.bfloat16)
    grad_out_bias = jnp.sum(d_branch, axis=0, dtype=jnp.float32)
    grad_out_weight = product_tn(merged_rows, d_branch)
    d_merged = product_nt(d_branch, out_weight).astype(jnp.bfloat16).reshape(images, tok_local, D)
    d_heads = lax.all_to_all(d_merged, "seq", split_axis=2, concat_axis=1, tiled=True)
    query_h = split_heads(head_view[:, :, 0])
    keyed_h = split_heads(head_view[:, :, 1])
    value_h = split_heads(head_view[:, :, 2])
    d_out_h = split_heads(d_heads)
    scores = masked_scores(query_h, keyed_h, key_mask)
    attn_probs = jnp.exp(scores - log_total)
    d_value = jnp.einsum(
        "ihqk,iqhd->ikhd",
        attn_probs.astype(jnp.bfloat16),
        d_out_h,
        preferred_element_type=jnp.float32,
    )
    d_probs = jnp.einsum("iqhd,ikhd->ihqk", d_out_h, value_h, preferred_element_type=jnp.float32)
    d_scores = attn_probs * (d_probs - jnp.sum(attn_probs * d_probs, axis=-1, keepdims=True))
    d_scores = d_scores.astype(jnp.bfloat16)
    d_query = jnp.einsum(
        "ihqk,ikhd->iqhd", d_scores, keyed_h, preferred_element_type=jnp.float32
    ) * HEAD_DIM ** (-0.5)
    d_key = jnp.einsum(
        "ihqk,iqhd->ikhd", d_scores, query_h, preferred_element_type=jnp.float32
    ) * HEAD_DIM ** (-0.5)
    seq_len = head_view.shape[1]
    d_packed = jnp.stack((d_query, d_key, d_value), axis=2).astype(jnp.bfloat16)
    d_packed = d_packed.reshape(images, seq_len, 3, head_view.shape[3])
    d_tokens = lax.all_to_all(d_packed, "seq", split_axis=1, concat_axis=3, tiled=True).reshape(
        row_count, 3 * D
    )
    grad_query_bias = jnp.sum(d_tokens[:, :D], axis=0, dtype=jnp.float32)
    grad_value_bias = jnp.sum(d_tokens[:, 2 * D :], axis=0, dtype=jnp.float32)
    grad_qkv_weight = product_tn(normed_low, d_tokens)
    d_normed = product_nt(d_tokens, qkv_weight)
    d_norm_a, grad_attn_gain, grad_attn_shift = norm_back(
        d_normed, scaled_a, inverse_a, attn_gain.astype(jnp.float32)
    )
    grads = (
        grad_attn_gain,
        grad_attn_shift,
        grad_qkv_weight,
        grad_query_bias,
        grad_value_bias,
        grad_out_weight,
        grad_out_bias,
        grad_mlp_gain,
        grad_mlp_shift,
        grad_up_weight,
        grad_up_bias,
        grad_down_weight,
        grad_down_bias,
    )
    return (d_middle + d_norm_a, grads)


def reduce_grads(grads):
    shares = (
        lax.psum_scatter(
            grads[0].astype(jnp.bfloat16), "shard", scatter_dimension=0, tiled=True
        ).astype(jnp.float32),
        lax.psum_scatter(
            grads[1].astype(jnp.bfloat16), "shard", scatter_dimension=0, tiled=True
        ).astype(jnp.float32),
        lax.psum_scatter(
            grads[2].astype(jnp.bfloat16), "shard", scatter_dimension=0, tiled=True
        ).astype(jnp.float32),
        lax.psum_scatter(
            grads[3].astype(jnp.bfloat16), "shard", scatter_dimension=0, tiled=True
        ).astype(jnp.float32),
        lax.psum_scatter(
            grads[4].astype(jnp.bfloat16), "shard", scatter_dimension=0, tiled=True
        ).astype(jnp.float32),
        lax.psum_scatter(
            grads[5].astype(jnp.bfloat16), "shard", scatter_dimension=0, tiled=True
        ).astype(jnp.float32),
        lax.psum_scatter(
            grads[6].astype(jnp.bfloat16), "shard", scatter_dimension=0, tiled=True
        ).astype(jnp.float32),
        lax.psum_scatter(
            grads[7].astype(jnp.bfloat16), "shard", scatter_dimension=0, tiled=True
        ).astype(jnp.float32),
        lax.psum_scatter(
            grads[8].astype(jnp.bfloat16), "shard", scatter_dimension=0, tiled=True
        ).astype(jnp.float32),
        lax.psum_scatter(
            grads[9].astype(jnp.bfloat16), "shard", scatter_dimension=0, tiled=True
        ).astype(jnp.float32),
        lax.psum_scatter(
            grads[10].astype(jnp.bfloat16), "shard", scatter_dimension=0, tiled=True
        ).astype(jnp.float32),
        lax.psum_scatter(
            grads[11].astype(jnp.bfloat16), "shard", scatter_dimension=0, tiled=True
        ).astype(jnp.float32),
        lax.psum_scatter(
            grads[12].astype(jnp.bfloat16), "shard", scatter_dimension=0, tiled=True
        ).astype(jnp.float32),
    )
    return (
        lax.psum(shares[0].astype(jnp.bfloat16), "seq").astype(jnp.float32),
        lax.psum(shares[1].astype(jnp.bfloat16), "seq").astype(jnp.float32),
        lax.psum(shares[2].astype(jnp.bfloat16), "seq").astype(jnp.float32),
        lax.psum(shares[3].astype(jnp.bfloat16), "seq").astype(jnp.float32),
        lax.psum(shares[4].astype(jnp.bfloat16), "seq").astype(jnp.float32),
        lax.psum(shares[5].astype(jnp.bfloat16), "seq").astype(jnp.float32),
        lax.psum(shares[6].astype(jnp.bfloat16), "seq").astype(jnp.float32),
        lax.psum(shares[7].astype(jnp.bfloat16), "seq").astype(jnp.float32),
        lax.psum(shares[8].astype(jnp.bfloat16), "seq").astype(jnp.float32),
        lax.psum(shares[9].astype(jnp.bfloat16), "seq").astype(jnp.float32),
        lax.psum(shares[10].astype(jnp.bfloat16), "seq").astype(jnp.float32),
        lax.psum(shares[11].astype(jnp.bfloat16), "seq").astype(jnp.float32),
        lax.psum(shares[12].astype(jnp.bfloat16), "seq").astype(jnp.float32),
    )


def per_device(
    inputs,
    key_mask,
    cotangent,
    attn_gain,
    attn_shift,
    qkv_weight,
    query_bias,
    value_bias,
    out_weight,
    out_bias,
    mlp_gain,
    mlp_shift,
    up_weight,
    up_bias,
    down_weight,
    down_bias,
):
    shard_set = (
        attn_gain,
        attn_shift,
        qkv_weight,
        query_bias,
        value_bias,
        out_weight,
        out_bias,
        mlp_gain,
        mlp_shift,
        up_weight,
        up_bias,
        down_weight,
        down_bias,
    )
    images = inputs.shape[0]
    tok_local = inputs.shape[1]
    row_count = images * tok_local
    current = inputs.astype(jnp.float32).reshape(row_count, D)
    gathered = (
        lax.all_gather(shard_set[0], "shard", axis=0, tiled=True),
        lax.all_gather(shard_set[1], "shard", axis=0, tiled=True),
        lax.all_gather(shard_set[2], "shard", axis=0, tiled=True),
        lax.all_gather(shard_set[3], "shard", axis=0, tiled=True),
        lax.all_gather(shard_set[4], "shard", axis=0, tiled=True),
        lax.all_gather(shard_set[5], "shard", axis=0, tiled=True),
        lax.all_gather(shard_set[6], "shard", axis=0, tiled=True),
        lax.all_gather(shard_set[7], "shard", axis=0, tiled=True),
        lax.all_gather(shard_set[8], "shard", axis=0, tiled=True),
        lax.all_gather(shard_set[9], "shard", axis=0, tiled=True),
        lax.all_gather(shard_set[10], "shard", axis=0, tiled=True),
        lax.all_gather(shard_set[11], "shard", axis=0, tiled=True),
        lax.all_gather(shard_set[12], "shard", axis=0, tiled=True),
    )
    result, stored = layer_forward(current, key_mask, gathered, images)
    output = result.astype(jnp.bfloat16).reshape(images, tok_local, D)
    start_row = lax.axis_index("seq") * tok_local
    own_mask = lax.dynamic_slice_in_dim(key_mask, start_row, tok_local, 1).astype(jnp.float32)
    upstream = (cotangent.astype(jnp.float32) * own_mask[:, :, None]).reshape(row_count, D)
    again = (
        lax.all_gather(shard_set[0], "shard", axis=0, tiled=True),
        lax.all_gather(shard_set[1], "shard", axis=0, tiled=True),
        lax.all_gather(shard_set[2], "shard", axis=0, tiled=True),
        lax.all_gather(shard_set[3], "shard", axis=0, tiled=True),
        lax.all_gather(shard_set[4], "shard", axis=0, tiled=True),
        lax.all_gather(shard_set[5], "shard", axis=0, tiled=True),
        lax.all_gather(shard_set[6], "shard", axis=0, tiled=True),
        lax.all_gather(shard_set[7], "shard", axis=0, tiled=True),
        lax.all_gather(shard_set[8], "shard", axis=0, tiled=True),
        lax.all_gather(shard_set[9], "shard", axis=0, tiled=True),
        lax.all_gather(shard_set[10], "shard", axis=0, tiled=True),
        lax.all_gather(shard_set[11], "shard", axis=0, tiled=True),
        lax.all_gather(shard_set[12], "shard", axis=0, tiled=True),
    )
    d_input, grads = layer_backward(upstream, key_mask, again, stored, images)
    reduced = reduce_grads(grads)
    input_grad = d_input.astype(jnp.bfloat16).reshape(images, tok_local, D)
    return (
        output,
        input_grad,
        reduced[0],
        reduced[1],
        reduced[2],
        reduced[3],
        reduced[4],
        reduced[5],
        reduced[6],
        reduced[7],
        reduced[8],
        reduced[9],
        reduced[10],
        reduced[11],
        reduced[12],
    )


STEPS = (1, 3, 2)
PUMPS = (1, 1, 1, 0, 0, 0, 0, 1, 1, 1, 1, 1, 1, 0, 1)
LIMITS = (2, 3, 3, 4, 6, 7, 8, 9, 10, 10, 10)
MT = 640
FLIGHT = 99
NSEQ = 4
NSH = 8
TOK = 160
ROWS = NSEQ * TOK
HEADS_DEV = 4
MASKED = -1e30
VMEM_LIMIT = 64 * 1024 * 1024 - 1024 * 1024
WIDEN_LIMIT = 64 * 1024 * 1024 - 1024 * 1024
MESH_ID = pl.DeviceIdType.MESH
BF = jnp.bfloat16
F32 = jnp.float32
GATE = 1.702


def dot_nn(left, right):
    return lax.dot_general(left, right, (((1,), (0,)), ((), ())), preferred_element_type=F32)


def dot_nt(left, right):
    return lax.dot_general(left, right, (((1,), (1,)), ((), ())), preferred_element_type=F32)


def dot_tn(left, right):
    return lax.dot_general(left, right, (((0,), (0,)), ((), ())), preferred_element_type=F32)


def layer_kernel(
    inp, cot, kmask, b0, b1, b2, b3, b4, b5, b6, b7, b8, wq_h, wo_h, wu_h, wd_h,
    out_o, dx_o, gq_o, go_o, gu_o, gd_o, sg_o,
    xin, dmin, pack, bias_t, xg, wq, wo, wu, wd, pg, qkv, dqkv, probs, mixt, mixed, part, rc, rx, rc2, rx2,
    hid, cg, act, gate, dmg, dhid, dmix,
    gq, go, gu, gd, ryq, ryo, ryu, ryd, rzq, rzo, rzu, rzd, sgs, sg1, sg2,
    ssem, rsem, lsem,
):
    s = lax.axis_index("seq")
    j = lax.axis_index("shard")
    x, k = s // 2, s % 2
    z, y = j // 2, j % 2
    zs = k * 2 + x
    s_core = x * 2 + (1 - k)
    s_x = (1 - x) * 2 + k
    s_diag = (1 - x) * 2 + (1 - k)
    j_y = z * 2 + (1 - y)
    core = (s_core, j)
    xdev = (s_x, j)
    ydev = (s, j_y)

    def zj(d):
        return lax.rem(z + d, 4) * 2 + y

    ids = {}

    def ix(*key):
        return ids.setdefault(key, len(ids))

    pending = {}

    def send(tag, key, src, dst, dev):
        n = ix(*key)
        copy = pltpu.make_async_remote_copy(
            src_ref=src, dst_ref=dst, send_sem=ssem.at[n], recv_sem=rsem.at[n],
            device_id=dev, device_id_type=MESH_ID)
        copy.start()
        pending.setdefault(tag, []).append(copy)

    def sent(tag):
        for copy in pending.pop(tag, []):
            copy.wait_send()

    def arrived(key, dst, dev):
        n = ix(*key)
        pltpu.make_async_remote_copy(
            src_ref=dst, dst_ref=dst, send_sem=ssem.at[n], recv_sem=rsem.at[n],
            device_id=dev, device_id_type=MESH_ID).wait_recv()

    local = {}

    def load(key, src, dst):
        copy = pltpu.make_async_copy(src, dst, lsem.at[local.setdefault(key, len(local))])
        copy.start()
        return copy

    def rows(block):
        return pl.ds(pl.multiple_of(block * TOK, TOK), TOK)

    def tiles(count, step, body, init=None, unroll=False):
        def inner(t, carry):
            return body(pl.multiple_of(t * step, step), carry)
        return lax.fori_loop(0, count // step, inner, init, unroll=unroll)

    barrier = pltpu.get_barrier_semaphore()
    for d in range(1, NSEQ):
        pl.semaphore_signal(barrier, inc=1, device_id=(lax.rem(s + d, NSEQ), j), device_id_type=MESH_ID)
    for d in range(1, NSH):
        pl.semaphore_signal(barrier, inc=1, device_id=(s, lax.rem(j + d, NSH)), device_id_type=MESH_ID)
    loads_q = [load(("wq", c), wq_h.at[:, pl.ds(pl.multiple_of(1024 * c + 256 * zs, 256), 256)],
                    wq.at[j, :, pl.ds(256 * c, 256)]) for c in range(3)]
    loads_u = [load(("wu", c), wu_h.at[:, pl.ds(pl.multiple_of(512 * c + 128 * s, 128), 128)],
                    wu.at[j, :, pl.ds(128 * c, 128)]) for c in range(8)]
    load_d = load(("wd",), wd_h.at[pl.ds(pl.multiple_of(128 * s, 128), 128)], wd.at[j])
    for row, ref in enumerate((b0, b1, b2, b3, b4, b5, b6, b7)):
        pack[row:row + 1, :] = ref[...].astype(F32)
    own_row = lax.broadcasted_iota(jnp.int32, (NSEQ, 128), 0) == s
    pack[8:9, :] = jnp.sum(jnp.where(own_row, b8[...].astype(F32), 0.0), axis=0, keepdims=True)
    pack[9:16, :] = jnp.zeros((7, 128), F32)
    pg[j] = pack[...]

    tok = inp.shape[0]

    def slots_of(source, i):
        row = lax.broadcasted_iota(jnp.int32, (TOK, 2 * tok), 0)
        col = lax.broadcasted_iota(jnp.int32, (TOK, 2 * tok), 1)
        chosen = (col == 2 * row + i).astype(F32).astype(BF)
        return dot_nn(chosen, source[...].reshape(2 * tok, D))
    for i in range(2):
        xin[i] = slots_of(inp, i).astype(BF)
    n_wo = local.setdefault("wo", len(local))

    @pl.when(z == zs)
    def _():
        pltpu.make_async_copy(wo_h, wo.at[y], lsem.at[n_wo]).start()
    pl.semaphore_wait(barrier, NSEQ - 1 + NSH - 1)

    def ag4_start(key, buf, i, src):
        send(key, (key, "c", i), src, buf.at[i, rows(s)], core)
        send(key, (key, "x", i), src, buf.at[i, rows(s)], xdev)

    def ag4_forward(key, buf, i):
        arrived((key, "x", i), buf.at[i, rows(s_x)], xdev)
        send(key + "f", (key, "d", i), buf.at[i, rows(s_x)], buf.at[i, rows(s_x)], core)

    def ag4_end(key, buf, i):
        arrived((key, "c", i), buf.at[i, rows(s_core)], core)
        arrived((key, "d", i), buf.at[i, rows(s_diag)], core)

    weights = {"wq": wq, "wu": wu, "wd": wd}
    n_oz, n_oy = [ix("wo", d) for d in (1, 2, 3)], ix("wo", "y")

    def out_copy(d):
        return pltpu.make_async_remote_copy(
            src_ref=wo.at[y], dst_ref=wo.at[y], send_sem=ssem.at[n_oz[d - 1]], recv_sem=rsem.at[n_oz[0]],
            device_id=(s, zj(d)), device_id_type=MESH_ID)

    def out_start():
        @pl.when(z == zs)
        def _():
            pltpu.make_async_copy(wo_h, wo.at[y], lsem.at[n_wo]).wait()
            for d in (2, 1, 3):
                out_copy(d).start()

    def out_forward():
        @pl.when(z != zs)
        def _():
            pltpu.make_async_remote_copy(
                src_ref=wo.at[y], dst_ref=wo.at[y], send_sem=ssem.at[n_oz[0]], recv_sem=rsem.at[n_oz[0]],
                device_id=(s, zs * 2 + y), device_id_type=MESH_ID).wait_recv()
        send("wo", ("wo", "y"), wo.at[y], wo.at[y], ydev)

    def block_rows(d):
        return (2, pl.ds(64 * (d - 20), 64)) if d >= 20 else (d, pl.ds(0, 128))

    def gather_start(key, d):
        if key == "wo":
            out_start()
            return
        buf = weights[key]
        if d == 1:
            send(key, (key, "y", 0), buf.at[j], buf.at[j], ydev)
        step, part_rows = block_rows(d)
        mine = buf.at[j, part_rows]
        send(key, (key, "z", d), mine, mine, (s, zj(step)))

    def gather_forward(key, d):
        if key == "wo":
            out_forward()
            return
        buf = weights[key]
        step, part_rows = block_rows(d)
        jf = zj(4 - step)
        block = buf.at[jf, part_rows]
        arrived((key, "z", d), block, (s, jf))
        send(key, (key, "y", d), block, block, ydev)

    issue_order = [("wq", d) for d in STEPS] + [("wo", 0)]
    issue_order += [(key, d) for key in ("wu", "wd") for d in STEPS]
    rounds = list(issue_order)
    at_round, issued = [0], [0]

    def gather_issue(upto):
        while issued[0] < min(upto, len(rounds)):
            gather_start(*issue_order[issued[0]])
            issued[0] += 1

    def pump(place):
        for _step in range(PUMPS[place]):
            n = at_round[0]
            gather_forward(*rounds[n])
            at_round[0] = n + 1
            gather_issue(LIMITS[n + 1])

    def agw_end(key, buf):
        for d in (0,) + STEPS:
            step, part_rows = block_rows(d)
            jf = lax.rem(z + 4 - step, 4) * 2 + (1 - y)
            arrived((key, "y", d), buf.at[jf, part_rows], ydev)

    def rs4_a(key, i, rcb):
        send(key, (key, "c0", i), part.at[i, rows(s_core)], rcb.at[i, 0], core)
        send(key, (key, "c1", i), part.at[i, rows(s_diag)], rcb.at[i, 1], core)

    def rs4_b(key, i, rcb, rxb):
        arrived((key, "c1", i), rcb.at[i, 1], core)

        def add(r, _):
            here = pl.ds(pl.multiple_of(s_x * TOK + r, 32), 32)
            total = part[i, here, :].astype(F32) + rcb[i, 1, pl.ds(r, 32), :].astype(F32)
            part[i, here, :] = total.astype(BF)
        tiles(TOK, 32, add, unroll=True)
        send(key, (key, "x", i), part.at[i, rows(s_x)], rxb.at[i], xdev)

    def rs4_wait(key, i, rcb, rxb):
        arrived((key, "c0", i), rcb.at[i, 0], core)
        arrived((key, "x", i), rxb.at[i], xdev)

    def rs4_sum(i, r, rcb, rxb):
        here = pl.ds(pl.multiple_of(s * TOK + r, 32), 32)
        return (part[i, here, :].astype(F32) + rcb[i, 0, pl.ds(r, 32), :].astype(F32)
                + rxb[i, pl.ds(r, 32), :].astype(F32))

    def add_into(g, row, others):
        def add(r, _):
            total = g[row, pl.ds(r, 32), :].astype(F32)
            for ref, at in others:
                total = total + ref[at, pl.ds(r, 32), :].astype(F32)
            g[row, pl.ds(r, 32), :] = total.astype(BF)
        tiles(128, 32, add, unroll=True)

    waiting, flying = [], []

    def reduce_fill():
        while waiting and len(flying) < FLIGHT:
            piece = waiting.pop(0)
            key, d, g, ry, rz = piece
            if key == "o":
                send("go", ("go", "y"), g.at[1 - y], ry, ydev)
            else:
                send(key, (key, "gy", d), g.at[lax.rem(z + d, 4) * 2 + (1 - y)], ry.at[d], ydev)
            flying.append(piece)

    def reduce_add(key, g, ry, rz):
        for d in ((0,) if key == "o" else (2, 1, 3, 0)):
            waiting.append((key, d, g, ry, rz))
        reduce_fill()

    def reduce_step(count=1):
        for _step in range(count):
            key, d, g, ry, rz = flying.pop(0)
            if key == "o":
                arrived(("go", "y"), ry, ydev)
                reduce_fill()
                add_out_block()
                continue
            arrived((key, "gy", d), ry.at[d], ydev)
            reduce_fill()
            add_into(g, zj(d), [(ry, d)])
            if d:
                send(key, (key, "gz", d), g.at[zj(d)], rz.at[d - 1], (s, zj(d)))

    n_gz = [ix("goz", d) for d in range(3)]
    n_gs = ix("gozs")

    def out_grad_copy(slot):
        return pltpu.make_async_remote_copy(
            src_ref=go.at[y], dst_ref=rzo.at[slot], send_sem=ssem.at[n_gs], recv_sem=rsem.at[n_gz[0] + slot],
            device_id=(s, zs * 2 + y), device_id_type=MESH_ID)

    def add_out_block():
        def add_out(r, _):
            total = go[y, pl.ds(r, 32), :].astype(F32) + ryo[pl.ds(r, 32), :].astype(F32)
            go[y, pl.ds(r, 32), :] = total.astype(BF)
        tiles(128, 32, add_out, unroll=True)

        @pl.when(z != zs)
        def _():
            out_grad_copy(lax.rem(z + 3 - zs, 4)).start()

    def rsw_end(key, g, rz, g_o):
        for d in (2, 1, 3):
            arrived((key, "gz", d), rz.at[d - 1], (s, zj(4 - d)))
        add_into(g, j, [(rz, 0), (rz, 1), (rz, 2)])
        copy = load((key, "go"), g.at[j], g_o.at[s])
        send(key, (key, "gc"), g.at[j], g_o.at[s], core)
        send(key, (key, "gx"), g.at[j], g_o.at[s], xdev)
        return copy

    def rsw_forward(key, g_o):
        arrived((key, "gx"), g_o.at[s_x], xdev)
        send(key, (key, "gd"), g_o.at[s_x], g_o.at[s_x], core)

    def rsw_done(key, g_o):
        arrived((key, "gc"), g_o.at[s_core], core)
        arrived((key, "gd"), g_o.at[s_diag], core)

    def param(p):
        return jnp.concatenate([pg[b, pl.ds(p, 1), :] for b in range(NSH)], axis=1)

    def head_param(p):
        return jnp.concatenate([pg[2 * zs, pl.ds(p, 1), :], pg[2 * zs + 1, pl.ds(p, 1), :]], axis=1)

    def normal(value):
        centre = jnp.mean(value, axis=-1, keepdims=True)
        centred = value - centre
        inverse = lax.rsqrt(jnp.mean(centred * centred, axis=-1, keepdims=True) + EPSILON)
        return centred * inverse, inverse

    def normal_back(incoming, scaled, inverse, gain):
        inner = incoming * gain
        return inverse * (inner - jnp.mean(inner, axis=-1, keepdims=True)
                          - scaled * jnp.mean(inner * scaled, axis=-1, keepdims=True))

    def fold(value):
        return value[0:8] + value[8:16] + value[16:24] + value[24:32]

    for d in range(1, NSH):
        send("pk", ("pk", d), pack, pg.at[j], (s, lax.rem(j + d, NSH)))
    for i in range(2):
        ag4_start("xg", xg, i, xin.at[i])
    for copy in loads_q:
        copy.wait()
    gather_issue(LIMITS[0])
    slot = lax.broadcasted_iota(jnp.int32, (ROWS, 1), 0)
    shift = sum(jnp.where(slot >= TOK * b, TOK - tok, 0) for b in range(1, NSEQ))
    used = slot - sum(jnp.where(slot >= TOK * b, TOK, 0) for b in range(1, NSEQ)) < tok
    place_of = jnp.where(used, slot - shift, -1)
    chosen = lax.broadcasted_iota(jnp.int32, (ROWS, kmask.shape[1]), 1) == place_of
    live = dot_nt(chosen.astype(F32).astype(BF), kmask[...].astype(F32).astype(BF))
    bias_t[:, 0:2] = jnp.where(live > 0.5, 0.0, MASKED)
    for i in range(2):
        mask = bias_t[pl.ds(pl.multiple_of(s * TOK, TOK), TOK), i:i + 1]
        dmin[i] = jnp.where(mask == 0.0, slots_of(cot, i), 0.0).astype(BF)
        xg[i, rows(s), :] = xin[i]
        dmg[i, rows(s), :] = dmin[i]
    for copy in loads_u:
        copy.wait()
    load_d.wait()
    pump(0)
    ag4_forward("xg", xg, 0)

    for d in range(1, NSH):
        jf = lax.rem(j + NSH - d, NSH)
        arrived(("pk", d), pg.at[jf], (s, jf))
    attn_gain, attn_shift = param(0), param(1)

    def norm_block(i, block):
        def body(r, _):
            here = pl.ds(pl.multiple_of(block * TOK + r, 32), 32)
            scaled, _inverse = normal(xg[i, here, :].astype(F32))
            xg[i, here, :] = (scaled * attn_gain + attn_shift).astype(BF)
        tiles(TOK, 32, body, unroll=True)

    norm_block(0, s)
    norm_block(1, s)
    pump(1)
    for i in range(2):
        arrived(("xg", "c", i), xg.at[i, rows(s_core)], core)
        norm_block(i, s_core)
    ag4_forward("xg", xg, 1)
    for i in range(2):
        ag4_start("dm", dmg, i, dmin.at[i])
    arrived(("xg", "d", 0), xg.at[0, rows(s_diag)], core)
    norm_block(0, s_diag)
    sent("xgf")
    pump(2)
    norm_block(0, s_x)
    norm_block(1, s_x)
    arrived(("xg", "d", 1), xg.at[1, rows(s_diag)], core)
    norm_block(1, s_diag)
    pump(3)
    agw_end("wq", wq)

    packed_bias = jnp.concatenate([head_param(2), jnp.zeros((1, 256), F32), head_param(3)], axis=1)

    def project_in(i):
        def project(r, _):
            here = pl.ds(r, MT)
            value = dot_nn(xg[i, here, :], wq[...].reshape(D, 768)) + packed_bias
            qkv[i, here, :] = value.astype(BF)
        tiles(ROWS, MT, project)

    def attend(i, first, last):
        if first == 0:
            mixt[...] = qkv[i, :, 512:768].astype(F32).T.astype(BF)
        lane = lax.broadcasted_iota(jnp.int32, (1, 256), 1) // HEAD_DIM

        def one_head(h, _):
            keyed = jnp.where(lane == h, qkv[i, :, 256:512], jnp.zeros((), BF))
            query = qkv[i, :, 0:256] * jnp.asarray(HEAD_DIM ** -0.5, BF)
            scores = dot_nt(keyed, query) + bias_t[:, i:i + 1]
            raised = jnp.exp(scores - jnp.max(scores, axis=0, keepdims=True))
            chances = (raised * (1.0 / jnp.sum(raised, axis=0, keepdims=True))).astype(BF)
            probs[i, h] = chances
            here = pl.ds(pl.multiple_of(h * HEAD_DIM, HEAD_DIM), HEAD_DIM)
            mixt[here, :] = dot_nn(mixt[here, :], chances).astype(BF)
        lax.fori_loop(first, last, one_head, None)
        if last == HEADS_DEV:
            mixed[i] = mixt[...].astype(F32).T.astype(BF)

    def project_out(i):
        def body(r, _):
            here = pl.ds(r, MT)
            part[i, here, :] = dot_nn(mixed[i, here, :], wo[...].reshape(256, D)).astype(BF)
        tiles(ROWS, MT, body)

    project_in(0)
    attend(0, 0, 2)
    pump(14)
    attend(0, 2, 4)
    pump(4)
    project_in(1)
    arrived(("wo", "y"), wo.at[1 - y], ydev)
    project_out(0)
    rs4_a("o", 0, rc)
    pump(5)
    attend(1, 0, 2)
    pump(6)
    attend(1, 2, 4)
    rs4_b("o", 0, rc, rx)
    project_out(1)
    rs4_a("o", 1, rc)
    pump(7)
    rs4_b("o", 1, rc, rx)
    for i in range(2):
        ag4_forward("dm", dmg, i)
    pump(8)

    out_bias, mlp_gain, mlp_shift, down_bias = param(4), param(5), param(6), param(7)
    up_bias = param(8)

    for i in range(2):
        rs4_wait("o", i, rc, rx)

        def middle(r, _, i=i):
            value = xin[i, pl.ds(r, 32), :].astype(F32) + (rs4_sum(i, r, rc, rx) + out_bias)
            hid[i, pl.ds(r, 32), :] = value
            scaled, _inverse = normal(value)
            here = pl.ds(pl.multiple_of(s * TOK + r, 32), 32)
            cg[i, here, :] = (scaled * mlp_gain + mlp_shift).astype(BF)
        tiles(TOK, 32, middle, unroll=True)
        ag4_start("c", cg, i, cg.at[i, rows(s)])
        pump(9 + i)
    for n in range(2):
        ag4_end("dm", dmg, n)
    agw_end("wu", wu)
    for i in range(2):
        ag4_forward("c", cg, i)
        ag4_end("c", cg, i)

        def up(r, _, i=i):
            here = pl.ds(r, MT)
            value = dot_nn(cg[i, here, :], wu[...].reshape(D, D)) + up_bias
            sig = jax.nn.sigmoid(GATE * value)
            act[i, here, :] = (value * sig).astype(BF)
            gate[i, here, :] = (sig + GATE * value * sig * (1.0 - sig)).astype(BF)
        tiles(ROWS, MT, up)
        pump(11 + i)
    sent("o")

    def weight_grad(left, right, g):
        def body(t, _):
            cols = pl.ds(pl.multiple_of(t * 512, 512), 512)
            value = dot_tn(left[:, :, cols].reshape(2 * ROWS, 512), right[...].reshape(2 * ROWS, right.shape[2]))
            g[pl.ds(4 * t, 4)] = value.astype(BF).reshape(4, 128, right.shape[2])
        lax.fori_loop(0, left.shape[2] // 512, body, None)

    weight_grad(act, dmg, gd)
    pump(13)
    reduce_add("d", gd, ryd, rzd)
    agw_end("wd", wd)

    def d_up(i, total):
        def body(r, carry):
            here = pl.ds(r, MT)
            value = dot_nt(dmg[i, here, :], wd[...].reshape(D, D)) * gate[i, here, :].astype(F32)
            value = value.astype(BF)
            gate[i, here, :] = value
            return carry + jnp.sum(value.astype(F32).reshape(MT // 8, 8, D), axis=0)
        return tiles(ROWS, MT, body, total)

    def d_second(i):
        def body(r, _):
            here = pl.ds(r, MT)
            part[i, here, :] = dot_nt(gate[i, here, :], wu[...].reshape(D, D)).astype(BF)
        tiles(ROWS, MT, body)

    sent("dmf")
    sent("dm")
    du_sum = d_up(0, jnp.zeros((8, D), F32))
    d_second(0)
    rs4_a("dc", 0, rc)
    du_sum = d_up(1, du_sum)
    rs4_b("dc", 0, rc, rx)
    d_second(1)
    rs4_a("dc", 1, rc)
    reduce_step()
    rs4_b("dc", 1, rc, rx)
    weight_grad(cg, gate, gu)
    reduce_add("u", gu, ryu, rzu)
    reduce_step()

    zero8 = jnp.zeros((8, D), F32)
    sums = (zero8, zero8, zero8, zero8)
    for i in range(2):
        rs4_wait("dc", i, rc, rx)

        def d_middle(r, carry, i=i):
            mine = pl.ds(r, 32)
            incoming = rs4_sum(i, r, rc, rx)
            scaled, inverse = normal(hid[i, mine, :])
            upstream = dmin[i, mine, :].astype(F32)
            value = upstream + normal_back(incoming, scaled, inverse, mlp_gain)
            dhid[i, mine, :] = value
            low = value.astype(BF)
            dmg[i, pl.ds(pl.multiple_of(s * TOK + r, 32), 32), :] = low
            return (carry[0] + fold(incoming * scaled), carry[1] + fold(incoming),
                    carry[2] + fold(low.astype(F32)), carry[3] + fold(upstream))
        sums = tiles(TOK, 32, d_middle, sums, unroll=True)
        ag4_start("db", dmg, i, dmg.at[i, rows(s)])
        reduce_step()
    sent("dc")

    for i in range(2):
        def down(r, _, i=i):
            here = pl.ds(r, MT)
            part[i, here, :] = dot_nn(act[i, here, :], wd[...].reshape(D, D)).astype(BF)
        tiles(ROWS, MT, down)

    def attend_back(i):
        def d_mixed(r, _):
            here = pl.ds(r, MT)
            dmix[i, here, :] = dot_nt(dmg[i, here, :], wo[...].reshape(256, D)).astype(BF)
        tiles(ROWS, MT, d_mixed)
        lane = lax.broadcasted_iota(jnp.int32, (1, 256), 1) // HEAD_DIM
        mixt[...] = qkv[i, :, 256:512].astype(F32).T.astype(BF)

        def one_head(h, _):
            own = lane == h
            chances = probs[i, h]
            d_value = dot_nn(chances, dmix[i])
            dqkv[i, :, 512:768] = jnp.where(own, d_value.astype(BF), dqkv[i, :, 512:768])
            valued = jnp.where(own, qkv[i, :, 512:768], jnp.zeros((), BF))
            d_chances = dot_nt(valued, dmix[i])
            wide = chances.astype(F32)
            d_scores = wide * (d_chances - jnp.sum(wide * d_chances, axis=0, keepdims=True))
            d_scores = d_scores.astype(BF)
            d_key = dot_nn(d_scores, qkv[i, :, 0:256]) * HEAD_DIM ** -0.5
            dqkv[i, :, 256:512] = jnp.where(own, d_key.astype(BF), dqkv[i, :, 256:512])
            here = pl.ds(pl.multiple_of(h * HEAD_DIM, HEAD_DIM), HEAD_DIM)
            mixt[here, :] = (dot_nn(mixt[here, :], d_scores) * HEAD_DIM ** -0.5).astype(BF)
        lax.fori_loop(0, HEADS_DEV, one_head, None)
        dqkv[i, :, 0:256] = mixt[...].astype(F32).T.astype(BF)

    def out_presum(i):
        arrived(("y", "c0", i), rc2.at[i, 0], core)
        arrived(("y", "c1", i), rc2.at[i, 1], core)

        def body(r, _):
            mine = pl.ds(r, 32)
            here = pl.ds(pl.multiple_of(s * TOK + r, 32), 32)
            there = pl.ds(pl.multiple_of(s_x * TOK + r, 32), 32)
            total = part[i, here, :].astype(F32) + rc2[i, 0, mine, :].astype(F32)
            hid[i, mine, :] = hid[i, mine, :] + (total + down_bias)
            total = part[i, there, :].astype(F32) + rc2[i, 1, mine, :].astype(F32)
            rc2[i, 1, mine, :] = total.astype(BF)
        tiles(TOK, 32, body, unroll=True)

    def d_normed(i):
        def body(r, _):
            here = pl.ds(r, MT)
            part[i, here, :] = dot_nt(dqkv[i, here, :], wq[...].reshape(D, 768)).astype(BF)
        tiles(ROWS, MT, body)
        rs4_a("da", i, rc)

    ag4_forward("db", dmg, 0)
    ag4_end("db", dmg, 0)
    for i in range(2):
        rs4_a("y", i, rc2)
    attend_back(0)
    reduce_step()
    ag4_forward("db", dmg, 1)
    for i in range(2):
        out_presum(i)
    sent("y")
    d_normed(0)
    ag4_end("db", dmg, 1)
    copy_d = rsw_end("d", gd, rzd, gd_o)
    rs4_b("da", 0, rc, rx)
    attend_back(1)
    reduce_step()
    d_normed(1)
    weight_grad(xg, dqkv, gq)
    rs4_b("da", 1, rc, rx)
    value = dot_tn(mixed[...].reshape(2 * ROWS, 256), dmg[...].reshape(2 * ROWS, D))
    go[...] = value.astype(BF).reshape(2, 128, D)
    reduce_add("o", go, ryo, rzo)
    reduce_add("q", gq, ryq, rzq)
    reduce_step()
    for i in range(2):
        send("y", ("y", "x", i), rc2.at[i, 1], rx2.at[i], xdev)
    reduce_step()

    n_gb = [ix("gob", d) for d in range(3)]

    def out_final_copy(d):
        return pltpu.make_async_remote_copy(
            src_ref=go.at[y], dst_ref=go_o, send_sem=ssem.at[n_gb[d - 1]], recv_sem=rsem.at[n_gb[0]],
            device_id=(lax.rem(s + d, 4), j), device_id_type=MESH_ID)
    n_ol = local.setdefault("go", len(local))

    sums_a = (zero8, zero8)
    for i in range(2):
        rs4_wait("da", i, rc, rx)

        def d_input(r, carry, i=i):
            mine = pl.ds(r, 32)
            incoming = rs4_sum(i, r, rc, rx)
            scaled, inverse = normal(xin[i, mine, :].astype(F32))
            value = dhid[i, mine, :] + normal_back(incoming, scaled, inverse, attn_gain)
            dx_o[i, mine, :] = value.astype(BF)
            return carry[0] + fold(incoming * scaled), carry[1] + fold(incoming)
        sums_a = tiles(TOK, 32, d_input, sums_a, unroll=True)
        if i == 0:
            rsw_forward("d", gd_o)
            reduce_step()

    sgs[...] = jnp.zeros_like(sgs)

    def place(row, total):
        for b in range(NSH):
            sgs[b, pl.ds(row, 1), :] = total[:, 128 * b:128 * b + 128]

    def flat(value):
        return jnp.sum(value, axis=0, keepdims=True)
    place(0, flat(sums_a[0]))
    place(1, flat(sums_a[1]))
    place(4, flat(sums[2]))
    place(5, flat(sums[0]))
    place(6, flat(sums[1]))
    place(7, flat(sums[3]))
    d_query_sum = jnp.sum(dqkv[0, :, 0:256].astype(F32) + dqkv[1, :, 0:256].astype(F32), axis=0, keepdims=True)
    d_value_sum = jnp.sum(dqkv[0, :, 512:768].astype(F32) + dqkv[1, :, 512:768].astype(F32), axis=0, keepdims=True)
    for b in range(2):
        sgs[2 * zs + b, pl.ds(2, 1), :] = d_query_sum[:, 128 * b:128 * b + 128]
        sgs[2 * zs + b, pl.ds(3, 1), :] = d_value_sum[:, 128 * b:128 * b + 128]
    up_sum = flat(du_sum)
    row_at = lax.broadcasted_iota(jnp.int32, (8, 128), 0)
    for b in range(NSH):
        wide = jnp.broadcast_to(up_sum[:, 128 * b:128 * b + 128], (8, 128))
        sgs[b, 8:16, :] = jnp.where(row_at == s, wide, 0.0)
    for d in range(1, NSH):
        send("sg", ("sg", d), sgs.at[lax.rem(j + d, NSH)], sg1.at[d - 1], (s, lax.rem(j + d, NSH)))

    copy_u = rsw_end("u", gu, rzu, gu_o)
    reduce_step(2)

    @pl.when(z == zs)
    def _():
        for slot in range(3):
            pltpu.make_async_remote_copy(
                src_ref=go.at[y], dst_ref=rzo.at[slot], send_sem=ssem.at[n_gs], recv_sem=rsem.at[n_gz[slot]],
                device_id=(s, zj(1)), device_id_type=MESH_ID).wait_recv()

        def add(r, _):
            total = go[y, pl.ds(r, 32), :].astype(F32)
            for slot in range(3):
                total = total + rzo[slot, pl.ds(r, 32), :].astype(F32)
            go[y, pl.ds(r, 32), :] = total.astype(BF)
        tiles(128, 32, add, unroll=True)
        pltpu.make_async_copy(go.at[y], go_o, lsem.at[n_ol]).start()
        for d in (1, 2, 3):
            out_final_copy(d).start()

    for d in range(1, NSH):
        jf = lax.rem(j + NSH - d, NSH)
        arrived(("sg", d), sg1.at[d - 1], (s, jf))
    total = sgs[j]
    for d in range(1, NSH):
        total = total + sg1[d - 1]
    sg2[0] = total
    for d in range(1, NSEQ):
        send("sg", ("sh", d), sg2.at[0], sg2.at[d], (lax.rem(s + d, NSEQ), j))
    for i in range(2):
        arrived(("y", "x", i), rx2.at[i], xdev)

        def last(r, _, i=i):
            mine = pl.ds(r, 32)
            out_o[i, mine, :] = (hid[i, mine, :] + rx2[i, mine, :].astype(F32)).astype(BF)
        tiles(TOK, 32, last, unroll=True)
    reduce_step(len(flying) + len(waiting))
    assert not waiting and not flying
    rsw_forward("u", gu_o)
    copy_q = rsw_end("q", gq, rzq, gq_o)
    for d in range(1, NSEQ):
        arrived(("sh", d), sg2.at[d], (lax.rem(s + NSEQ - d, NSEQ), j))
    sg_o[...] = sg2[0] + sg2[1] + sg2[2] + sg2[3]
    rsw_forward("q", gq_o)
    rsw_done("d", gd_o)
    rsw_done("u", gu_o)
    rsw_done("q", gq_o)

    @pl.when(z == zs)
    def _():
        for d in (1, 2, 3):
            out_final_copy(d).wait_send()
        pltpu.make_async_copy(go.at[y], go_o, lsem.at[n_ol]).wait()

    @pl.when(z != zs)
    def _():
        out_final_copy(1).wait_recv()
        out_grad_copy(0).wait_send()
    for copy in (copy_d, copy_u, copy_q):
        copy.wait()

    @pl.when(z == zs)
    def _():
        for d in (1, 2, 3):
            out_copy(d).wait_send()
    for tag in list(pending):
        sent(tag)

def widen_kernel(
    result, d_input, gq, go, gu, gd, small,
    output, input_grad, attn_gain, attn_shift, qkv, query, value, out, out_b, mlp_gain, mlp_shift, up, up_b, down, down_b,
):
    tok = output.shape[0]
    for i in range(2):
        output[:, i, :] = result[i, 0:tok, :]
        input_grad[:, i, :] = d_input[i, 0:tok, :]
    for at, ref in enumerate((attn_gain, attn_shift, query, value, out_b, mlp_gain, mlp_shift, down_b)):
        ref[...] = small[at]
    for b in range(NSEQ):
        up_b[128 * b:128 * b + 128] = small[8 + b]
        for c in range(3):
            qkv[:, 1024 * c + 256 * b:1024 * c + 256 * b + 256] = gq[(b % 2) * 2 + b // 2, :, 256 * c:256 * c + 256].astype(F32)
        for c in range(8):
            up[:, 512 * c + 128 * b:512 * c + 128 * b + 128] = gu[b, :, 128 * c:128 * c + 128].astype(F32)
        down[128 * b:128 * b + 128, :] = gd[b].astype(F32)
    out[...] = go[...].astype(F32)


def fused_device(
    inputs, key_mask, cotangent, attn_gain, attn_shift, qkv_weight, query_bias, value_bias,
    out_weight, out_bias, mlp_gain, mlp_shift, up_weight, up_bias, down_weight, down_bias,
):
    tok = inputs.shape[1]
    lines = [
        entry.reshape(1, 128)
        for entry in (attn_gain, attn_shift, query_bias, value_bias, out_bias, mlp_gain, mlp_shift, down_bias)
    ]
    vm = pl.BlockSpec(memory_space=pltpu.VMEM)
    hbm = pl.BlockSpec(memory_space=pl.ANY)

    def shape(dims, dtype=BF):
        return jax.ShapeDtypeStruct(dims, dtype)

    outs = pl.pallas_call(
        layer_kernel,
        out_shape=(
            shape((2, TOK, D)), shape((2, TOK, D)), shape((4, 128, 768)), shape((128, D)),
            shape((4, 128, D)), shape((4, 128, D)), shape((16, 128), F32),
        ),
        in_specs=[vm] * 12 + [hbm] * 4,
        out_specs=(vm, vm, hbm, hbm, hbm, hbm, vm),
        scratch_shapes=[
            pltpu.VMEM((2, TOK, D), BF),
            pltpu.VMEM((2, TOK, D), BF),
            pltpu.VMEM((16, 128), F32),
            pltpu.VMEM((ROWS, 8), F32),
            pltpu.VMEM((2, ROWS, D), BF),
            pltpu.VMEM((8, 128, 768), BF),
            pltpu.VMEM((2, 128, D), BF),
            pltpu.VMEM((8, 128, D), BF),
            pltpu.VMEM((8, 128, D), BF),
            pltpu.VMEM((8, 16, 128), F32),
            pltpu.VMEM((2, ROWS, 768), BF),
            pltpu.VMEM((2, ROWS, 768), BF),
            pltpu.VMEM((2, HEADS_DEV, ROWS, ROWS), BF),
            pltpu.VMEM((256, ROWS), BF),
            pltpu.VMEM((2, ROWS, 256), BF),
            pltpu.VMEM((2, ROWS, D), BF),
            pltpu.VMEM((2, 2, TOK, D), BF),
            pltpu.VMEM((2, TOK, D), BF),
            pltpu.VMEM((2, 2, TOK, D), BF),
            pltpu.VMEM((2, TOK, D), BF),
            pltpu.VMEM((2, TOK, D), F32),
            pltpu.VMEM((2, ROWS, D), BF),
            pltpu.VMEM((2, ROWS, D), BF),
            pltpu.VMEM((2, ROWS, D), BF),
            pltpu.VMEM((2, ROWS, D), BF),
            pltpu.VMEM((2, TOK, D), F32),
            pltpu.VMEM((2, ROWS, 256), BF),
            pltpu.VMEM((8, 128, 768), BF),
            pltpu.VMEM((2, 128, D), BF),
            pltpu.VMEM((8, 128, D), BF),
            pltpu.VMEM((8, 128, D), BF),
            pltpu.VMEM((4, 128, 768), BF),
            pltpu.VMEM((128, D), BF),
            pltpu.VMEM((4, 128, D), BF),
            pltpu.VMEM((4, 128, D), BF),
            pltpu.VMEM((3, 128, 768), BF),
            pltpu.VMEM((3, 128, D), BF),
            pltpu.VMEM((3, 128, D), BF),
            pltpu.VMEM((3, 128, D), BF),
            pltpu.VMEM((8, 16, 128), F32),
            pltpu.VMEM((7, 16, 128), F32),
            pltpu.VMEM((4, 16, 128), F32),
            pltpu.SemaphoreType.DMA((160,)),
            pltpu.SemaphoreType.DMA((160,)),
            pltpu.SemaphoreType.DMA((24,)),
        ],
        compiler_params=pltpu.CompilerParams(
            collective_id=0, has_side_effects=True, vmem_limit_bytes=VMEM_LIMIT
        ),
        cost_estimate=pl.CostEstimate(flops=26_000_000_000, bytes_accessed=30_000_000, transcendentals=8_000_000),
    )(inputs.transpose(1, 0, 2), cotangent.transpose(1, 0, 2), key_mask, *lines, up_bias.reshape(NSEQ, 128), qkv_weight, out_weight, up_weight, down_weight)
    out, d_input, gq, go, gu, gd, small = outs
    line = shape((128,), F32)
    grads = pl.pallas_call(
        widen_kernel,
        out_shape=(
            shape((tok, 2, D)), shape((tok, 2, D)), line, line, shape((128, 3 * D), F32), line, line, shape((128, D), F32), line, line, line,
            shape((128, 4 * D), F32), shape((512,), F32), shape((512, D), F32), line,
        ),
        in_specs=[vm] * 7,
        out_specs=(vm,) * 15,
        compiler_params=pltpu.CompilerParams(vmem_limit_bytes=WIDEN_LIMIT),
    )(out, d_input, gq, go, gu, gd, small)
    return (grads[0].transpose(1, 0, 2), grads[1].transpose(1, 0, 2)) + tuple(grads[2:])


def solution(mesh):
    in_specs = (
        P("shard", "seq", None),
        P("shard", None),
        P("shard", "seq", None),
        P("shard"),
        P("shard"),
        P("shard", None),
        P("shard"),
        P("shard"),
        P("shard", None),
        P("shard"),
        P("shard"),
        P("shard"),
        P("shard", None),
        P("shard"),
        P("shard", None),
        P("shard"),
    )
    out_specs = (
        P("shard", "seq", None),
        P("shard", "seq", None),
        P("shard"),
        P("shard"),
        P("shard", None),
        P("shard"),
        P("shard"),
        P("shard", None),
        P("shard"),
        P("shard"),
        P("shard"),
        P("shard", None),
        P("shard"),
        P("shard", None),
        P("shard"),
    )
    fits = dict(mesh.shape) == {"seq": NSEQ, "shard": NSH}
    return jax.shard_map(
        fused_device if fits else per_device, mesh=mesh, in_specs=in_specs, out_specs=out_specs, check_vma=False
    )
```

```python
import jax
import jax.numpy as jnp
from jax import lax
from jax.experimental import pallas as pl
from jax.experimental.pallas import tpu as pltpu
from jax.sharding import PartitionSpec as P

D = 1024
HEAD_DIM = 64


EPSILON = 1e-05


def product(left, right):
    return jnp.dot(left, right, preferred_element_type=jnp.float32)


def product_tn(left, right):
    return lax.dot_general(
        left, right, (((0,), (0,)), ((), ())), preferred_element_type=jnp.float32
    )


def product_nt(left, right):
    return lax.dot_general(
        left, right, (((1,), (1,)), ((), ())), preferred_element_type=jnp.float32
    )


def norm_rows(current, gain, shift):
    centre = jnp.mean(current, axis=-1, keepdims=True)
    centred = current - centre
    inverse = lax.rsqrt(jnp.mean(centred * centred, axis=-1, keepdims=True) + EPSILON)
    scaled = centred * inverse
    return (scaled * gain + shift, scaled, inverse)


def norm_back(incoming, scaled, inverse, gain):
    inner = incoming * gain
    d_current = inverse * (
        inner
        - jnp.mean(inner, axis=-1, keepdims=True)
        - scaled * jnp.mean(inner * scaled, axis=-1, keepdims=True)
    )
    return (d_current, jnp.sum(incoming * scaled, axis=0), jnp.sum(incoming, axis=0))


def split_heads(block):
    images, length, width = block.shape
    return block.reshape(images, length, width // HEAD_DIM, HEAD_DIM)


def masked_scores(query_h, keyed_h, key_mask):
    scores = jnp.einsum("iqhd,ikhd->ihqk", query_h, keyed_h, preferred_element_type=jnp.float32)
    scores = scores * HEAD_DIM ** (-0.5)
    return jnp.where(key_mask[:, None, None, :] > 0, scores, -1e30)


def layer_forward(current, key_mask, weights, images):
    (
        attn_gain,
        attn_shift,
        qkv_weight,
        query_bias,
        value_bias,
        out_weight,
        out_bias,
        mlp_gain,
        mlp_shift,
        up_weight,
        up_bias,
        down_weight,
        down_bias,
    ) = weights
    row_count = current.shape[0]
    tok_local = row_count // images
    normed, scaled_a, inverse_a = norm_rows(
        current, attn_gain.astype(jnp.float32), attn_shift.astype(jnp.float32)
    )
    normed_low = normed.astype(jnp.bfloat16)
    packed_bias = jnp.concatenate(
        [
            query_bias.astype(jnp.float32),
            jnp.zeros((D,), jnp.float32),
            value_bias.astype(jnp.float32),
        ]
    )
    packed = (product(normed_low, qkv_weight) + packed_bias).astype(jnp.bfloat16)
    packed = packed.reshape(images, tok_local, 3, D)
    head_view = lax.all_to_all(packed, "seq", split_axis=3, concat_axis=1, tiled=True)
    query_h = split_heads(head_view[:, :, 0])
    keyed_h = split_heads(head_view[:, :, 1])
    value_h = split_heads(head_view[:, :, 2])
    scores = masked_scores(query_h, keyed_h, key_mask)
    row_max = jnp.max(scores, axis=-1, keepdims=True)
    raised = jnp.exp(scores - row_max)
    row_sum = jnp.sum(raised, axis=-1, keepdims=True)
    attn_probs = raised / row_sum
    log_total = row_max + jnp.log(row_sum)
    mixed = jnp.einsum(
        "ihqk,ikhd->iqhd",
        attn_probs.astype(jnp.bfloat16),
        value_h,
        preferred_element_type=jnp.float32,
    )
    seq_len = head_view.shape[1]
    mixed = mixed.reshape(images, seq_len, head_view.shape[3]).astype(jnp.bfloat16)
    merged = lax.all_to_all(mixed, "seq", split_axis=1, concat_axis=2, tiled=True)
    merged_rows = merged.reshape(row_count, D)
    middle = current + product(merged_rows, out_weight) + out_bias.astype(jnp.float32)
    second, scaled_b, inverse_b = norm_rows(
        middle, mlp_gain.astype(jnp.float32), mlp_shift.astype(jnp.float32)
    )
    second_low = second.astype(jnp.bfloat16)
    hidden = product(second_low, up_weight) + up_bias.astype(jnp.float32)
    active = (hidden * jax.nn.sigmoid(1.702 * hidden)).astype(jnp.bfloat16)
    result = middle + product(active, down_weight) + down_bias.astype(jnp.float32)
    stored = (
        scaled_a,
        inverse_a,
        normed_low,
        head_view,
        log_total,
        merged_rows,
        scaled_b,
        inverse_b,
        second_low,
        hidden,
        active,
    )
    return (result, stored)


def layer_backward(upstream, key_mask, weights, stored, images):
    (
        attn_gain,
        attn_shift,
        qkv_weight,
        query_bias,
        value_bias,
        out_weight,
        out_bias,
        mlp_gain,
        mlp_shift,
        up_weight,
        up_bias,
        down_weight,
        down_bias,
    ) = weights
    (
        scaled_a,
        inverse_a,
        normed_low,
        head_view,
        log_total,
        merged_rows,
        scaled_b,
        inverse_b,
        second_low,
        hidden,
        active,
    ) = stored
    row_count = upstream.shape[0]
    tok_local = row_count // images
    branch_low = upstream.astype(jnp.bfloat16)
    grad_down_bias = jnp.sum(branch_low, axis=0, dtype=jnp.float32)
    grad_down_weight = product_tn(active, branch_low)
    d_active = product_nt(branch_low, down_weight)
    gate_sig = jax.nn.sigmoid(1.702 * hidden)
    d_hidden = (d_active * (gate_sig + 1.702 * hidden * gate_sig * (1.0 - gate_sig))).astype(
        jnp.bfloat16
    )
    grad_up_bias = jnp.sum(d_hidden, axis=0, dtype=jnp.float32)
    grad_up_weight = product_tn(second_low, d_hidden)
    d_second = product_nt(d_hidden, up_weight)
    d_norm_b, grad_mlp_gain, grad_mlp_shift = norm_back(
        d_second, scaled_b, inverse_b, mlp_gain.astype(jnp.float32)
    )
    d_middle = upstream + d_norm_b
    d_branch = d_middle.astype(jnp.bfloat16)
    grad_out_bias = jnp.sum(d_branch, axis=0, dtype=jnp.float32)
    grad_out_weight = product_tn(merged_rows, d_branch)
    d_merged = product_nt(d_branch, out_weight).astype(jnp.bfloat16).reshape(images, tok_local, D)
    d_heads = lax.all_to_all(d_merged, "seq", split_axis=2, concat_axis=1, tiled=True)
    query_h = split_heads(head_view[:, :, 0])
    keyed_h = split_heads(head_view[:, :, 1])
    value_h = split_heads(head_view[:, :, 2])
    d_out_h = split_heads(d_heads)
    scores = masked_scores(query_h, keyed_h, key_mask)
    attn_probs = jnp.exp(scores - log_total)
    d_value = jnp.einsum(
        "ihqk,iqhd->ikhd",
        attn_probs.astype(jnp.bfloat16),
        d_out_h,
        preferred_element_type=jnp.float32,
    )
    d_probs = jnp.einsum("iqhd,ikhd->ihqk", d_out_h, value_h, preferred_element_type=jnp.float32)
    d_scores = attn_probs * (d_probs - jnp.sum(attn_probs * d_probs, axis=-1, keepdims=True))
    d_scores = d_scores.astype(jnp.bfloat16)
    d_query = jnp.einsum(
        "ihqk,ikhd->iqhd", d_scores, keyed_h, preferred_element_type=jnp.float32
    ) * HEAD_DIM ** (-0.5)
    d_key = jnp.einsum(
        "ihqk,iqhd->ikhd", d_scores, query_h, preferred_element_type=jnp.float32
    ) * HEAD_DIM ** (-0.5)
    seq_len = head_view.shape[1]
    d_packed = jnp.stack((d_query, d_key, d_value), axis=2).astype(jnp.bfloat16)
    d_packed = d_packed.reshape(images, seq_len, 3, head_view.shape[3])
    d_tokens = lax.all_to_all(d_packed, "seq", split_axis=1, concat_axis=3, tiled=True).reshape(
        row_count, 3 * D
    )
    grad_query_bias = jnp.sum(d_tokens[:, :D], axis=0, dtype=jnp.float32)
    grad_value_bias = jnp.sum(d_tokens[:, 2 * D :], axis=0, dtype=jnp.float32)
    grad_qkv_weight = product_tn(normed_low, d_tokens)
    d_normed = product_nt(d_tokens, qkv_weight)
    d_norm_a, grad_attn_gain, grad_attn_shift = norm_back(
        d_normed, scaled_a, inverse_a, attn_gain.astype(jnp.float32)
    )
    grads = (
        grad_attn_gain,
        grad_attn_shift,
        grad_qkv_weight,
        grad_query_bias,
        grad_value_bias,
        grad_out_weight,
        grad_out_bias,
        grad_mlp_gain,
        grad_mlp_shift,
        grad_up_weight,
        grad_up_bias,
        grad_down_weight,
        grad_down_bias,
    )
    return (d_middle + d_norm_a, grads)


def reduce_grads(grads):
    shares = (
        lax.psum_scatter(
            grads[0].astype(jnp.bfloat16), "shard", scatter_dimension=0, tiled=True
        ).astype(jnp.float32),
        lax.psum_scatter(
            grads[1].astype(jnp.bfloat16), "shard", scatter_dimension=0, tiled=True
        ).astype(jnp.float32),
        lax.psum_scatter(
            grads[2].astype(jnp.bfloat16), "shard", scatter_dimension=0, tiled=True
        ).astype(jnp.float32),
        lax.psum_scatter(
            grads[3].astype(jnp.bfloat16), "shard", scatter_dimension=0, tiled=True
        ).astype(jnp.float32),
        lax.psum_scatter(
            grads[4].astype(jnp.bfloat16), "shard", scatter_dimension=0, tiled=True
        ).astype(jnp.float32),
        lax.psum_scatter(
            grads[5].astype(jnp.bfloat16), "shard", scatter_dimension=0, tiled=True
        ).astype(jnp.float32),
        lax.psum_scatter(
            grads[6].astype(jnp.bfloat16), "shard", scatter_dimension=0, tiled=True
        ).astype(jnp.float32),
        lax.psum_scatter(
            grads[7].astype(jnp.bfloat16), "shard", scatter_dimension=0, tiled=True
        ).astype(jnp.float32),
        lax.psum_scatter(
            grads[8].astype(jnp.bfloat16), "shard", scatter_dimension=0, tiled=True
        ).astype(jnp.float32),
        lax.psum_scatter(
            grads[9].astype(jnp.bfloat16), "shard", scatter_dimension=0, tiled=True
        ).astype(jnp.float32),
        lax.psum_scatter(
            grads[10].astype(jnp.bfloat16), "shard", scatter_dimension=0, tiled=True
        ).astype(jnp.float32),
        lax.psum_scatter(
            grads[11].astype(jnp.bfloat16), "shard", scatter_dimension=0, tiled=True
        ).astype(jnp.float32),
        lax.psum_scatter(
            grads[12].astype(jnp.bfloat16), "shard", scatter_dimension=0, tiled=True
        ).astype(jnp.float32),
    )
    return (
        lax.psum(shares[0].astype(jnp.bfloat16), "seq").astype(jnp.float32),
        lax.psum(shares[1].astype(jnp.bfloat16), "seq").astype(jnp.float32),
        lax.psum(shares[2].astype(jnp.bfloat16), "seq").astype(jnp.float32),
        lax.psum(shares[3].astype(jnp.bfloat16), "seq").astype(jnp.float32),
        lax.psum(shares[4].astype(jnp.bfloat16), "seq").astype(jnp.float32),
        lax.psum(shares[5].astype(jnp.bfloat16), "seq").astype(jnp.float32),
        lax.psum(shares[6].astype(jnp.bfloat16), "seq").astype(jnp.float32),
        lax.psum(shares[7].astype(jnp.bfloat16), "seq").astype(jnp.float32),
        lax.psum(shares[8].astype(jnp.bfloat16), "seq").astype(jnp.float32),
        lax.psum(shares[9].astype(jnp.bfloat16), "seq").astype(jnp.float32),
        lax.psum(shares[10].astype(jnp.bfloat16), "seq").astype(jnp.float32),
        lax.psum(shares[11].astype(jnp.bfloat16), "seq").astype(jnp.float32),
        lax.psum(shares[12].astype(jnp.bfloat16), "seq").astype(jnp.float32),
    )


def per_device(
    inputs,
    key_mask,
    cotangent,
    attn_gain,
    attn_shift,
    qkv_weight,
    query_bias,
    value_bias,
    out_weight,
    out_bias,
    mlp_gain,
    mlp_shift,
    up_weight,
    up_bias,
    down_weight,
    down_bias,
):
    shard_set = (
        attn_gain,
        attn_shift,
        qkv_weight,
        query_bias,
        value_bias,
        out_weight,
        out_bias,
        mlp_gain,
        mlp_shift,
        up_weight,
        up_bias,
        down_weight,
        down_bias,
    )
    images = inputs.shape[0]
    tok_local = inputs.shape[1]
    row_count = images * tok_local
    current = inputs.astype(jnp.float32).reshape(row_count, D)
    gathered = (
        lax.all_gather(shard_set[0], "shard", axis=0, tiled=True),
        lax.all_gather(shard_set[1], "shard", axis=0, tiled=True),
        lax.all_gather(shard_set[2], "shard", axis=0, tiled=True),
        lax.all_gather(shard_set[3], "shard", axis=0, tiled=True),
        lax.all_gather(shard_set[4], "shard", axis=0, tiled=True),
        lax.all_gather(shard_set[5], "shard", axis=0, tiled=True),
        lax.all_gather(shard_set[6], "shard", axis=0, tiled=True),
        lax.all_gather(shard_set[7], "shard", axis=0, tiled=True),
        lax.all_gather(shard_set[8], "shard", axis=0, tiled=True),
        lax.all_gather(shard_set[9], "shard", axis=0, tiled=True),
        lax.all_gather(shard_set[10], "shard", axis=0, tiled=True),
        lax.all_gather(shard_set[11], "shard", axis=0, tiled=True),
        lax.all_gather(shard_set[12], "shard", axis=0, tiled=True),
    )
    result, stored = layer_forward(current, key_mask, gathered, images)
    output = result.astype(jnp.bfloat16).reshape(images, tok_local, D)
    start_row = lax.axis_index("seq") * tok_local
    own_mask = lax.dynamic_slice_in_dim(key_mask, start_row, tok_local, 1).astype(jnp.float32)
    upstream = (cotangent.astype(jnp.float32) * own_mask[:, :, None]).reshape(row_count, D)
    again = (
        lax.all_gather(shard_set[0], "shard", axis=0, tiled=True),
        lax.all_gather(shard_set[1], "shard", axis=0, tiled=True),
        lax.all_gather(shard_set[2], "shard", axis=0, tiled=True),
        lax.all_gather(shard_set[3], "shard", axis=0, tiled=True),
        lax.all_gather(shard_set[4], "shard", axis=0, tiled=True),
        lax.all_gather(shard_set[5], "shard", axis=0, tiled=True),
        lax.all_gather(shard_set[6], "shard", axis=0, tiled=True),
        lax.all_gather(shard_set[7], "shard", axis=0, tiled=True),
        lax.all_gather(shard_set[8], "shard", axis=0, tiled=True),
        lax.all_gather(shard_set[9], "shard", axis=0, tiled=True),
        lax.all_gather(shard_set[10], "shard", axis=0, tiled=True),
        lax.all_gather(shard_set[11], "shard", axis=0, tiled=True),
        lax.all_gather(shard_set[12], "shard", axis=0, tiled=True),
    )
    d_input, grads = layer_backward(upstream, key_mask, again, stored, images)
    reduced = reduce_grads(grads)
    input_grad = d_input.astype(jnp.bfloat16).reshape(images, tok_local, D)
    return (
        output,
        input_grad,
        reduced[0],
        reduced[1],
        reduced[2],
        reduced[3],
        reduced[4],
        reduced[5],
        reduced[6],
        reduced[7],
        reduced[8],
        reduced[9],
        reduced[10],
        reduced[11],
        reduced[12],
    )


STEPS = (1, 3, 2)
PUMPS = (1, 1, 1, 0, 0, 0, 0, 1, 1, 1, 1, 1, 1, 0, 1)
LIMITS = (2, 3, 3, 4, 6, 7, 8, 9, 10, 10, 10)
MT = 640
FLIGHT = 3
NSEQ = 4
NSH = 8
TOK = 160
ROWS = NSEQ * TOK
HEADS_DEV = 4
MASKED = -1e30
VMEM_LIMIT = 64 * 1024 * 1024 - 1024 * 1024
WIDEN_LIMIT = 64 * 1024 * 1024 - 1024 * 1024
MESH_ID = pl.DeviceIdType.MESH
BF = jnp.bfloat16
F32 = jnp.float32
GATE = 1.702


def dot_nn(left, right):
    return lax.dot_general(left, right, (((1,), (0,)), ((), ())), preferred_element_type=F32)


def dot_nt(left, right):
    return lax.dot_general(left, right, (((1,), (1,)), ((), ())), preferred_element_type=F32)


def dot_tn(left, right):
    return lax.dot_general(left, right, (((0,), (0,)), ((), ())), preferred_element_type=F32)


def layer_kernel(
    inp, cot, kmask, b0, b1, b2, b3, b4, b5, b6, b7, b8, wq_h, wo_h, wu_h, wd_h,
    out_o, dx_o, gq_o, go_o, gu_o, gd_o, sg_o,
    xin, dmin, pack, bias_t, xg, wq, wo, wu, wd, pg, qkv, dqkv, probs, mixt, mixed, part, rc, rx, rc2, rx2,
    hid, cg, act, gate, dmg, dhid, dmix,
    gq, go, gu, gd, ryq, ryo, ryu, ryd, rzq, rzo, rzu, rzd, sgs, sg1, sg2,
    ssem, rsem, lsem,
):
    s = lax.axis_index("seq")
    j = lax.axis_index("shard")
    x, k = s // 2, s % 2
    z, y = j // 2, j % 2
    zs = k * 2 + x
    s_core = x * 2 + (1 - k)
    s_x = (1 - x) * 2 + k
    s_diag = (1 - x) * 2 + (1 - k)
    j_y = z * 2 + (1 - y)
    core = (s_core, j)
    xdev = (s_x, j)
    ydev = (s, j_y)

    def zj(d):
        return lax.rem(z + d, 4) * 2 + y

    ids = {}

    def ix(*key):
        return ids.setdefault(key, len(ids))

    pending = {}
    parts = part

    def send(tag, key, src, dst, dev):
        n = ix(*key)
        copy = pltpu.make_async_remote_copy(
            src_ref=src, dst_ref=dst, send_sem=ssem.at[n], recv_sem=rsem.at[n],
            device_id=dev, device_id_type=MESH_ID)
        copy.start()
        pending.setdefault(tag, []).append(copy)

    def sent(tag):
        for copy in pending.pop(tag, []):
            copy.wait_send()

    def arrived(key, dst, dev):
        n = ix(*key)
        pltpu.make_async_remote_copy(
            src_ref=dst, dst_ref=dst, send_sem=ssem.at[n], recv_sem=rsem.at[n],
            device_id=dev, device_id_type=MESH_ID).wait_recv()

    local = {}

    def load(key, src, dst):
        copy = pltpu.make_async_copy(src, dst, lsem.at[local.setdefault(key, len(local))])
        copy.start()
        return copy

    def rows(block):
        return pl.ds(pl.multiple_of(block * TOK, TOK), TOK)

    def tiles(count, step, body, init=None, unroll=False):
        def inner(t, carry):
            return body(pl.multiple_of(t * step, step), carry)
        return lax.fori_loop(0, count // step, inner, init, unroll=unroll)

    barrier = pltpu.get_barrier_semaphore()
    for d in range(1, NSEQ):
        pl.semaphore_signal(barrier, inc=1, device_id=(lax.rem(s + d, NSEQ), j), device_id_type=MESH_ID)
    for d in range(1, NSH):
        pl.semaphore_signal(barrier, inc=1, device_id=(s, lax.rem(j + d, NSH)), device_id_type=MESH_ID)
    loads_q = [load(("wq", c), wq_h.at[:, pl.ds(pl.multiple_of(1024 * c + 256 * zs, 256), 256)],
                    wq.at[j, :, pl.ds(256 * c, 256)]) for c in range(3)]
    loads_u = [load(("wu", c), wu_h.at[:, pl.ds(pl.multiple_of(512 * c + 128 * s, 128), 128)],
                    wu.at[j, :, pl.ds(128 * c, 128)]) for c in range(8)]
    load_d = load(("wd",), wd_h.at[pl.ds(pl.multiple_of(128 * s, 128), 128)], wd.at[j])
    for row, ref in enumerate((b0, b1, b2, b3, b4, b5, b6, b7)):
        pack[row:row + 1, :] = ref[...].astype(F32)
    own_row = lax.broadcasted_iota(jnp.int32, (NSEQ, 128), 0) == s
    pack[8:9, :] = jnp.sum(jnp.where(own_row, b8[...].astype(F32), 0.0), axis=0, keepdims=True)
    pack[9:16, :] = jnp.zeros((7, 128), F32)
    pg[j] = pack[...]

    tok = inp.shape[0]

    def slots_of(source, i):
        row = lax.broadcasted_iota(jnp.int32, (TOK, 2 * tok), 0)
        col = lax.broadcasted_iota(jnp.int32, (TOK, 2 * tok), 1)
        chosen = (col == 2 * row + i).astype(F32).astype(BF)
        return dot_nn(chosen, source[...].reshape(2 * tok, D))
    for i in range(2):
        xin[i] = slots_of(inp, i).astype(BF)
    n_wo = local.setdefault("wo", len(local))

    @pl.when(z == zs)
    def _():
        pltpu.make_async_copy(wo_h, wo.at[y], lsem.at[n_wo]).start()
    pl.semaphore_wait(barrier, NSEQ - 1 + NSH - 1)

    def ag4_start(key, buf, i, src):
        send(key, (key, "c", i), src, buf.at[i, rows(s)], core)
        send(key, (key, "x", i), src, buf.at[i, rows(s)], xdev)

    def ag4_forward(key, buf, i):
        arrived((key, "x", i), buf.at[i, rows(s_x)], xdev)
        send(key + "f", (key, "d", i), buf.at[i, rows(s_x)], buf.at[i, rows(s_x)], core)

    def ag4_end(key, buf, i):
        arrived((key, "c", i), buf.at[i, rows(s_core)], core)
        arrived((key, "d", i), buf.at[i, rows(s_diag)], core)

    weights = {"wq": wq, "wu": wu, "wd": wd}
    n_oz, n_oy = [ix("wo", d) for d in (1, 2, 3)], ix("wo", "y")

    def out_copy(d):
        return pltpu.make_async_remote_copy(
            src_ref=wo.at[y], dst_ref=wo.at[y], send_sem=ssem.at[n_oz[d - 1]], recv_sem=rsem.at[n_oz[0]],
            device_id=(s, zj(d)), device_id_type=MESH_ID)

    def out_start():
        @pl.when(z == zs)
        def _():
            pltpu.make_async_copy(wo_h, wo.at[y], lsem.at[n_wo]).wait()
            for d in (2, 1, 3):
                out_copy(d).start()

    def out_forward():
        @pl.when(z != zs)
        def _():
            pltpu.make_async_remote_copy(
                src_ref=wo.at[y], dst_ref=wo.at[y], send_sem=ssem.at[n_oz[0]], recv_sem=rsem.at[n_oz[0]],
                device_id=(s, zs * 2 + y), device_id_type=MESH_ID).wait_recv()
        send("wo", ("wo", "y"), wo.at[y], wo.at[y], ydev)

    def block_rows(d):
        return (2, pl.ds(64 * (d - 20), 64)) if d >= 20 else (d, pl.ds(0, 128))

    def gather_start(key, d):
        if key == "wo":
            out_start()
            return
        buf = weights[key]
        if d == 1:
            send(key, (key, "y", 0), buf.at[j], buf.at[j], ydev)
        step, part_rows = block_rows(d)
        mine = buf.at[j, part_rows]
        send(key, (key, "z", d), mine, mine, (s, zj(step)))

    def gather_forward(key, d):
        if key == "wo":
            out_forward()
            return
        buf = weights[key]
        step, part_rows = block_rows(d)
        jf = zj(4 - step)
        block = buf.at[jf, part_rows]
        arrived((key, "z", d), block, (s, jf))
        send(key, (key, "y", d), block, block, ydev)

    issue_order = [("wq", d) for d in STEPS] + [("wo", 0)]
    issue_order += [(key, d) for key in ("wu", "wd") for d in STEPS]
    rounds = list(issue_order)
    at_round, issued = [0], [0]

    def gather_issue(upto):
        while issued[0] < min(upto, len(rounds)):
            gather_start(*issue_order[issued[0]])
            issued[0] += 1

    def pump(place):
        for _step in range(PUMPS[place]):
            n = at_round[0]
            gather_forward(*rounds[n])
            at_round[0] = n + 1
            gather_issue(LIMITS[n + 1])

    def agw_end(key, buf):
        for d in (0,) + STEPS:
            step, part_rows = block_rows(d)
            jf = lax.rem(z + 4 - step, 4) * 2 + (1 - y)
            arrived((key, "y", d), buf.at[jf, part_rows], ydev)

    def rs4_a(key, i, rcb):
        part = act if key == "da" else parts
        send(key, (key, "c0", i), part.at[i, rows(s_core)], rcb.at[i, 0], core)
        send(key, (key, "c1", i), part.at[i, rows(s_diag)], rcb.at[i, 1], core)

    def rs4_b(key, i, rcb, rxb):
        arrived((key, "c1", i), rcb.at[i, 1], core)
        part = act if key == "da" else parts

        def add(r, _):
            here = pl.ds(pl.multiple_of(s_x * TOK + r, 32), 32)
            total = part[i, here, :].astype(F32) + rcb[i, 1, pl.ds(r, 32), :].astype(F32)
            part[i, here, :] = total.astype(BF)
        tiles(TOK, 32, add, unroll=True)
        send(key, (key, "x", i), part.at[i, rows(s_x)], rxb.at[i], xdev)

    def rs4_wait(key, i, rcb, rxb):
        arrived((key, "c0", i), rcb.at[i, 0], core)
        arrived((key, "x", i), rxb.at[i], xdev)

    def rs4_sum(i, r, rcb, rxb, part=None):
        part = parts if part is None else part
        here = pl.ds(pl.multiple_of(s * TOK + r, 32), 32)
        return (part[i, here, :].astype(F32) + rcb[i, 0, pl.ds(r, 32), :].astype(F32)
                + rxb[i, pl.ds(r, 32), :].astype(F32))

    def add_into(g, row, others):
        def add(r, _):
            total = g[row, pl.ds(r, 32), :].astype(F32)
            for ref, at in others:
                total = total + ref[at, pl.ds(r, 32), :].astype(F32)
            g[row, pl.ds(r, 32), :] = total.astype(BF)
        tiles(128, 32, add, unroll=True)

    waiting, flying = [], []

    def reduce_fill():
        while waiting and len(flying) < FLIGHT:
            piece = waiting.pop(0)
            key, d, g, ry, rz = piece
            if key == "o":
                send("go", ("go", "y"), g.at[1 - y], ry, ydev)
            else:
                send(key, (key, "gy", d), g.at[lax.rem(z + d, 4) * 2 + (1 - y)], ry.at[d], ydev)
            flying.append(piece)

    def reduce_add(key, g, ry, rz):
        for d in ((0,) if key == "o" else (2, 1, 3, 0)):
            waiting.append((key, d, g, ry, rz))
        reduce_fill()

    def reduce_step(count=1):
        for _step in range(count):
            key, d, g, ry, rz = flying.pop(0)
            if key == "o":
                arrived(("go", "y"), ry, ydev)
                reduce_fill()
                add_out_block()
                continue
            arrived((key, "gy", d), ry.at[d], ydev)
            reduce_fill()
            add_into(g, zj(d), [(ry, d)])
            if d:
                send(key, (key, "gz", d), g.at[zj(d)], rz.at[d - 1], (s, zj(d)))

    n_gz = [ix("goz", d) for d in range(3)]
    n_gs = ix("gozs")

    def out_grad_copy(slot):
        return pltpu.make_async_remote_copy(
            src_ref=go.at[y], dst_ref=rzo.at[slot], send_sem=ssem.at[n_gs], recv_sem=rsem.at[n_gz[0] + slot],
            device_id=(s, zs * 2 + y), device_id_type=MESH_ID)

    def add_out_block():
        def add_out(r, _):
            total = go[y, pl.ds(r, 32), :].astype(F32) + ryo[pl.ds(r, 32), :].astype(F32)
            go[y, pl.ds(r, 32), :] = total.astype(BF)
        tiles(128, 32, add_out, unroll=True)

        @pl.when(z != zs)
        def _():
            out_grad_copy(lax.rem(z + 3 - zs, 4)).start()

    def rsw_end(key, g, rz, g_o):
        for d in (2, 1, 3):
            arrived((key, "gz", d), rz.at[d - 1], (s, zj(4 - d)))
        add_into(g, j, [(rz, 0), (rz, 1), (rz, 2)])
        copy = load((key, "go"), g.at[j], g_o.at[s])
        send(key, (key, "gc"), g.at[j], g_o.at[s], core)
        send(key, (key, "gx"), g.at[j], g_o.at[s], xdev)
        return copy

    def rsw_forward(key, g_o):
        arrived((key, "gx"), g_o.at[s_x], xdev)
        send(key, (key, "gd"), g_o.at[s_x], g_o.at[s_x], core)

    def rsw_done(key, g_o):
        arrived((key, "gc"), g_o.at[s_core], core)
        arrived((key, "gd"), g_o.at[s_diag], core)

    def param(p):
        return jnp.concatenate([pg[b, pl.ds(p, 1), :] for b in range(NSH)], axis=1)

    def head_param(p):
        return jnp.concatenate([pg[2 * zs, pl.ds(p, 1), :], pg[2 * zs + 1, pl.ds(p, 1), :]], axis=1)

    def normal(value):
        centre = jnp.mean(value, axis=-1, keepdims=True)
        centred = value - centre
        inverse = lax.rsqrt(jnp.mean(centred * centred, axis=-1, keepdims=True) + EPSILON)
        return centred * inverse, inverse

    def normal_back(incoming, scaled, inverse, gain):
        inner = incoming * gain
        return inverse * (inner - jnp.mean(inner, axis=-1, keepdims=True)
                          - scaled * jnp.mean(inner * scaled, axis=-1, keepdims=True))

    def fold(value):
        return value[0:8] + value[8:16] + value[16:24] + value[24:32]

    for d in range(1, NSH):
        send("pk", ("pk", d), pack, pg.at[j], (s, lax.rem(j + d, NSH)))
    for i in range(2):
        ag4_start("xg", xg, i, xin.at[i])
    for copy in loads_q:
        copy.wait()
    gather_issue(LIMITS[0])
    slot = lax.broadcasted_iota(jnp.int32, (ROWS, 1), 0)
    shift = sum(jnp.where(slot >= TOK * b, TOK - tok, 0) for b in range(1, NSEQ))
    used = slot - sum(jnp.where(slot >= TOK * b, TOK, 0) for b in range(1, NSEQ)) < tok
    place_of = jnp.where(used, slot - shift, -1)
    chosen = lax.broadcasted_iota(jnp.int32, (ROWS, kmask.shape[1]), 1) == place_of
    live = dot_nt(chosen.astype(F32).astype(BF), kmask[...].astype(F32).astype(BF))
    bias_t[:, 0:2] = jnp.where(live > 0.5, 0.0, MASKED)
    for i in range(2):
        mask = bias_t[pl.ds(pl.multiple_of(s * TOK, TOK), TOK), i:i + 1]
        dmin[i] = jnp.where(mask == 0.0, slots_of(cot, i), 0.0).astype(BF)
        xg[i, rows(s), :] = xin[i]
        dmg[i, rows(s), :] = dmin[i]
    for copy in loads_u:
        copy.wait()
    load_d.wait()
    pump(0)
    ag4_forward("xg", xg, 0)

    for d in range(1, NSH):
        jf = lax.rem(j + NSH - d, NSH)
        arrived(("pk", d), pg.at[jf], (s, jf))
    attn_gain, attn_shift = param(0), param(1)

    def norm_block(i, block):
        def body(r, _):
            here = pl.ds(pl.multiple_of(block * TOK + r, 32), 32)
            scaled, _inverse = normal(xg[i, here, :].astype(F32))
            xg[i, here, :] = (scaled * attn_gain + attn_shift).astype(BF)
        tiles(TOK, 32, body, unroll=True)

    norm_block(0, s)
    norm_block(1, s)
    pump(1)
    for i in range(2):
        arrived(("xg", "c", i), xg.at[i, rows(s_core)], core)
        norm_block(i, s_core)
    ag4_forward("xg", xg, 1)
    for i in range(2):
        ag4_start("dm", dmg, i, dmin.at[i])
    arrived(("xg", "d", 0), xg.at[0, rows(s_diag)], core)
    norm_block(0, s_diag)
    sent("xgf")
    pump(2)
    norm_block(0, s_x)
    norm_block(1, s_x)
    arrived(("xg", "d", 1), xg.at[1, rows(s_diag)], core)
    norm_block(1, s_diag)
    pump(3)
    agw_end("wq", wq)

    packed_bias = jnp.concatenate([head_param(2), jnp.zeros((1, 256), F32), head_param(3)], axis=1)

    def project_in(i):
        def project(r, _):
            here = pl.ds(r, MT)
            value = dot_nn(xg[i, here, :], wq[...].reshape(D, 768)) + packed_bias
            qkv[i, here, :] = value.astype(BF)
        tiles(ROWS, MT, project)

    def attend(i, first, last):
        if first == 0:
            mixt[...] = qkv[i, :, 512:768].astype(F32).T.astype(BF)
        lane = lax.broadcasted_iota(jnp.int32, (1, 256), 1) // HEAD_DIM

        def one_head(h, _):
            keyed = jnp.where(lane == h, qkv[i, :, 256:512], jnp.zeros((), BF))
            query = qkv[i, :, 0:256] * jnp.asarray(HEAD_DIM ** -0.5, BF)
            scores = dot_nt(keyed, query) + bias_t[:, i:i + 1]
            raised = jnp.exp(scores - jnp.max(scores, axis=0, keepdims=True))
            chances = (raised * (1.0 / jnp.sum(raised, axis=0, keepdims=True))).astype(BF)
            probs[i, h] = chances
            here = pl.ds(pl.multiple_of(h * HEAD_DIM, HEAD_DIM), HEAD_DIM)
            mixt[here, :] = dot_nn(mixt[here, :], chances).astype(BF)
        lax.fori_loop(first, last, one_head, None)
        if last == HEADS_DEV:
            mixed[i] = mixt[...].astype(F32).T.astype(BF)

    def project_out(i):
        def body(r, _):
            here = pl.ds(r, MT)
            part[i, here, :] = dot_nn(mixed[i, here, :], wo[...].reshape(256, D)).astype(BF)
        tiles(ROWS, MT, body)

    project_in(0)
    attend(0, 0, 2)
    pump(14)
    attend(0, 2, 4)
    pump(4)
    project_in(1)
    arrived(("wo", "y"), wo.at[1 - y], ydev)
    project_out(0)
    rs4_a("o", 0, rc)
    pump(5)
    attend(1, 0, 2)
    pump(6)
    attend(1, 2, 4)
    rs4_b("o", 0, rc, rx)
    project_out(1)
    rs4_a("o", 1, rc)
    pump(7)
    rs4_b("o", 1, rc, rx)
    for i in range(2):
        ag4_forward("dm", dmg, i)
    pump(8)

    out_bias, mlp_gain, mlp_shift, down_bias = param(4), param(5), param(6), param(7)
    up_bias = param(8)

    for i in range(2):
        rs4_wait("o", i, rc, rx)

        def middle(r, _, i=i):
            value = xin[i, pl.ds(r, 32), :].astype(F32) + (rs4_sum(i, r, rc, rx) + out_bias)
            hid[i, pl.ds(r, 32), :] = value
            scaled, _inverse = normal(value)
            here = pl.ds(pl.multiple_of(s * TOK + r, 32), 32)
            cg[i, here, :] = (scaled * mlp_gain + mlp_shift).astype(BF)
        tiles(TOK, 32, middle, unroll=True)
        ag4_start("c", cg, i, cg.at[i, rows(s)])
        pump(9 + i)
    for n in range(2):
        ag4_end("dm", dmg, n)
    agw_end("wu", wu)
    for i in range(2):
        ag4_forward("c", cg, i)
        ag4_end("c", cg, i)

        def up(r, _, i=i):
            here = pl.ds(r, MT)
            value = dot_nn(cg[i, here, :], wu[...].reshape(D, D)) + up_bias
            sig = jax.nn.sigmoid(GATE * value)
            act[i, here, :] = (value * sig).astype(BF)
            gate[i, here, :] = (sig + GATE * value * sig * (1.0 - sig)).astype(BF)
        tiles(ROWS, MT, up)
        pump(11 + i)
    sent("o")

    def weight_grad(left, right, g):
        def body(t, _):
            cols = pl.ds(pl.multiple_of(t * 512, 512), 512)
            value = dot_tn(left[:, :, cols].reshape(2 * ROWS, 512), right[...].reshape(2 * ROWS, right.shape[2]))
            g[pl.ds(4 * t, 4)] = value.astype(BF).reshape(4, 128, right.shape[2])
        lax.fori_loop(0, left.shape[2] // 512, body, None)

    weight_grad(act, dmg, gd)
    pump(13)
    reduce_add("d", gd, ryd, rzd)
    agw_end("wd", wd)

    def d_up(i, total):
        def body(r, carry):
            here = pl.ds(r, MT)
            value = dot_nt(dmg[i, here, :], wd[...].reshape(D, D)) * gate[i, here, :].astype(F32)
            value = value.astype(BF)
            gate[i, here, :] = value
            return carry + jnp.sum(value.astype(F32).reshape(MT // 8, 8, D), axis=0)
        return tiles(ROWS, MT, body, total)

    def d_second(i):
        def body(r, _):
            here = pl.ds(r, MT)
            part[i, here, :] = dot_nt(gate[i, here, :], wu[...].reshape(D, D)).astype(BF)
        tiles(ROWS, MT, body)

    sent("dmf")
    sent("dm")
    du_sum = d_up(0, jnp.zeros((8, D), F32))
    d_second(0)
    rs4_a("dc", 0, rc)
    du_sum = d_up(1, du_sum)
    rs4_b("dc", 0, rc, rx)
    d_second(1)
    rs4_a("dc", 1, rc)
    reduce_step()
    rs4_b("dc", 1, rc, rx)
    weight_grad(cg, gate, gu)
    reduce_add("u", gu, ryu, rzu)
    reduce_step()

    zero8 = jnp.zeros((8, D), F32)
    sums = (zero8, zero8, zero8, zero8)
    for i in range(2):
        rs4_wait("dc", i, rc, rx)

        def d_middle(r, carry, i=i):
            mine = pl.ds(r, 32)
            incoming = rs4_sum(i, r, rc, rx)
            scaled, inverse = normal(hid[i, mine, :])
            upstream = dmin[i, mine, :].astype(F32)
            value = upstream + normal_back(incoming, scaled, inverse, mlp_gain)
            dhid[i, mine, :] = value
            low = value.astype(BF)
            dmg[i, pl.ds(pl.multiple_of(s * TOK + r, 32), 32), :] = low
            return (carry[0] + fold(incoming * scaled), carry[1] + fold(incoming),
                    carry[2] + fold(low.astype(F32)), carry[3] + fold(upstream))
        sums = tiles(TOK, 32, d_middle, sums, unroll=True)
        ag4_start("db", dmg, i, dmg.at[i, rows(s)])
        reduce_step()
    sent("dc")

    for i in range(2):
        def down(r, _, i=i):
            here = pl.ds(r, MT)
            part[i, here, :] = dot_nn(act[i, here, :], wd[...].reshape(D, D)).astype(BF)
        tiles(ROWS, MT, down)

    def attend_back(i):
        def d_mixed(r, _):
            here = pl.ds(r, MT)
            dmix[i, here, :] = dot_nt(dmg[i, here, :], wo[...].reshape(256, D)).astype(BF)
        tiles(ROWS, MT, d_mixed)
        lane = lax.broadcasted_iota(jnp.int32, (1, 256), 1) // HEAD_DIM
        mixt[...] = qkv[i, :, 256:512].astype(F32).T.astype(BF)

        def one_head(h, _):
            own = lane == h
            chances = probs[i, h]
            d_value = dot_nn(chances, dmix[i])
            dqkv[i, :, 512:768] = jnp.where(own, d_value.astype(BF), dqkv[i, :, 512:768])
            valued = jnp.where(own, qkv[i, :, 512:768], jnp.zeros((), BF))
            d_chances = dot_nt(valued, dmix[i])
            wide = chances.astype(F32)
            d_scores = wide * (d_chances - jnp.sum(wide * d_chances, axis=0, keepdims=True))
            d_scores = d_scores.astype(BF)
            d_key = dot_nn(d_scores, qkv[i, :, 0:256]) * HEAD_DIM ** -0.5
            dqkv[i, :, 256:512] = jnp.where(own, d_key.astype(BF), dqkv[i, :, 256:512])
            here = pl.ds(pl.multiple_of(h * HEAD_DIM, HEAD_DIM), HEAD_DIM)
            mixt[here, :] = (dot_nn(mixt[here, :], d_scores) * HEAD_DIM ** -0.5).astype(BF)
        lax.fori_loop(0, HEADS_DEV, one_head, None)
        dqkv[i, :, 0:256] = mixt[...].astype(F32).T.astype(BF)

    def out_presum(i):
        arrived(("y", "c0", i), rc2.at[i, 0], core)
        arrived(("y", "c1", i), rc2.at[i, 1], core)

        def body(r, _):
            mine = pl.ds(r, 32)
            here = pl.ds(pl.multiple_of(s * TOK + r, 32), 32)
            there = pl.ds(pl.multiple_of(s_x * TOK + r, 32), 32)
            total = part[i, here, :].astype(F32) + rc2[i, 0, mine, :].astype(F32)
            hid[i, mine, :] = hid[i, mine, :] + (total + down_bias)
            total = part[i, there, :].astype(F32) + rc2[i, 1, mine, :].astype(F32)
            rc2[i, 1, mine, :] = total.astype(BF)
        tiles(TOK, 32, body, unroll=True)

    def d_normed(i):
        def body(r, _):
            here = pl.ds(r, MT)
            act[i, here, :] = dot_nt(dqkv[i, here, :], wq[...].reshape(D, 768)).astype(BF)
        tiles(ROWS, MT, body)
        rs4_a("da", i, rc)

    ag4_forward("db", dmg, 0)
    ag4_end("db", dmg, 0)
    for i in range(2):
        rs4_a("y", i, rc2)
    attend_back(0)
    reduce_step()
    ag4_forward("db", dmg, 1)
    d_normed(0)
    ag4_end("db", dmg, 1)
    copy_d = rsw_end("d", gd, rzd, gd_o)
    rs4_b("da", 0, rc, rx)
    attend_back(1)
    reduce_step()
    d_normed(1)
    weight_grad(xg, dqkv, gq)
    rs4_b("da", 1, rc, rx)
    value = dot_tn(mixed[...].reshape(2 * ROWS, 256), dmg[...].reshape(2 * ROWS, D))
    go[...] = value.astype(BF).reshape(2, 128, D)
    reduce_add("o", go, ryo, rzo)
    reduce_add("q", gq, ryq, rzq)
    reduce_step()
    for i in range(2):
        out_presum(i)
        send("y", ("y", "x", i), rc2.at[i, 1], rx2.at[i], xdev)
    reduce_step()

    n_gb = [ix("gob", d) for d in range(3)]

    def out_final_copy(d):
        return pltpu.make_async_remote_copy(
            src_ref=go.at[y], dst_ref=go_o, send_sem=ssem.at[n_gb[d - 1]], recv_sem=rsem.at[n_gb[0]],
            device_id=(lax.rem(s + d, 4), j), device_id_type=MESH_ID)
    n_ol = local.setdefault("go", len(local))

    sgs[...] = jnp.zeros_like(sgs)

    def place(row, total):
        for b in range(NSH):
            sgs[b, pl.ds(row, 1), :] = total[:, 128 * b:128 * b + 128]

    def flat(value):
        return jnp.sum(value, axis=0, keepdims=True)
    place(4, flat(sums[2]))
    place(5, flat(sums[0]))
    place(6, flat(sums[1]))
    place(7, flat(sums[3]))
    d_query_sum = jnp.sum(dqkv[0, :, 0:256].astype(F32) + dqkv[1, :, 0:256].astype(F32), axis=0, keepdims=True)
    d_value_sum = jnp.sum(dqkv[0, :, 512:768].astype(F32) + dqkv[1, :, 512:768].astype(F32), axis=0, keepdims=True)
    for b in range(2):
        sgs[2 * zs + b, pl.ds(2, 1), :] = d_query_sum[:, 128 * b:128 * b + 128]
        sgs[2 * zs + b, pl.ds(3, 1), :] = d_value_sum[:, 128 * b:128 * b + 128]
    up_sum = flat(du_sum)
    row_at = lax.broadcasted_iota(jnp.int32, (8, 128), 0)
    for b in range(NSH):
        wide = jnp.broadcast_to(up_sum[:, 128 * b:128 * b + 128], (8, 128))
        sgs[b, 8:16, :] = jnp.where(row_at == s, wide, 0.0)
    sums_a = (zero8, zero8)
    for i in range(2):
        rs4_wait("da", i, rc, rx)

        def d_input(r, carry, i=i):
            mine = pl.ds(r, 32)
            incoming = rs4_sum(i, r, rc, rx, act)
            scaled, inverse = normal(xin[i, mine, :].astype(F32))
            value = dhid[i, mine, :] + normal_back(incoming, scaled, inverse, attn_gain)
            dx_o[i, mine, :] = value.astype(BF)
            return carry[0] + fold(incoming * scaled), carry[1] + fold(incoming)
        sums_a = tiles(TOK, 32, d_input, sums_a, unroll=True)
        if i == 0:
            rsw_forward("d", gd_o)
            reduce_step()

    place(0, flat(sums_a[0]))
    place(1, flat(sums_a[1]))
    for d in range(1, NSH):
        send("sg", ("sg", d), sgs.at[lax.rem(j + d, NSH)], sg1.at[d - 1], (s, lax.rem(j + d, NSH)))

    copy_u = rsw_end("u", gu, rzu, gu_o)
    reduce_step(2)

    @pl.when(z == zs)
    def _():
        for slot in range(3):
            pltpu.make_async_remote_copy(
                src_ref=go.at[y], dst_ref=rzo.at[slot], send_sem=ssem.at[n_gs], recv_sem=rsem.at[n_gz[slot]],
                device_id=(s, zj(1)), device_id_type=MESH_ID).wait_recv()

        def add(r, _):
            total = go[y, pl.ds(r, 32), :].astype(F32)
            for slot in range(3):
                total = total + rzo[slot, pl.ds(r, 32), :].astype(F32)
            go[y, pl.ds(r, 32), :] = total.astype(BF)
        tiles(128, 32, add, unroll=True)
        pltpu.make_async_copy(go.at[y], go_o, lsem.at[n_ol]).start()
        for d in (1, 2, 3):
            out_final_copy(d).start()

    for d in range(1, NSH):
        jf = lax.rem(j + NSH - d, NSH)
        arrived(("sg", d), sg1.at[d - 1], (s, jf))
    total = sgs[j]
    for d in range(1, NSH):
        total = total + sg1[d - 1]
    sg2[0] = total
    for d in range(1, NSEQ):
        send("sg", ("sh", d), sg2.at[0], sg2.at[d], (lax.rem(s + d, NSEQ), j))
    for i in range(2):
        arrived(("y", "x", i), rx2.at[i], xdev)

        def last(r, _, i=i):
            mine = pl.ds(r, 32)
            out_o[i, mine, :] = (hid[i, mine, :] + rx2[i, mine, :].astype(F32)).astype(BF)
        tiles(TOK, 32, last, unroll=True)
    reduce_step(len(flying) + len(waiting))
    assert not waiting and not flying
    rsw_forward("u", gu_o)
    copy_q = rsw_end("q", gq, rzq, gq_o)
    for d in range(1, NSEQ):
        arrived(("sh", d), sg2.at[d], (lax.rem(s + NSEQ - d, NSEQ), j))
    sg_o[...] = sg2[0] + sg2[1] + sg2[2] + sg2[3]
    rsw_forward("q", gq_o)
    rsw_done("d", gd_o)
    rsw_done("u", gu_o)
    rsw_done("q", gq_o)

    @pl.when(z == zs)
    def _():
        for d in (1, 2, 3):
            out_final_copy(d).wait_send()
        pltpu.make_async_copy(go.at[y], go_o, lsem.at[n_ol]).wait()

    @pl.when(z != zs)
    def _():
        out_final_copy(1).wait_recv()
        out_grad_copy(0).wait_send()
    for copy in (copy_d, copy_u, copy_q):
        copy.wait()

    @pl.when(z == zs)
    def _():
        for d in (1, 2, 3):
            out_copy(d).wait_send()
    for tag in list(pending):
        sent(tag)

def widen_kernel(
    result, d_input, gq, go, gu, gd, small,
    output, input_grad, attn_gain, attn_shift, qkv, query, value, out, out_b, mlp_gain, mlp_shift, up, up_b, down, down_b,
):
    tok = output.shape[0]
    for i in range(2):
        output[:, i, :] = result[i, 0:tok, :]
        input_grad[:, i, :] = d_input[i, 0:tok, :]
    for at, ref in enumerate((attn_gain, attn_shift, query, value, out_b, mlp_gain, mlp_shift, down_b)):
        ref[...] = small[at]
    for b in range(NSEQ):
        up_b[128 * b:128 * b + 128] = small[8 + b]
        for c in range(3):
            qkv[:, 1024 * c + 256 * b:1024 * c + 256 * b + 256] = gq[(b % 2) * 2 + b // 2, :, 256 * c:256 * c + 256].astype(F32)
        for c in range(8):
            up[:, 512 * c + 128 * b:512 * c + 128 * b + 128] = gu[b, :, 128 * c:128 * c + 128].astype(F32)
        down[128 * b:128 * b + 128, :] = gd[b].astype(F32)
    out[...] = go[...].astype(F32)


def fused_device(
    inputs, key_mask, cotangent, attn_gain, attn_shift, qkv_weight, query_bias, value_bias,
    out_weight, out_bias, mlp_gain, mlp_shift, up_weight, up_bias, down_weight, down_bias,
):
    tok = inputs.shape[1]
    lines = [
        entry.reshape(1, 128)
        for entry in (attn_gain, attn_shift, query_bias, value_bias, out_bias, mlp_gain, mlp_shift, down_bias)
    ]
    vm = pl.BlockSpec(memory_space=pltpu.VMEM)
    hbm = pl.BlockSpec(memory_space=pl.ANY)

    def shape(dims, dtype=BF):
        return jax.ShapeDtypeStruct(dims, dtype)

    outs = pl.pallas_call(
        layer_kernel,
        out_shape=(
            shape((2, TOK, D)), shape((2, TOK, D)), shape((4, 128, 768)), shape((128, D)),
            shape((4, 128, D)), shape((4, 128, D)), shape((16, 128), F32),
        ),
        in_specs=[vm] * 12 + [hbm] * 4,
        out_specs=(vm, vm, hbm, hbm, hbm, hbm, vm),
        scratch_shapes=[
            pltpu.VMEM((2, TOK, D), BF),
            pltpu.VMEM((2, TOK, D), BF),
            pltpu.VMEM((16, 128), F32),
            pltpu.VMEM((ROWS, 8), F32),
            pltpu.VMEM((2, ROWS, D), BF),
            pltpu.VMEM((8, 128, 768), BF),
            pltpu.VMEM((2, 128, D), BF),
            pltpu.VMEM((8, 128, D), BF),
            pltpu.VMEM((8, 128, D), BF),
            pltpu.VMEM((8, 16, 128), F32),
            pltpu.VMEM((2, ROWS, 768), BF),
            pltpu.VMEM((2, ROWS, 768), BF),
            pltpu.VMEM((2, HEADS_DEV, ROWS, ROWS), BF),
            pltpu.VMEM((256, ROWS), BF),
            pltpu.VMEM((2, ROWS, 256), BF),
            pltpu.VMEM((2, ROWS, D), BF),
            pltpu.VMEM((2, 2, TOK, D), BF),
            pltpu.VMEM((2, TOK, D), BF),
            pltpu.VMEM((2, 2, TOK, D), BF),
            pltpu.VMEM((2, TOK, D), BF),
            pltpu.VMEM((2, TOK, D), F32),
            pltpu.VMEM((2, ROWS, D), BF),
            pltpu.VMEM((2, ROWS, D), BF),
            pltpu.VMEM((2, ROWS, D), BF),
            pltpu.VMEM((2, ROWS, D), BF),
            pltpu.VMEM((2, TOK, D), F32),
            pltpu.VMEM((2, ROWS, 256), BF),
            pltpu.VMEM((8, 128, 768), BF),
            pltpu.VMEM((2, 128, D), BF),
            pltpu.VMEM((8, 128, D), BF),
            pltpu.VMEM((8, 128, D), BF),
            pltpu.VMEM((4, 128, 768), BF),
            pltpu.VMEM((128, D), BF),
            pltpu.VMEM((4, 128, D), BF),
            pltpu.VMEM((4, 128, D), BF),
            pltpu.VMEM((3, 128, 768), BF),
            pltpu.VMEM((3, 128, D), BF),
            pltpu.VMEM((3, 128, D), BF),
            pltpu.VMEM((3, 128, D), BF),
            pltpu.VMEM((8, 16, 128), F32),
            pltpu.VMEM((7, 16, 128), F32),
            pltpu.VMEM((4, 16, 128), F32),
            pltpu.SemaphoreType.DMA((160,)),
            pltpu.SemaphoreType.DMA((160,)),
            pltpu.SemaphoreType.DMA((24,)),
        ],
        compiler_params=pltpu.CompilerParams(
            collective_id=0, has_side_effects=True, vmem_limit_bytes=VMEM_LIMIT
        ),
        cost_estimate=pl.CostEstimate(flops=26_000_000_000, bytes_accessed=30_000_000, transcendentals=8_000_000),
    )(inputs.transpose(1, 0, 2), cotangent.transpose(1, 0, 2), key_mask, *lines, up_bias.reshape(NSEQ, 128), qkv_weight, out_weight, up_weight, down_weight)
    out, d_input, gq, go, gu, gd, small = outs
    line = shape((128,), F32)
    grads = pl.pallas_call(
        widen_kernel,
        out_shape=(
            shape((tok, 2, D)), shape((tok, 2, D)), line, line, shape((128, 3 * D), F32), line, line, shape((128, D), F32), line, line, line,
            shape((128, 4 * D), F32), shape((512,), F32), shape((512, D), F32), line,
        ),
        in_specs=[vm] * 7,
        out_specs=(vm,) * 15,
        compiler_params=pltpu.CompilerParams(vmem_limit_bytes=WIDEN_LIMIT),
    )(out, d_input, gq, go, gu, gd, small)
    return (grads[0].transpose(1, 0, 2), grads[1].transpose(1, 0, 2)) + tuple(grads[2:])


def solution(mesh):
    in_specs = (
        P("shard", "seq", None),
        P("shard", None),
        P("shard", "seq", None),
        P("shard"),
        P("shard"),
        P("shard", None),
        P("shard"),
        P("shard"),
        P("shard", None),
        P("shard"),
        P("shard"),
        P("shard"),
        P("shard", None),
        P("shard"),
        P("shard", None),
        P("shard"),
    )
    out_specs = (
        P("shard", "seq", None),
        P("shard", "seq", None),
        P("shard"),
        P("shard"),
        P("shard", None),
        P("shard"),
        P("shard"),
        P("shard", None),
        P("shard"),
        P("shard"),
        P("shard"),
        P("shard", None),
        P("shard"),
        P("shard", None),
        P("shard"),
    )
    fits = dict(mesh.shape) == {"seq": NSEQ, "shard": NSH}
    return jax.shard_map(
        fused_device if fits else per_device, mesh=mesh, in_specs=in_specs, out_specs=out_specs, check_vma=False
    )
```

```python
import jax
import jax.numpy as jnp
from jax import lax
from jax.experimental import pallas as pl
from jax.experimental.pallas import tpu as pltpu
from jax.sharding import PartitionSpec as P

D = 1024
HEAD_DIM = 64


EPSILON = 1e-05


def product(left, right):
    return jnp.dot(left, right, preferred_element_type=jnp.float32)


def product_tn(left, right):
    return lax.dot_general(
        left, right, (((0,), (0,)), ((), ())), preferred_element_type=jnp.float32
    )


def product_nt(left, right):
    return lax.dot_general(
        left, right, (((1,), (1,)), ((), ())), preferred_element_type=jnp.float32
    )


def norm_rows(current, gain, shift):
    centre = jnp.mean(current, axis=-1, keepdims=True)
    centred = current - centre
    inverse = lax.rsqrt(jnp.mean(centred * centred, axis=-1, keepdims=True) + EPSILON)
    scaled = centred * inverse
    return (scaled * gain + shift, scaled, inverse)


def norm_back(incoming, scaled, inverse, gain):
    inner = incoming * gain
    d_current = inverse * (
        inner
        - jnp.mean(inner, axis=-1, keepdims=True)
        - scaled * jnp.mean(inner * scaled, axis=-1, keepdims=True)
    )
    return (d_current, jnp.sum(incoming * scaled, axis=0), jnp.sum(incoming, axis=0))


def split_heads(block):
    images, length, width = block.shape
    return block.reshape(images, length, width // HEAD_DIM, HEAD_DIM)


def masked_scores(query_h, keyed_h, key_mask):
    scores = jnp.einsum("iqhd,ikhd->ihqk", query_h, keyed_h, preferred_element_type=jnp.float32)
    scores = scores * HEAD_DIM ** (-0.5)
    return jnp.where(key_mask[:, None, None, :] > 0, scores, -1e30)


def layer_forward(current, key_mask, weights, images):
    (
        attn_gain,
        attn_shift,
        qkv_weight,
        query_bias,
        value_bias,
        out_weight,
        out_bias,
        mlp_gain,
        mlp_shift,
        up_weight,
        up_bias,
        down_weight,
        down_bias,
    ) = weights
    row_count = current.shape[0]
    tok_local = row_count // images
    normed, scaled_a, inverse_a = norm_rows(
        current, attn_gain.astype(jnp.float32), attn_shift.astype(jnp.float32)
    )
    normed_low = normed.astype(jnp.bfloat16)
    packed_bias = jnp.concatenate(
        [
            query_bias.astype(jnp.float32),
            jnp.zeros((D,), jnp.float32),
            value_bias.astype(jnp.float32),
        ]
    )
    packed = (product(normed_low, qkv_weight) + packed_bias).astype(jnp.bfloat16)
    packed = packed.reshape(images, tok_local, 3, D)
    head_view = lax.all_to_all(packed, "seq", split_axis=3, concat_axis=1, tiled=True)
    query_h = split_heads(head_view[:, :, 0])
    keyed_h = split_heads(head_view[:, :, 1])
    value_h = split_heads(head_view[:, :, 2])
    scores = masked_scores(query_h, keyed_h, key_mask)
    row_max = jnp.max(scores, axis=-1, keepdims=True)
    raised = jnp.exp(scores - row_max)
    row_sum = jnp.sum(raised, axis=-1, keepdims=True)
    attn_probs = raised / row_sum
    log_total = row_max + jnp.log(row_sum)
    mixed = jnp.einsum(
        "ihqk,ikhd->iqhd",
        attn_probs.astype(jnp.bfloat16),
        value_h,
        preferred_element_type=jnp.float32,
    )
    seq_len = head_view.shape[1]
    mixed = mixed.reshape(images, seq_len, head_view.shape[3]).astype(jnp.bfloat16)
    merged = lax.all_to_all(mixed, "seq", split_axis=1, concat_axis=2, tiled=True)
    merged_rows = merged.reshape(row_count, D)
    middle = current + product(merged_rows, out_weight) + out_bias.astype(jnp.float32)
    second, scaled_b, inverse_b = norm_rows(
        middle, mlp_gain.astype(jnp.float32), mlp_shift.astype(jnp.float32)
    )
    second_low = second.astype(jnp.bfloat16)
    hidden = product(second_low, up_weight) + up_bias.astype(jnp.float32)
    active = (hidden * jax.nn.sigmoid(1.702 * hidden)).astype(jnp.bfloat16)
    result = middle + product(active, down_weight) + down_bias.astype(jnp.float32)
    stored = (
        scaled_a,
        inverse_a,
        normed_low,
        head_view,
        log_total,
        merged_rows,
        scaled_b,
        inverse_b,
        second_low,
        hidden,
        active,
    )
    return (result, stored)


def layer_backward(upstream, key_mask, weights, stored, images):
    (
        attn_gain,
        attn_shift,
        qkv_weight,
        query_bias,
        value_bias,
        out_weight,
        out_bias,
        mlp_gain,
        mlp_shift,
        up_weight,
        up_bias,
        down_weight,
        down_bias,
    ) = weights
    (
        scaled_a,
        inverse_a,
        normed_low,
        head_view,
        log_total,
        merged_rows,
        scaled_b,
        inverse_b,
        second_low,
        hidden,
        active,
    ) = stored
    row_count = upstream.shape[0]
    tok_local = row_count // images
    branch_low = upstream.astype(jnp.bfloat16)
    grad_down_bias = jnp.sum(branch_low, axis=0, dtype=jnp.float32)
    grad_down_weight = product_tn(active, branch_low)
    d_active = product_nt(branch_low, down_weight)
    gate_sig = jax.nn.sigmoid(1.702 * hidden)
    d_hidden = (d_active * (gate_sig + 1.702 * hidden * gate_sig * (1.0 - gate_sig))).astype(
        jnp.bfloat16
    )
    grad_up_bias = jnp.sum(d_hidden, axis=0, dtype=jnp.float32)
    grad_up_weight = product_tn(second_low, d_hidden)
    d_second = product_nt(d_hidden, up_weight)
    d_norm_b, grad_mlp_gain, grad_mlp_shift = norm_back(
        d_second, scaled_b, inverse_b, mlp_gain.astype(jnp.float32)
    )
    d_middle = upstream + d_norm_b
    d_branch = d_middle.astype(jnp.bfloat16)
    grad_out_bias = jnp.sum(d_branch, axis=0, dtype=jnp.float32)
    grad_out_weight = product_tn(merged_rows, d_branch)
    d_merged = product_nt(d_branch, out_weight).astype(jnp.bfloat16).reshape(images, tok_local, D)
    d_heads = lax.all_to_all(d_merged, "seq", split_axis=2, concat_axis=1, tiled=True)
    query_h = split_heads(head_view[:, :, 0])
    keyed_h = split_heads(head_view[:, :, 1])
    value_h = split_heads(head_view[:, :, 2])
    d_out_h = split_heads(d_heads)
    scores = masked_scores(query_h, keyed_h, key_mask)
    attn_probs = jnp.exp(scores - log_total)
    d_value = jnp.einsum(
        "ihqk,iqhd->ikhd",
        attn_probs.astype(jnp.bfloat16),
        d_out_h,
        preferred_element_type=jnp.float32,
    )
    d_probs = jnp.einsum("iqhd,ikhd->ihqk", d_out_h, value_h, preferred_element_type=jnp.float32)
    d_scores = attn_probs * (d_probs - jnp.sum(attn_probs * d_probs, axis=-1, keepdims=True))
    d_scores = d_scores.astype(jnp.bfloat16)
    d_query = jnp.einsum(
        "ihqk,ikhd->iqhd", d_scores, keyed_h, preferred_element_type=jnp.float32
    ) * HEAD_DIM ** (-0.5)
    d_key = jnp.einsum(
        "ihqk,iqhd->ikhd", d_scores, query_h, preferred_element_type=jnp.float32
    ) * HEAD_DIM ** (-0.5)
    seq_len = head_view.shape[1]
    d_packed = jnp.stack((d_query, d_key, d_value), axis=2).astype(jnp.bfloat16)
    d_packed = d_packed.reshape(images, seq_len, 3, head_view.shape[3])
    d_tokens = lax.all_to_all(d_packed, "seq", split_axis=1, concat_axis=3, tiled=True).reshape(
        row_count, 3 * D
    )
    grad_query_bias = jnp.sum(d_tokens[:, :D], axis=0, dtype=jnp.float32)
    grad_value_bias = jnp.sum(d_tokens[:, 2 * D :], axis=0, dtype=jnp.float32)
    grad_qkv_weight = product_tn(normed_low, d_tokens)
    d_normed = product_nt(d_tokens, qkv_weight)
    d_norm_a, grad_attn_gain, grad_attn_shift = norm_back(
        d_normed, scaled_a, inverse_a, attn_gain.astype(jnp.float32)
    )
    grads = (
        grad_attn_gain,
        grad_attn_shift,
        grad_qkv_weight,
        grad_query_bias,
        grad_value_bias,
        grad_out_weight,
        grad_out_bias,
        grad_mlp_gain,
        grad_mlp_shift,
        grad_up_weight,
        grad_up_bias,
        grad_down_weight,
        grad_down_bias,
    )
    return (d_middle + d_norm_a, grads)


def reduce_grads(grads):
    shares = (
        lax.psum_scatter(
            grads[0].astype(jnp.bfloat16), "shard", scatter_dimension=0, tiled=True
        ).astype(jnp.float32),
        lax.psum_scatter(
            grads[1].astype(jnp.bfloat16), "shard", scatter_dimension=0, tiled=True
        ).astype(jnp.float32),
        lax.psum_scatter(
            grads[2].astype(jnp.bfloat16), "shard", scatter_dimension=0, tiled=True
        ).astype(jnp.float32),
        lax.psum_scatter(
            grads[3].astype(jnp.bfloat16), "shard", scatter_dimension=0, tiled=True
        ).astype(jnp.float32),
        lax.psum_scatter(
            grads[4].astype(jnp.bfloat16), "shard", scatter_dimension=0, tiled=True
        ).astype(jnp.float32),
        lax.psum_scatter(
            grads[5].astype(jnp.bfloat16), "shard", scatter_dimension=0, tiled=True
        ).astype(jnp.float32),
        lax.psum_scatter(
            grads[6].astype(jnp.bfloat16), "shard", scatter_dimension=0, tiled=True
        ).astype(jnp.float32),
        lax.psum_scatter(
            grads[7].astype(jnp.bfloat16), "shard", scatter_dimension=0, tiled=True
        ).astype(jnp.float32),
        lax.psum_scatter(
            grads[8].astype(jnp.bfloat16), "shard", scatter_dimension=0, tiled=True
        ).astype(jnp.float32),
        lax.psum_scatter(
            grads[9].astype(jnp.bfloat16), "shard", scatter_dimension=0, tiled=True
        ).astype(jnp.float32),
        lax.psum_scatter(
            grads[10].astype(jnp.bfloat16), "shard", scatter_dimension=0, tiled=True
        ).astype(jnp.float32),
        lax.psum_scatter(
            grads[11].astype(jnp.bfloat16), "shard", scatter_dimension=0, tiled=True
        ).astype(jnp.float32),
        lax.psum_scatter(
            grads[12].astype(jnp.bfloat16), "shard", scatter_dimension=0, tiled=True
        ).astype(jnp.float32),
    )
    return (
        lax.psum(shares[0].astype(jnp.bfloat16), "seq").astype(jnp.float32),
        lax.psum(shares[1].astype(jnp.bfloat16), "seq").astype(jnp.float32),
        lax.psum(shares[2].astype(jnp.bfloat16), "seq").astype(jnp.float32),
        lax.psum(shares[3].astype(jnp.bfloat16), "seq").astype(jnp.float32),
        lax.psum(shares[4].astype(jnp.bfloat16), "seq").astype(jnp.float32),
        lax.psum(shares[5].astype(jnp.bfloat16), "seq").astype(jnp.float32),
        lax.psum(shares[6].astype(jnp.bfloat16), "seq").astype(jnp.float32),
        lax.psum(shares[7].astype(jnp.bfloat16), "seq").astype(jnp.float32),
        lax.psum(shares[8].astype(jnp.bfloat16), "seq").astype(jnp.float32),
        lax.psum(shares[9].astype(jnp.bfloat16), "seq").astype(jnp.float32),
        lax.psum(shares[10].astype(jnp.bfloat16), "seq").astype(jnp.float32),
        lax.psum(shares[11].astype(jnp.bfloat16), "seq").astype(jnp.float32),
        lax.psum(shares[12].astype(jnp.bfloat16), "seq").astype(jnp.float32),
    )


def per_device(
    inputs,
    key_mask,
    cotangent,
    attn_gain,
    attn_shift,
    qkv_weight,
    query_bias,
    value_bias,
    out_weight,
    out_bias,
    mlp_gain,
    mlp_shift,
    up_weight,
    up_bias,
    down_weight,
    down_bias,
):
    shard_set = (
        attn_gain,
        attn_shift,
        qkv_weight,
        query_bias,
        value_bias,
        out_weight,
        out_bias,
        mlp_gain,
        mlp_shift,
        up_weight,
        up_bias,
        down_weight,
        down_bias,
    )
    images = inputs.shape[0]
    tok_local = inputs.shape[1]
    row_count = images * tok_local
    current = inputs.astype(jnp.float32).reshape(row_count, D)
    gathered = (
        lax.all_gather(shard_set[0], "shard", axis=0, tiled=True),
        lax.all_gather(shard_set[1], "shard", axis=0, tiled=True),
        lax.all_gather(shard_set[2], "shard", axis=0, tiled=True),
        lax.all_gather(shard_set[3], "shard", axis=0, tiled=True),
        lax.all_gather(shard_set[4], "shard", axis=0, tiled=True),
        lax.all_gather(shard_set[5], "shard", axis=0, tiled=True),
        lax.all_gather(shard_set[6], "shard", axis=0, tiled=True),
        lax.all_gather(shard_set[7], "shard", axis=0, tiled=True),
        lax.all_gather(shard_set[8], "shard", axis=0, tiled=True),
        lax.all_gather(shard_set[9], "shard", axis=0, tiled=True),
        lax.all_gather(shard_set[10], "shard", axis=0, tiled=True),
        lax.all_gather(shard_set[11], "shard", axis=0, tiled=True),
        lax.all_gather(shard_set[12], "shard", axis=0, tiled=True),
    )
    result, stored = layer_forward(current, key_mask, gathered, images)
    output = result.astype(jnp.bfloat16).reshape(images, tok_local, D)
    start_row = lax.axis_index("seq") * tok_local
    own_mask = lax.dynamic_slice_in_dim(key_mask, start_row, tok_local, 1).astype(jnp.float32)
    upstream = (cotangent.astype(jnp.float32) * own_mask[:, :, None]).reshape(row_count, D)
    again = (
        lax.all_gather(shard_set[0], "shard", axis=0, tiled=True),
        lax.all_gather(shard_set[1], "shard", axis=0, tiled=True),
        lax.all_gather(shard_set[2], "shard", axis=0, tiled=True),
        lax.all_gather(shard_set[3], "shard", axis=0, tiled=True),
        lax.all_gather(shard_set[4], "shard", axis=0, tiled=True),
        lax.all_gather(shard_set[5], "shard", axis=0, tiled=True),
        lax.all_gather(shard_set[6], "shard", axis=0, tiled=True),
        lax.all_gather(shard_set[7], "shard", axis=0, tiled=True),
        lax.all_gather(shard_set[8], "shard", axis=0, tiled=True),
        lax.all_gather(shard_set[9], "shard", axis=0, tiled=True),
        lax.all_gather(shard_set[10], "shard", axis=0, tiled=True),
        lax.all_gather(shard_set[11], "shard", axis=0, tiled=True),
        lax.all_gather(shard_set[12], "shard", axis=0, tiled=True),
    )
    d_input, grads = layer_backward(upstream, key_mask, again, stored, images)
    reduced = reduce_grads(grads)
    input_grad = d_input.astype(jnp.bfloat16).reshape(images, tok_local, D)
    return (
        output,
        input_grad,
        reduced[0],
        reduced[1],
        reduced[2],
        reduced[3],
        reduced[4],
        reduced[5],
        reduced[6],
        reduced[7],
        reduced[8],
        reduced[9],
        reduced[10],
        reduced[11],
        reduced[12],
    )


STEPS = (1, 3, 2)
PUMPS = (1, 1, 1, 0, 0, 0, 0, 1, 1, 1, 1, 1, 1, 0, 1)
LIMITS = (2, 3, 3, 4, 6, 7, 8, 9, 10, 10, 10)
MT = 640
FLIGHT = 3
NSEQ = 4
NSH = 8
TOK = 160
ROWS = NSEQ * TOK
HEADS_DEV = 4
MASKED = -1e30
VMEM_LIMIT = 64 * 1024 * 1024 - 1024 * 1024
WIDEN_LIMIT = 64 * 1024 * 1024 - 1024 * 1024
MESH_ID = pl.DeviceIdType.MESH
BF = jnp.bfloat16
F32 = jnp.float32
GATE = 1.702


def dot_nn(left, right):
    return lax.dot_general(left, right, (((1,), (0,)), ((), ())), preferred_element_type=F32)


def dot_nt(left, right):
    return lax.dot_general(left, right, (((1,), (1,)), ((), ())), preferred_element_type=F32)


def dot_tn(left, right):
    return lax.dot_general(left, right, (((0,), (0,)), ((), ())), preferred_element_type=F32)


def layer_kernel(
    inp, cot, kmask, b0, b1, b2, b3, b4, b5, b6, b7, b8, wq_h, wo_h, wu_h, wd_h,
    out_o, dx_o, gq_o, go_o, gu_o, gd_o, sg_o,
    xin, dmin, pack, bias_t, xg, wq, wo, wu, wd, pg, qkv, dqkv, probs, mixt, mixed, part, rc, rx, rc2, rx2,
    hid, cg, act, gate, dmg, dhid, dmix,
    gq, go, gu, gd, ryq, ryo, ryu, ryd, rzq, rzo, rzu, rzd, sgs, sg1, sg2,
    ssem, rsem, lsem,
):
    s = lax.axis_index("seq")
    j = lax.axis_index("shard")
    x, k = s // 2, s % 2
    z, y = j // 2, j % 2
    zs = k * 2 + x
    s_core = x * 2 + (1 - k)
    s_x = (1 - x) * 2 + k
    s_diag = (1 - x) * 2 + (1 - k)
    j_y = z * 2 + (1 - y)
    core = (s_core, j)
    xdev = (s_x, j)
    ydev = (s, j_y)

    def zj(d):
        return lax.rem(z + d, 4) * 2 + y

    ids = {}

    def ix(*key):
        return ids.setdefault(key, len(ids))

    pending = {}
    parts = part

    def send(tag, key, src, dst, dev):
        n = ix(*key)
        copy = pltpu.make_async_remote_copy(
            src_ref=src, dst_ref=dst, send_sem=ssem.at[n], recv_sem=rsem.at[n],
            device_id=dev, device_id_type=MESH_ID)
        copy.start()
        pending.setdefault(tag, []).append(copy)

    def sent(tag):
        for copy in pending.pop(tag, []):
            copy.wait_send()

    def arrived(key, dst, dev):
        n = ix(*key)
        pltpu.make_async_remote_copy(
            src_ref=dst, dst_ref=dst, send_sem=ssem.at[n], recv_sem=rsem.at[n],
            device_id=dev, device_id_type=MESH_ID).wait_recv()

    local = {}

    def load(key, src, dst):
        copy = pltpu.make_async_copy(src, dst, lsem.at[local.setdefault(key, len(local))])
        copy.start()
        return copy

    def rows(block):
        return pl.ds(pl.multiple_of(block * TOK, TOK), TOK)

    def tiles(count, step, body, init=None, unroll=False):
        def inner(t, carry):
            return body(pl.multiple_of(t * step, step), carry)
        return lax.fori_loop(0, count // step, inner, init, unroll=unroll)

    barrier = pltpu.get_barrier_semaphore()
    for d in range(1, NSEQ):
        pl.semaphore_signal(barrier, inc=1, device_id=(lax.rem(s + d, NSEQ), j), device_id_type=MESH_ID)
    for d in range(1, NSH):
        pl.semaphore_signal(barrier, inc=1, device_id=(s, lax.rem(j + d, NSH)), device_id_type=MESH_ID)
    loads_q = [load(("wq", c), wq_h.at[:, pl.ds(pl.multiple_of(1024 * c + 256 * zs, 256), 256)],
                    wq.at[j, :, pl.ds(256 * c, 256)]) for c in range(3)]
    loads_u = [load(("wu", c), wu_h.at[:, pl.ds(pl.multiple_of(512 * c + 128 * s, 128), 128)],
                    wu.at[j, :, pl.ds(128 * c, 128)]) for c in range(8)]
    load_d = load(("wd",), wd_h.at[pl.ds(pl.multiple_of(128 * s, 128), 128)], wd.at[j])
    for row, ref in enumerate((b0, b1, b2, b3, b4, b5, b6, b7)):
        pack[row:row + 1, :] = ref[...].astype(F32)
    own_row = lax.broadcasted_iota(jnp.int32, (NSEQ, 128), 0) == s
    pack[8:9, :] = jnp.sum(jnp.where(own_row, b8[...].astype(F32), 0.0), axis=0, keepdims=True)
    pack[9:16, :] = jnp.zeros((7, 128), F32)
    pg[j] = pack[...]

    tok = inp.shape[0]

    def slots_of(source, i):
        row = lax.broadcasted_iota(jnp.int32, (TOK, 2 * tok), 0)
        col = lax.broadcasted_iota(jnp.int32, (TOK, 2 * tok), 1)
        chosen = (col == 2 * row + i).astype(F32).astype(BF)
        return dot_nn(chosen, source[...].reshape(2 * tok, D))
    for i in range(2):
        xin[i] = slots_of(inp, i).astype(BF)
    n_wo = local.setdefault("wo", len(local))

    @pl.when(z == zs)
    def _():
        pltpu.make_async_copy(wo_h, wo.at[y], lsem.at[n_wo]).start()
    pl.semaphore_wait(barrier, NSEQ - 1 + NSH - 1)

    def ag4_start(key, buf, i, src):
        send(key, (key, "c", i), src, buf.at[i, rows(s)], core)
        send(key, (key, "x", i), src, buf.at[i, rows(s)], xdev)

    def ag4_forward(key, buf, i):
        arrived((key, "x", i), buf.at[i, rows(s_x)], xdev)
        send(key + "f", (key, "d", i), buf.at[i, rows(s_x)], buf.at[i, rows(s_x)], core)

    def ag4_end(key, buf, i):
        arrived((key, "c", i), buf.at[i, rows(s_core)], core)
        arrived((key, "d", i), buf.at[i, rows(s_diag)], core)

    weights = {"wq": wq, "wu": wu, "wd": wd}
    n_oz, n_oy = [ix("wo", d) for d in (1, 2, 3)], ix("wo", "y")

    def out_copy(d):
        return pltpu.make_async_remote_copy(
            src_ref=wo.at[y], dst_ref=wo.at[y], send_sem=ssem.at[n_oz[d - 1]], recv_sem=rsem.at[n_oz[0]],
            device_id=(s, zj(d)), device_id_type=MESH_ID)

    def out_start():
        @pl.when(z == zs)
        def _():
            pltpu.make_async_copy(wo_h, wo.at[y], lsem.at[n_wo]).wait()
            for d in (2, 1, 3):
                out_copy(d).start()

    def out_forward():
        @pl.when(z != zs)
        def _():
            pltpu.make_async_remote_copy(
                src_ref=wo.at[y], dst_ref=wo.at[y], send_sem=ssem.at[n_oz[0]], recv_sem=rsem.at[n_oz[0]],
                device_id=(s, zs * 2 + y), device_id_type=MESH_ID).wait_recv()
        send("wo", ("wo", "y"), wo.at[y], wo.at[y], ydev)

    def block_rows(d):
        return (2, pl.ds(64 * (d - 20), 64)) if d >= 20 else (d, pl.ds(0, 128))

    def gather_start(key, d):
        if key == "wo":
            out_start()
            return
        buf = weights[key]
        if d == 1:
            send(key, (key, "y", 0), buf.at[j], buf.at[j], ydev)
        step, part_rows = block_rows(d)
        mine = buf.at[j, part_rows]
        send(key, (key, "z", d), mine, mine, (s, zj(step)))

    def gather_forward(key, d):
        if key == "wo":
            out_forward()
            return
        buf = weights[key]
        step, part_rows = block_rows(d)
        jf = zj(4 - step)
        block = buf.at[jf, part_rows]
        arrived((key, "z", d), block, (s, jf))
        send(key, (key, "y", d), block, block, ydev)

    issue_order = [("wq", d) for d in STEPS] + [("wo", 0)]
    issue_order += [(key, d) for key in ("wu", "wd") for d in STEPS]
    rounds = list(issue_order)
    at_round, issued = [0], [0]

    def gather_issue(upto):
        while issued[0] < min(upto, len(rounds)):
            gather_start(*issue_order[issued[0]])
            issued[0] += 1

    def pump(place):
        for _step in range(PUMPS[place]):
            n = at_round[0]
            gather_forward(*rounds[n])
            at_round[0] = n + 1
            gather_issue(LIMITS[n + 1])

    def agw_end(key, buf):
        for d in (0,) + STEPS:
            step, part_rows = block_rows(d)
            jf = lax.rem(z + 4 - step, 4) * 2 + (1 - y)
            arrived((key, "y", d), buf.at[jf, part_rows], ydev)

    def rs4_a(key, i, rcb):
        part = act if key == "da" else parts
        send(key, (key, "c0", i), part.at[i, rows(s_core)], rcb.at[i, 0], core)
        send(key, (key, "c1", i), part.at[i, rows(s_diag)], rcb.at[i, 1], core)

    def rs4_b(key, i, rcb, rxb):
        arrived((key, "c1", i), rcb.at[i, 1], core)
        part = act if key == "da" else parts

        def add(r, _):
            here = pl.ds(pl.multiple_of(s_x * TOK + r, 32), 32)
            total = part[i, here, :].astype(F32) + rcb[i, 1, pl.ds(r, 32), :].astype(F32)
            part[i, here, :] = total.astype(BF)
        tiles(TOK, 32, add, unroll=True)
        send(key, (key, "x", i), part.at[i, rows(s_x)], rxb.at[i], xdev)

    def rs4_wait(key, i, rcb, rxb):
        arrived((key, "c0", i), rcb.at[i, 0], core)
        arrived((key, "x", i), rxb.at[i], xdev)

    def rs4_sum(i, r, rcb, rxb, part=None):
        part = parts if part is None else part
        here = pl.ds(pl.multiple_of(s * TOK + r, 32), 32)
        return (part[i, here, :].astype(F32) + rcb[i, 0, pl.ds(r, 32), :].astype(F32)
                + rxb[i, pl.ds(r, 32), :].astype(F32))

    def add_into(g, row, others):
        def add(r, _):
            total = g[row, pl.ds(r, 32), :].astype(F32)
            for ref, at in others:
                total = total + ref[at, pl.ds(r, 32), :].astype(F32)
            g[row, pl.ds(r, 32), :] = total.astype(BF)
        tiles(128, 32, add, unroll=True)

    waiting, flying = [], []

    def reduce_fill():
        while waiting and len(flying) < FLIGHT:
            piece = waiting.pop(0)
            key, d, g, ry, rz = piece
            if key == "o":
                send("go", ("go", "y"), g.at[1 - y], ry, ydev)
            else:
                send(key, (key, "gy", d), g.at[lax.rem(z + d, 4) * 2 + (1 - y)], ry.at[d], ydev)
            flying.append(piece)

    def reduce_add(key, g, ry, rz):
        for d in ((0,) if key == "o" else (2, 1, 3, 0)):
            waiting.append((key, d, g, ry, rz))
        reduce_fill()

    def reduce_step(count=1):
        for _step in range(count):
            key, d, g, ry, rz = flying.pop(0)
            if key == "o":
                arrived(("go", "y"), ry, ydev)
                reduce_fill()
                add_out_block()
                continue
            arrived((key, "gy", d), ry.at[d], ydev)
            reduce_fill()
            add_into(g, zj(d), [(ry, d)])
            if d:
                send(key, (key, "gz", d), g.at[zj(d)], rz.at[d - 1], (s, zj(d)))

    n_gz = [ix("goz", d) for d in range(3)]
    n_gs = ix("gozs")

    def out_grad_copy(slot):
        return pltpu.make_async_remote_copy(
            src_ref=go.at[y], dst_ref=rzo.at[slot], send_sem=ssem.at[n_gs], recv_sem=rsem.at[n_gz[0] + slot],
            device_id=(s, zs * 2 + y), device_id_type=MESH_ID)

    def add_out_block():
        def add_out(r, _):
            total = go[y, pl.ds(r, 32), :].astype(F32) + ryo[pl.ds(r, 32), :].astype(F32)
            go[y, pl.ds(r, 32), :] = total.astype(BF)
        tiles(128, 32, add_out, unroll=True)

        @pl.when(z != zs)
        def _():
            out_grad_copy(lax.rem(z + 3 - zs, 4)).start()

    def rsw_end(key, g, rz, g_o):
        for d in (2, 1, 3):
            arrived((key, "gz", d), rz.at[d - 1], (s, zj(4 - d)))
        add_into(g, j, [(rz, 0), (rz, 1), (rz, 2)])
        copy = load((key, "go"), g.at[j], g_o.at[s])
        send(key, (key, "gc"), g.at[j], g_o.at[s], core)
        send(key, (key, "gx"), g.at[j], g_o.at[s], xdev)
        return copy

    def rsw_forward(key, g_o):
        arrived((key, "gx"), g_o.at[s_x], xdev)
        send(key, (key, "gd"), g_o.at[s_x], g_o.at[s_x], core)

    def rsw_done(key, g_o):
        arrived((key, "gc"), g_o.at[s_core], core)
        arrived((key, "gd"), g_o.at[s_diag], core)

    def param(p):
        return jnp.concatenate([pg[b, pl.ds(p, 1), :] for b in range(NSH)], axis=1)

    def head_param(p):
        return jnp.concatenate([pg[2 * zs, pl.ds(p, 1), :], pg[2 * zs + 1, pl.ds(p, 1), :]], axis=1)

    def normal(value):
        centre = jnp.mean(value, axis=-1, keepdims=True)
        centred = value - centre
        inverse = lax.rsqrt(jnp.mean(centred * centred, axis=-1, keepdims=True) + EPSILON)
        return centred * inverse, inverse

    def normal_back(incoming, scaled, inverse, gain):
        inner = incoming * gain
        return inverse * (inner - jnp.mean(inner, axis=-1, keepdims=True)
                          - scaled * jnp.mean(inner * scaled, axis=-1, keepdims=True))

    def fold(value):
        return value[0:8] + value[8:16] + value[16:24] + value[24:32]

    for d in range(1, NSH):
        send("pk", ("pk", d), pack, pg.at[j], (s, lax.rem(j + d, NSH)))
    for i in range(2):
        ag4_start("xg", xg, i, xin.at[i])
    for copy in loads_q:
        copy.wait()
    gather_issue(LIMITS[0])
    slot = lax.broadcasted_iota(jnp.int32, (ROWS, 1), 0)
    shift = sum(jnp.where(slot >= TOK * b, TOK - tok, 0) for b in range(1, NSEQ))
    used = slot - sum(jnp.where(slot >= TOK * b, TOK, 0) for b in range(1, NSEQ)) < tok
    place_of = jnp.where(used, slot - shift, -1)
    chosen = lax.broadcasted_iota(jnp.int32, (ROWS, kmask.shape[1]), 1) == place_of
    live = dot_nt(chosen.astype(F32).astype(BF), kmask[...].astype(F32).astype(BF))
    bias_t[:, 0:2] = jnp.where(live > 0.5, 0.0, MASKED)
    for i in range(2):
        mask = bias_t[pl.ds(pl.multiple_of(s * TOK, TOK), TOK), i:i + 1]
        dmin[i] = jnp.where(mask == 0.0, slots_of(cot, i), 0.0).astype(BF)
        xg[i, rows(s), :] = xin[i]
        dmg[i, rows(s), :] = dmin[i]
    for copy in loads_u:
        copy.wait()
    load_d.wait()
    pump(0)
    ag4_forward("xg", xg, 0)

    for d in range(1, NSH):
        jf = lax.rem(j + NSH - d, NSH)
        arrived(("pk", d), pg.at[jf], (s, jf))
    attn_gain, attn_shift = param(0), param(1)

    def norm_block(i, block):
        def body(r, _):
            here = pl.ds(pl.multiple_of(block * TOK + r, 32), 32)
            scaled, _inverse = normal(xg[i, here, :].astype(F32))
            xg[i, here, :] = (scaled * attn_gain + attn_shift).astype(BF)
        tiles(TOK, 32, body, unroll=True)

    norm_block(0, s)
    norm_block(1, s)
    pump(1)
    for i in range(2):
        arrived(("xg", "c", i), xg.at[i, rows(s_core)], core)
        norm_block(i, s_core)
    ag4_forward("xg", xg, 1)
    for i in range(2):
        ag4_start("dm", dmg, i, dmin.at[i])
    arrived(("xg", "d", 0), xg.at[0, rows(s_diag)], core)
    norm_block(0, s_diag)
    sent("xgf")
    pump(2)
    norm_block(0, s_x)
    norm_block(1, s_x)
    arrived(("xg", "d", 1), xg.at[1, rows(s_diag)], core)
    norm_block(1, s_diag)
    pump(3)
    agw_end("wq", wq)

    packed_bias = jnp.concatenate([head_param(2), jnp.zeros((1, 256), F32), head_param(3)], axis=1)

    def project_in(i):
        def project(r, _):
            here = pl.ds(r, MT)
            value = dot_nn(xg[i, here, :], wq[...].reshape(D, 768)) + packed_bias
            qkv[i, here, :] = value.astype(BF)
        tiles(ROWS, MT, project)

    def attend(i, first, last):
        if first == 0:
            mixt[...] = qkv[i, :, 512:768].astype(F32).T.astype(BF)
        lane = lax.broadcasted_iota(jnp.int32, (1, 256), 1) // HEAD_DIM

        def one_head(h, _):
            keyed = jnp.where(lane == h, qkv[i, :, 256:512], jnp.zeros((), BF))
            query = qkv[i, :, 0:256] * jnp.asarray(HEAD_DIM ** -0.5, BF)
            scores = dot_nt(keyed, query) + bias_t[:, i:i + 1]
            raised = jnp.exp(scores - jnp.max(scores, axis=0, keepdims=True))
            chances = (raised * (1.0 / jnp.sum(raised, axis=0, keepdims=True))).astype(BF)
            probs[i, h] = chances
            here = pl.ds(pl.multiple_of(h * HEAD_DIM, HEAD_DIM), HEAD_DIM)
            mixt[here, :] = dot_nn(mixt[here, :], chances).astype(BF)
        lax.fori_loop(first, last, one_head, None)
        if last == HEADS_DEV:
            mixed[i] = mixt[...].astype(F32).T.astype(BF)

    def project_out(i):
        def body(r, _):
            here = pl.ds(r, MT)
            part[i, here, :] = dot_nn(mixed[i, here, :], wo[...].reshape(256, D)).astype(BF)
        tiles(ROWS, MT, body)

    project_in(0)
    attend(0, 0, 2)
    pump(14)
    attend(0, 2, 4)
    pump(4)
    project_in(1)
    arrived(("wo", "y"), wo.at[1 - y], ydev)
    project_out(0)
    rs4_a("o", 0, rc)
    pump(5)
    attend(1, 0, 2)
    pump(6)
    attend(1, 2, 4)
    rs4_b("o", 0, rc, rx)
    project_out(1)
    rs4_a("o", 1, rc)
    pump(7)
    rs4_b("o", 1, rc, rx)
    for i in range(2):
        ag4_forward("dm", dmg, i)
    pump(8)

    out_bias, mlp_gain, mlp_shift, down_bias = param(4), param(5), param(6), param(7)
    up_bias = param(8)

    for i in range(2):
        rs4_wait("o", i, rc, rx)

        def middle(r, _, i=i):
            value = xin[i, pl.ds(r, 32), :].astype(F32) + (rs4_sum(i, r, rc, rx) + out_bias)
            hid[i, pl.ds(r, 32), :] = value
            scaled, _inverse = normal(value)
            here = pl.ds(pl.multiple_of(s * TOK + r, 32), 32)
            cg[i, here, :] = (scaled * mlp_gain + mlp_shift).astype(BF)
        tiles(TOK, 32, middle, unroll=True)
        ag4_start("c", cg, i, cg.at[i, rows(s)])
        pump(9 + i)
    for n in range(2):
        ag4_end("dm", dmg, n)
    agw_end("wu", wu)
    for i in range(2):
        ag4_forward("c", cg, i)
        ag4_end("c", cg, i)

        def up(r, _, i=i):
            here = pl.ds(r, MT)
            value = dot_nn(cg[i, here, :], wu[...].reshape(D, D)) + up_bias
            sig = jax.nn.sigmoid(GATE * value)
            act[i, here, :] = (value * sig).astype(BF)
            gate[i, here, :] = (sig + GATE * value * sig * (1.0 - sig)).astype(BF)
        tiles(ROWS, MT, up)
        pump(11 + i)
    sent("o")

    def weight_grad(left, right, g):
        def body(t, _):
            cols = pl.ds(pl.multiple_of(t * 512, 512), 512)
            value = dot_tn(left[:, :, cols].reshape(2 * ROWS, 512), right[...].reshape(2 * ROWS, right.shape[2]))
            g[pl.ds(4 * t, 4)] = value.astype(BF).reshape(4, 128, right.shape[2])
        lax.fori_loop(0, left.shape[2] // 512, body, None)

    weight_grad(act, dmg, gd)
    pump(13)
    reduce_add("d", gd, ryd, rzd)
    agw_end("wd", wd)

    def d_up(i, total):
        def body(r, carry):
            here = pl.ds(r, MT)
            value = dot_nt(dmg[i, here, :], wd[...].reshape(D, D)) * gate[i, here, :].astype(F32)
            value = value.astype(BF)
            gate[i, here, :] = value
            return carry + jnp.sum(value.astype(F32).reshape(MT // 8, 8, D), axis=0)
        return tiles(ROWS, MT, body, total)

    def d_second(i):
        def body(r, _):
            here = pl.ds(r, MT)
            part[i, here, :] = dot_nt(gate[i, here, :], wu[...].reshape(D, D)).astype(BF)
        tiles(ROWS, MT, body)

    sent("dmf")
    sent("dm")
    du_sum = d_up(0, jnp.zeros((8, D), F32))
    d_second(0)
    rs4_a("dc", 0, rc)
    du_sum = d_up(1, du_sum)
    rs4_b("dc", 0, rc, rx)
    d_second(1)
    rs4_a("dc", 1, rc)
    reduce_step()
    rs4_b("dc", 1, rc, rx)
    weight_grad(cg, gate, gu)
    reduce_add("u", gu, ryu, rzu)
    reduce_step()

    zero8 = jnp.zeros((8, D), F32)
    sums = (zero8, zero8, zero8, zero8)
    for i in range(2):
        rs4_wait("dc", i, rc, rx)

        def d_middle(r, carry, i=i):
            mine = pl.ds(r, 32)
            incoming = rs4_sum(i, r, rc, rx)
            scaled, inverse = normal(hid[i, mine, :])
            upstream = dmin[i, mine, :].astype(F32)
            value = upstream + normal_back(incoming, scaled, inverse, mlp_gain)
            dhid[i, mine, :] = value
            low = value.astype(BF)
            dmg[i, pl.ds(pl.multiple_of(s * TOK + r, 32), 32), :] = low
            return (carry[0] + fold(incoming * scaled), carry[1] + fold(incoming),
                    carry[2] + fold(low.astype(F32)), carry[3] + fold(upstream))
        sums = tiles(TOK, 32, d_middle, sums, unroll=True)
        ag4_start("db", dmg, i, dmg.at[i, rows(s)])
        reduce_step()
    sent("dc")

    for i in range(2):
        def down(r, _, i=i):
            here = pl.ds(r, MT)
            part[i, here, :] = dot_nn(act[i, here, :], wd[...].reshape(D, D)).astype(BF)
        tiles(ROWS, MT, down)

    def attend_back(i, first, last):
        if first == 0:
            def d_mixed(r, _):
                here = pl.ds(r, MT)
                dmix[i, here, :] = dot_nt(dmg[i, here, :], wo[...].reshape(256, D)).astype(BF)
            tiles(ROWS, MT, d_mixed)
            mixt[...] = qkv[i, :, 256:512].astype(F32).T.astype(BF)
        lane = lax.broadcasted_iota(jnp.int32, (1, 256), 1) // HEAD_DIM

        def one_head(h, _):
            own = lane == h
            chances = probs[i, h]
            d_value = dot_nn(chances, dmix[i])
            dqkv[i, :, 512:768] = jnp.where(own, d_value.astype(BF), dqkv[i, :, 512:768])
            valued = jnp.where(own, qkv[i, :, 512:768], jnp.zeros((), BF))
            d_chances = dot_nt(valued, dmix[i])
            wide = chances.astype(F32)
            d_scores = wide * (d_chances - jnp.sum(wide * d_chances, axis=0, keepdims=True))
            d_scores = d_scores.astype(BF)
            d_key = dot_nn(d_scores, qkv[i, :, 0:256]) * HEAD_DIM ** -0.5
            dqkv[i, :, 256:512] = jnp.where(own, d_key.astype(BF), dqkv[i, :, 256:512])
            here = pl.ds(pl.multiple_of(h * HEAD_DIM, HEAD_DIM), HEAD_DIM)
            mixt[here, :] = (dot_nn(mixt[here, :], d_scores) * HEAD_DIM ** -0.5).astype(BF)
        lax.fori_loop(first, last, one_head, None)
        if last == HEADS_DEV:
            dqkv[i, :, 0:256] = mixt[...].astype(F32).T.astype(BF)

    def out_presum(i):
        arrived(("y", "c0", i), rc2.at[i, 0], core)
        arrived(("y", "c1", i), rc2.at[i, 1], core)

        def body(r, _):
            mine = pl.ds(r, 32)
            here = pl.ds(pl.multiple_of(s * TOK + r, 32), 32)
            there = pl.ds(pl.multiple_of(s_x * TOK + r, 32), 32)
            total = part[i, here, :].astype(F32) + rc2[i, 0, mine, :].astype(F32)
            hid[i, mine, :] = hid[i, mine, :] + (total + down_bias)
            total = part[i, there, :].astype(F32) + rc2[i, 1, mine, :].astype(F32)
            rc2[i, 1, mine, :] = total.astype(BF)
        tiles(TOK, 32, body, unroll=True)

    def d_normed(i):
        def body(r, _):
            here = pl.ds(r, MT)
            act[i, here, :] = dot_nt(dqkv[i, here, :], wq[...].reshape(D, 768)).astype(BF)
        tiles(ROWS, MT, body)
        rs4_a("da", i, rc)

    ag4_forward("db", dmg, 0)
    ag4_end("db", dmg, 0)
    for i in range(2):
        rs4_a("y", i, rc2)
    attend_back(0, 0, 4)
    reduce_step()
    ag4_forward("db", dmg, 1)
    d_normed(0)
    ag4_end("db", dmg, 1)
    copy_d = rsw_end("d", gd, rzd, gd_o)
    attend_back(1, 0, 2)
    rs4_b("da", 0, rc, rx)
    attend_back(1, 2, 4)
    reduce_step()
    d_normed(1)
    weight_grad(xg, dqkv, gq)
    rs4_b("da", 1, rc, rx)
    value = dot_tn(mixed[...].reshape(2 * ROWS, 256), dmg[...].reshape(2 * ROWS, D))
    go[...] = value.astype(BF).reshape(2, 128, D)
    reduce_add("o", go, ryo, rzo)
    reduce_add("q", gq, ryq, rzq)
    reduce_step()
    for i in range(2):
        out_presum(i)
        send("y", ("y", "x", i), rc2.at[i, 1], rx2.at[i], xdev)
    reduce_step()

    n_gb = [ix("gob", d) for d in range(3)]

    def out_final_copy(d):
        return pltpu.make_async_remote_copy(
            src_ref=go.at[y], dst_ref=go_o, send_sem=ssem.at[n_gb[d - 1]], recv_sem=rsem.at[n_gb[0]],
            device_id=(lax.rem(s + d, 4), j), device_id_type=MESH_ID)
    n_ol = local.setdefault("go", len(local))

    sgs[...] = jnp.zeros_like(sgs)

    def place(row, total):
        for b in range(NSH):
            sgs[b, pl.ds(row, 1), :] = total[:, 128 * b:128 * b + 128]

    def flat(value):
        return jnp.sum(value, axis=0, keepdims=True)
    place(4, flat(sums[2]))
    place(5, flat(sums[0]))
    place(6, flat(sums[1]))
    place(7, flat(sums[3]))
    d_query_sum = jnp.sum(dqkv[0, :, 0:256].astype(F32) + dqkv[1, :, 0:256].astype(F32), axis=0, keepdims=True)
    d_value_sum = jnp.sum(dqkv[0, :, 512:768].astype(F32) + dqkv[1, :, 512:768].astype(F32), axis=0, keepdims=True)
    for b in range(2):
        sgs[2 * zs + b, pl.ds(2, 1), :] = d_query_sum[:, 128 * b:128 * b + 128]
        sgs[2 * zs + b, pl.ds(3, 1), :] = d_value_sum[:, 128 * b:128 * b + 128]
    up_sum = flat(du_sum)
    row_at = lax.broadcasted_iota(jnp.int32, (8, 128), 0)
    for b in range(NSH):
        wide = jnp.broadcast_to(up_sum[:, 128 * b:128 * b + 128], (8, 128))
        sgs[b, 8:16, :] = jnp.where(row_at == s, wide, 0.0)
    sums_a = (zero8, zero8)
    for i in range(2):
        rs4_wait("da", i, rc, rx)

        def d_input(r, carry, i=i):
            mine = pl.ds(r, 32)
            incoming = rs4_sum(i, r, rc, rx, act)
            scaled, inverse = normal(xin[i, mine, :].astype(F32))
            value = dhid[i, mine, :] + normal_back(incoming, scaled, inverse, attn_gain)
            dx_o[i, mine, :] = value.astype(BF)
            return carry[0] + fold(incoming * scaled), carry[1] + fold(incoming)
        sums_a = tiles(TOK, 32, d_input, sums_a, unroll=True)
        if i == 0:
            rsw_forward("d", gd_o)
            reduce_step()

    place(0, flat(sums_a[0]))
    place(1, flat(sums_a[1]))
    for d in range(1, NSH):
        send("sg", ("sg", d), sgs.at[lax.rem(j + d, NSH)], sg1.at[d - 1], (s, lax.rem(j + d, NSH)))

    copy_u = rsw_end("u", gu, rzu, gu_o)
    reduce_step(2)

    @pl.when(z == zs)
    def _():
        for slot in range(3):
            pltpu.make_async_remote_copy(
                src_ref=go.at[y], dst_ref=rzo.at[slot], send_sem=ssem.at[n_gs], recv_sem=rsem.at[n_gz[slot]],
                device_id=(s, zj(1)), device_id_type=MESH_ID).wait_recv()

        def add(r, _):
            total = go[y, pl.ds(r, 32), :].astype(F32)
            for slot in range(3):
                total = total + rzo[slot, pl.ds(r, 32), :].astype(F32)
            go[y, pl.ds(r, 32), :] = total.astype(BF)
        tiles(128, 32, add, unroll=True)
        pltpu.make_async_copy(go.at[y], go_o, lsem.at[n_ol]).start()
        for d in (1, 2, 3):
            out_final_copy(d).start()

    for d in range(1, NSH):
        jf = lax.rem(j + NSH - d, NSH)
        arrived(("sg", d), sg1.at[d - 1], (s, jf))
    total = sgs[j]
    for d in range(1, NSH):
        total = total + sg1[d - 1]
    sg2[0] = total
    for d in range(1, NSEQ):
        send("sg", ("sh", d), sg2.at[0], sg2.at[d], (lax.rem(s + d, NSEQ), j))
    for i in range(2):
        arrived(("y", "x", i), rx2.at[i], xdev)

        def last(r, _, i=i):
            mine = pl.ds(r, 32)
            out_o[i, mine, :] = (hid[i, mine, :] + rx2[i, mine, :].astype(F32)).astype(BF)
        tiles(TOK, 32, last, unroll=True)
    reduce_step(len(flying) + len(waiting))
    assert not waiting and not flying
    rsw_forward("u", gu_o)
    copy_q = rsw_end("q", gq, rzq, gq_o)
    for d in range(1, NSEQ):
        arrived(("sh", d), sg2.at[d], (lax.rem(s + NSEQ - d, NSEQ), j))
    sg_o[...] = sg2[0] + sg2[1] + sg2[2] + sg2[3]
    rsw_forward("q", gq_o)
    rsw_done("d", gd_o)
    rsw_done("u", gu_o)
    rsw_done("q", gq_o)

    @pl.when(z == zs)
    def _():
        for d in (1, 2, 3):
            out_final_copy(d).wait_send()
        pltpu.make_async_copy(go.at[y], go_o, lsem.at[n_ol]).wait()

    @pl.when(z != zs)
    def _():
        out_final_copy(1).wait_recv()
        out_grad_copy(0).wait_send()
    for copy in (copy_d, copy_u, copy_q):
        copy.wait()

    @pl.when(z == zs)
    def _():
        for d in (1, 2, 3):
            out_copy(d).wait_send()
    for tag in list(pending):
        sent(tag)

def widen_kernel(
    result, d_input, gq, go, gu, gd, small,
    output, input_grad, attn_gain, attn_shift, qkv, query, value, out, out_b, mlp_gain, mlp_shift, up, up_b, down, down_b,
):
    tok = output.shape[0]
    for i in range(2):
        output[:, i, :] = result[i, 0:tok, :]
        input_grad[:, i, :] = d_input[i, 0:tok, :]
    for at, ref in enumerate((attn_gain, attn_shift, query, value, out_b, mlp_gain, mlp_shift, down_b)):
        ref[...] = small[at]
    for b in range(NSEQ):
        up_b[128 * b:128 * b + 128] = small[8 + b]
        for c in range(3):
            qkv[:, 1024 * c + 256 * b:1024 * c + 256 * b + 256] = gq[(b % 2) * 2 + b // 2, :, 256 * c:256 * c + 256].astype(F32)
        for c in range(8):
            up[:, 512 * c + 128 * b:512 * c + 128 * b + 128] = gu[b, :, 128 * c:128 * c + 128].astype(F32)
        down[128 * b:128 * b + 128, :] = gd[b].astype(F32)
    out[...] = go[...].astype(F32)


def fused_device(
    inputs, key_mask, cotangent, attn_gain, attn_shift, qkv_weight, query_bias, value_bias,
    out_weight, out_bias, mlp_gain, mlp_shift, up_weight, up_bias, down_weight, down_bias,
):
    tok = inputs.shape[1]
    lines = [
        entry.reshape(1, 128)
        for entry in (attn_gain, attn_shift, query_bias, value_bias, out_bias, mlp_gain, mlp_shift, down_bias)
    ]
    vm = pl.BlockSpec(memory_space=pltpu.VMEM)
    hbm = pl.BlockSpec(memory_space=pl.ANY)

    def shape(dims, dtype=BF):
        return jax.ShapeDtypeStruct(dims, dtype)

    outs = pl.pallas_call(
        layer_kernel,
        out_shape=(
            shape((2, TOK, D)), shape((2, TOK, D)), shape((4, 128, 768)), shape((128, D)),
            shape((4, 128, D)), shape((4, 128, D)), shape((16, 128), F32),
        ),
        in_specs=[vm] * 12 + [hbm] * 4,
        out_specs=(vm, vm, hbm, hbm, hbm, hbm, vm),
        scratch_shapes=[
            pltpu.VMEM((2, TOK, D), BF),
            pltpu.VMEM((2, TOK, D), BF),
            pltpu.VMEM((16, 128), F32),
            pltpu.VMEM((ROWS, 8), F32),
            pltpu.VMEM((2, ROWS, D), BF),
            pltpu.VMEM((8, 128, 768), BF),
            pltpu.VMEM((2, 128, D), BF),
            pltpu.VMEM((8, 128, D), BF),
            pltpu.VMEM((8, 128, D), BF),
            pltpu.VMEM((8, 16, 128), F32),
            pltpu.VMEM((2, ROWS, 768), BF),
            pltpu.VMEM((2, ROWS, 768), BF),
            pltpu.VMEM((2, HEADS_DEV, ROWS, ROWS), BF),
            pltpu.VMEM((256, ROWS), BF),
            pltpu.VMEM((2, ROWS, 256), BF),
            pltpu.VMEM((2, ROWS, D), BF),
            pltpu.VMEM((2, 2, TOK, D), BF),
            pltpu.VMEM((2, TOK, D), BF),
            pltpu.VMEM((2, 2, TOK, D), BF),
            pltpu.VMEM((2, TOK, D), BF),
            pltpu.VMEM((2, TOK, D), F32),
            pltpu.VMEM((2, ROWS, D), BF),
            pltpu.VMEM((2, ROWS, D), BF),
            pltpu.VMEM((2, ROWS, D), BF),
            pltpu.VMEM((2, ROWS, D), BF),
            pltpu.VMEM((2, TOK, D), F32),
            pltpu.VMEM((2, ROWS, 256), BF),
            pltpu.VMEM((8, 128, 768), BF),
            pltpu.VMEM((2, 128, D), BF),
            pltpu.VMEM((8, 128, D), BF),
            pltpu.VMEM((8, 128, D), BF),
            pltpu.VMEM((4, 128, 768), BF),
            pltpu.VMEM((128, D), BF),
            pltpu.VMEM((4, 128, D), BF),
            pltpu.VMEM((4, 128, D), BF),
            pltpu.VMEM((3, 128, 768), BF),
            pltpu.VMEM((3, 128, D), BF),
            pltpu.VMEM((3, 128, D), BF),
            pltpu.VMEM((3, 128, D), BF),
            pltpu.VMEM((8, 16, 128), F32),
            pltpu.VMEM((7, 16, 128), F32),
            pltpu.VMEM((4, 16, 128), F32),
            pltpu.SemaphoreType.DMA((160,)),
            pltpu.SemaphoreType.DMA((160,)),
            pltpu.SemaphoreType.DMA((24,)),
        ],
        compiler_params=pltpu.CompilerParams(
            collective_id=0, has_side_effects=True, vmem_limit_bytes=VMEM_LIMIT
        ),
        cost_estimate=pl.CostEstimate(flops=26_000_000_000, bytes_accessed=30_000_000, transcendentals=8_000_000),
    )(inputs.transpose(1, 0, 2), cotangent.transpose(1, 0, 2), key_mask, *lines, up_bias.reshape(NSEQ, 128), qkv_weight, out_weight, up_weight, down_weight)
    out, d_input, gq, go, gu, gd, small = outs
    line = shape((128,), F32)
    grads = pl.pallas_call(
        widen_kernel,
        out_shape=(
            shape((tok, 2, D)), shape((tok, 2, D)), line, line, shape((128, 3 * D), F32), line, line, shape((128, D), F32), line, line, line,
            shape((128, 4 * D), F32), shape((512,), F32), shape((512, D), F32), line,
        ),
        in_specs=[vm] * 7,
        out_specs=(vm,) * 15,
        compiler_params=pltpu.CompilerParams(vmem_limit_bytes=WIDEN_LIMIT),
    )(out, d_input, gq, go, gu, gd, small)
    return (grads[0].transpose(1, 0, 2), grads[1].transpose(1, 0, 2)) + tuple(grads[2:])


def solution(mesh):
    in_specs = (
        P("shard", "seq", None),
        P("shard", None),
        P("shard", "seq", None),
        P("shard"),
        P("shard"),
        P("shard", None),
        P("shard"),
        P("shard"),
        P("shard", None),
        P("shard"),
        P("shard"),
        P("shard"),
        P("shard", None),
        P("shard"),
        P("shard", None),
        P("shard"),
    )
    out_specs = (
        P("shard", "seq", None),
        P("shard", "seq", None),
        P("shard"),
        P("shard"),
        P("shard", None),
        P("shard"),
        P("shard"),
        P("shard", None),
        P("shard"),
        P("shard"),
        P("shard"),
        P("shard", None),
        P("shard"),
        P("shard", None),
        P("shard"),
    )
    fits = dict(mesh.shape) == {"seq": NSEQ, "shard": NSH}
    return jax.shard_map(
        fused_device if fits else per_device, mesh=mesh, in_specs=in_specs, out_specs=out_specs, check_vma=False
    )
```

```python
import jax
import jax.numpy as jnp
from jax import lax
from jax.experimental import pallas as pl
from jax.experimental.pallas import tpu as pltpu
from jax.sharding import PartitionSpec as P

D = 1024
HEAD_DIM = 64


EPSILON = 1e-05


def product(left, right):
    return jnp.dot(left, right, preferred_element_type=jnp.float32)


def product_tn(left, right):
    return lax.dot_general(
        left, right, (((0,), (0,)), ((), ())), preferred_element_type=jnp.float32
    )


def product_nt(left, right):
    return lax.dot_general(
        left, right, (((1,), (1,)), ((), ())), preferred_element_type=jnp.float32
    )


def norm_rows(current, gain, shift):
    centre = jnp.mean(current, axis=-1, keepdims=True)
    centred = current - centre
    inverse = lax.rsqrt(jnp.mean(centred * centred, axis=-1, keepdims=True) + EPSILON)
    scaled = centred * inverse
    return (scaled * gain + shift, scaled, inverse)


def norm_back(incoming, scaled, inverse, gain):
    inner = incoming * gain
    d_current = inverse * (
        inner
        - jnp.mean(inner, axis=-1, keepdims=True)
        - scaled * jnp.mean(inner * scaled, axis=-1, keepdims=True)
    )
    return (d_current, jnp.sum(incoming * scaled, axis=0), jnp.sum(incoming, axis=0))


def split_heads(block):
    images, length, width = block.shape
    return block.reshape(images, length, width // HEAD_DIM, HEAD_DIM)


def masked_scores(query_h, keyed_h, key_mask):
    scores = jnp.einsum("iqhd,ikhd->ihqk", query_h, keyed_h, preferred_element_type=jnp.float32)
    scores = scores * HEAD_DIM ** (-0.5)
    return jnp.where(key_mask[:, None, None, :] > 0, scores, -1e30)


def layer_forward(current, key_mask, weights, images):
    (
        attn_gain,
        attn_shift,
        qkv_weight,
        query_bias,
        value_bias,
        out_weight,
        out_bias,
        mlp_gain,
        mlp_shift,
        up_weight,
        up_bias,
        down_weight,
        down_bias,
    ) = weights
    row_count = current.shape[0]
    tok_local = row_count // images
    normed, scaled_a, inverse_a = norm_rows(
        current, attn_gain.astype(jnp.float32), attn_shift.astype(jnp.float32)
    )
    normed_low = normed.astype(jnp.bfloat16)
    packed_bias = jnp.concatenate(
        [
            query_bias.astype(jnp.float32),
            jnp.zeros((D,), jnp.float32),
            value_bias.astype(jnp.float32),
        ]
    )
    packed = (product(normed_low, qkv_weight) + packed_bias).astype(jnp.bfloat16)
    packed = packed.reshape(images, tok_local, 3, D)
    head_view = lax.all_to_all(packed, "seq", split_axis=3, concat_axis=1, tiled=True)
    query_h = split_heads(head_view[:, :, 0])
    keyed_h = split_heads(head_view[:, :, 1])
    value_h = split_heads(head_view[:, :, 2])
    scores = masked_scores(query_h, keyed_h, key_mask)
    row_max = jnp.max(scores, axis=-1, keepdims=True)
    raised = jnp.exp(scores - row_max)
    row_sum = jnp.sum(raised, axis=-1, keepdims=True)
    attn_probs = raised / row_sum
    log_total = row_max + jnp.log(row_sum)
    mixed = jnp.einsum(
        "ihqk,ikhd->iqhd",
        attn_probs.astype(jnp.bfloat16),
        value_h,
        preferred_element_type=jnp.float32,
    )
    seq_len = head_view.shape[1]
    mixed = mixed.reshape(images, seq_len, head_view.shape[3]).astype(jnp.bfloat16)
    merged = lax.all_to_all(mixed, "seq", split_axis=1, concat_axis=2, tiled=True)
    merged_rows = merged.reshape(row_count, D)
    middle = current + product(merged_rows, out_weight) + out_bias.astype(jnp.float32)
    second, scaled_b, inverse_b = norm_rows(
        middle, mlp_gain.astype(jnp.float32), mlp_shift.astype(jnp.float32)
    )
    second_low = second.astype(jnp.bfloat16)
    hidden = product(second_low, up_weight) + up_bias.astype(jnp.float32)
    active = (hidden * jax.nn.sigmoid(1.702 * hidden)).astype(jnp.bfloat16)
    result = middle + product(active, down_weight) + down_bias.astype(jnp.float32)
    stored = (
        scaled_a,
        inverse_a,
        normed_low,
        head_view,
        log_total,
        merged_rows,
        scaled_b,
        inverse_b,
        second_low,
        hidden,
        active,
    )
    return (result, stored)


def layer_backward(upstream, key_mask, weights, stored, images):
    (
        attn_gain,
        attn_shift,
        qkv_weight,
        query_bias,
        value_bias,
        out_weight,
        out_bias,
        mlp_gain,
        mlp_shift,
        up_weight,
        up_bias,
        down_weight,
        down_bias,
    ) = weights
    (
        scaled_a,
        inverse_a,
        normed_low,
        head_view,
        log_total,
        merged_rows,
        scaled_b,
        inverse_b,
        second_low,
        hidden,
        active,
    ) = stored
    row_count = upstream.shape[0]
    tok_local = row_count // images
    branch_low = upstream.astype(jnp.bfloat16)
    grad_down_bias = jnp.sum(branch_low, axis=0, dtype=jnp.float32)
    grad_down_weight = product_tn(active, branch_low)
    d_active = product_nt(branch_low, down_weight)
    gate_sig = jax.nn.sigmoid(1.702 * hidden)
    d_hidden = (d_active * (gate_sig + 1.702 * hidden * gate_sig * (1.0 - gate_sig))).astype(
        jnp.bfloat16
    )
    grad_up_bias = jnp.sum(d_hidden, axis=0, dtype=jnp.float32)
    grad_up_weight = product_tn(second_low, d_hidden)
    d_second = product_nt(d_hidden, up_weight)
    d_norm_b, grad_mlp_gain, grad_mlp_shift = norm_back(
        d_second, scaled_b, inverse_b, mlp_gain.astype(jnp.float32)
    )
    d_middle = upstream + d_norm_b
    d_branch = d_middle.astype(jnp.bfloat16)
    grad_out_bias = jnp.sum(d_branch, axis=0, dtype=jnp.float32)
    grad_out_weight = product_tn(merged_rows, d_branch)
    d_merged = product_nt(d_branch, out_weight).astype(jnp.bfloat16).reshape(images, tok_local, D)
    d_heads = lax.all_to_all(d_merged, "seq", split_axis=2, concat_axis=1, tiled=True)
    query_h = split_heads(head_view[:, :, 0])
    keyed_h = split_heads(head_view[:, :, 1])
    value_h = split_heads(head_view[:, :, 2])
    d_out_h = split_heads(d_heads)
    scores = masked_scores(query_h, keyed_h, key_mask)
    attn_probs = jnp.exp(scores - log_total)
    d_value = jnp.einsum(
        "ihqk,iqhd->ikhd",
        attn_probs.astype(jnp.bfloat16),
        d_out_h,
        preferred_element_type=jnp.float32,
    )
    d_probs = jnp.einsum("iqhd,ikhd->ihqk", d_out_h, value_h, preferred_element_type=jnp.float32)
    d_scores = attn_probs * (d_probs - jnp.sum(attn_probs * d_probs, axis=-1, keepdims=True))
    d_scores = d_scores.astype(jnp.bfloat16)
    d_query = jnp.einsum(
        "ihqk,ikhd->iqhd", d_scores, keyed_h, preferred_element_type=jnp.float32
    ) * HEAD_DIM ** (-0.5)
    d_key = jnp.einsum(
        "ihqk,iqhd->ikhd", d_scores, query_h, preferred_element_type=jnp.float32
    ) * HEAD_DIM ** (-0.5)
    seq_len = head_view.shape[1]
    d_packed = jnp.stack((d_query, d_key, d_value), axis=2).astype(jnp.bfloat16)
    d_packed = d_packed.reshape(images, seq_len, 3, head_view.shape[3])
    d_tokens = lax.all_to_all(d_packed, "seq", split_axis=1, concat_axis=3, tiled=True).reshape(
        row_count, 3 * D
    )
    grad_query_bias = jnp.sum(d_tokens[:, :D], axis=0, dtype=jnp.float32)
    grad_value_bias = jnp.sum(d_tokens[:, 2 * D :], axis=0, dtype=jnp.float32)
    grad_qkv_weight = product_tn(normed_low, d_tokens)
    d_normed = product_nt(d_tokens, qkv_weight)
    d_norm_a, grad_attn_gain, grad_attn_shift = norm_back(
        d_normed, scaled_a, inverse_a, attn_gain.astype(jnp.float32)
    )
    grads = (
        grad_attn_gain,
        grad_attn_shift,
        grad_qkv_weight,
        grad_query_bias,
        grad_value_bias,
        grad_out_weight,
        grad_out_bias,
        grad_mlp_gain,
        grad_mlp_shift,
        grad_up_weight,
        grad_up_bias,
        grad_down_weight,
        grad_down_bias,
    )
    return (d_middle + d_norm_a, grads)


def reduce_grads(grads):
    shares = (
        lax.psum_scatter(
            grads[0].astype(jnp.bfloat16), "shard", scatter_dimension=0, tiled=True
        ).astype(jnp.float32),
        lax.psum_scatter(
            grads[1].astype(jnp.bfloat16), "shard", scatter_dimension=0, tiled=True
        ).astype(jnp.float32),
        lax.psum_scatter(
            grads[2].astype(jnp.bfloat16), "shard", scatter_dimension=0, tiled=True
        ).astype(jnp.float32),
        lax.psum_scatter(
            grads[3].astype(jnp.bfloat16), "shard", scatter_dimension=0, tiled=True
        ).astype(jnp.float32),
        lax.psum_scatter(
            grads[4].astype(jnp.bfloat16), "shard", scatter_dimension=0, tiled=True
        ).astype(jnp.float32),
        lax.psum_scatter(
            grads[5].astype(jnp.bfloat16), "shard", scatter_dimension=0, tiled=True
        ).astype(jnp.float32),
        lax.psum_scatter(
            grads[6].astype(jnp.bfloat16), "shard", scatter_dimension=0, tiled=True
        ).astype(jnp.float32),
        lax.psum_scatter(
            grads[7].astype(jnp.bfloat16), "shard", scatter_dimension=0, tiled=True
        ).astype(jnp.float32),
        lax.psum_scatter(
            grads[8].astype(jnp.bfloat16), "shard", scatter_dimension=0, tiled=True
        ).astype(jnp.float32),
        lax.psum_scatter(
            grads[9].astype(jnp.bfloat16), "shard", scatter_dimension=0, tiled=True
        ).astype(jnp.float32),
        lax.psum_scatter(
            grads[10].astype(jnp.bfloat16), "shard", scatter_dimension=0, tiled=True
        ).astype(jnp.float32),
        lax.psum_scatter(
            grads[11].astype(jnp.bfloat16), "shard", scatter_dimension=0, tiled=True
        ).astype(jnp.float32),
        lax.psum_scatter(
            grads[12].astype(jnp.bfloat16), "shard", scatter_dimension=0, tiled=True
        ).astype(jnp.float32),
    )
    return (
        lax.psum(shares[0].astype(jnp.bfloat16), "seq").astype(jnp.float32),
        lax.psum(shares[1].astype(jnp.bfloat16), "seq").astype(jnp.float32),
        lax.psum(shares[2].astype(jnp.bfloat16), "seq").astype(jnp.float32),
        lax.psum(shares[3].astype(jnp.bfloat16), "seq").astype(jnp.float32),
        lax.psum(shares[4].astype(jnp.bfloat16), "seq").astype(jnp.float32),
        lax.psum(shares[5].astype(jnp.bfloat16), "seq").astype(jnp.float32),
        lax.psum(shares[6].astype(jnp.bfloat16), "seq").astype(jnp.float32),
        lax.psum(shares[7].astype(jnp.bfloat16), "seq").astype(jnp.float32),
        lax.psum(shares[8].astype(jnp.bfloat16), "seq").astype(jnp.float32),
        lax.psum(shares[9].astype(jnp.bfloat16), "seq").astype(jnp.float32),
        lax.psum(shares[10].astype(jnp.bfloat16), "seq").astype(jnp.float32),
        lax.psum(shares[11].astype(jnp.bfloat16), "seq").astype(jnp.float32),
        lax.psum(shares[12].astype(jnp.bfloat16), "seq").astype(jnp.float32),
    )


def per_device(
    inputs,
    key_mask,
    cotangent,
    attn_gain,
    attn_shift,
    qkv_weight,
    query_bias,
    value_bias,
    out_weight,
    out_bias,
    mlp_gain,
    mlp_shift,
    up_weight,
    up_bias,
    down_weight,
    down_bias,
):
    shard_set = (
        attn_gain,
        attn_shift,
        qkv_weight,
        query_bias,
        value_bias,
        out_weight,
        out_bias,
        mlp_gain,
        mlp_shift,
        up_weight,
        up_bias,
        down_weight,
        down_bias,
    )
    images = inputs.shape[0]
    tok_local = inputs.shape[1]
    row_count = images * tok_local
    current = inputs.astype(jnp.float32).reshape(row_count, D)
    gathered = (
        lax.all_gather(shard_set[0], "shard", axis=0, tiled=True),
        lax.all_gather(shard_set[1], "shard", axis=0, tiled=True),
        lax.all_gather(shard_set[2], "shard", axis=0, tiled=True),
        lax.all_gather(shard_set[3], "shard", axis=0, tiled=True),
        lax.all_gather(shard_set[4], "shard", axis=0, tiled=True),
        lax.all_gather(shard_set[5], "shard", axis=0, tiled=True),
        lax.all_gather(shard_set[6], "shard", axis=0, tiled=True),
        lax.all_gather(shard_set[7], "shard", axis=0, tiled=True),
        lax.all_gather(shard_set[8], "shard", axis=0, tiled=True),
        lax.all_gather(shard_set[9], "shard", axis=0, tiled=True),
        lax.all_gather(shard_set[10], "shard", axis=0, tiled=True),
        lax.all_gather(shard_set[11], "shard", axis=0, tiled=True),
        lax.all_gather(shard_set[12], "shard", axis=0, tiled=True),
    )
    result, stored = layer_forward(current, key_mask, gathered, images)
    output = result.astype(jnp.bfloat16).reshape(images, tok_local, D)
    start_row = lax.axis_index("seq") * tok_local
    own_mask = lax.dynamic_slice_in_dim(key_mask, start_row, tok_local, 1).astype(jnp.float32)
    upstream = (cotangent.astype(jnp.float32) * own_mask[:, :, None]).reshape(row_count, D)
    again = (
        lax.all_gather(shard_set[0], "shard", axis=0, tiled=True),
        lax.all_gather(shard_set[1], "shard", axis=0, tiled=True),
        lax.all_gather(shard_set[2], "shard", axis=0, tiled=True),
        lax.all_gather(shard_set[3], "shard", axis=0, tiled=True),
        lax.all_gather(shard_set[4], "shard", axis=0, tiled=True),
        lax.all_gather(shard_set[5], "shard", axis=0, tiled=True),
        lax.all_gather(shard_set[6], "shard", axis=0, tiled=True),
        lax.all_gather(shard_set[7], "shard", axis=0, tiled=True),
        lax.all_gather(shard_set[8], "shard", axis=0, tiled=True),
        lax.all_gather(shard_set[9], "shard", axis=0, tiled=True),
        lax.all_gather(shard_set[10], "shard", axis=0, tiled=True),
        lax.all_gather(shard_set[11], "shard", axis=0, tiled=True),
        lax.all_gather(shard_set[12], "shard", axis=0, tiled=True),
    )
    d_input, grads = layer_backward(upstream, key_mask, again, stored, images)
    reduced = reduce_grads(grads)
    input_grad = d_input.astype(jnp.bfloat16).reshape(images, tok_local, D)
    return (
        output,
        input_grad,
        reduced[0],
        reduced[1],
        reduced[2],
        reduced[3],
        reduced[4],
        reduced[5],
        reduced[6],
        reduced[7],
        reduced[8],
        reduced[9],
        reduced[10],
        reduced[11],
        reduced[12],
    )


STEPS = (1, 3, 2)
PUMPS = (1, 1, 1, 0, 0, 0, 0, 1, 1, 1, 1, 1, 1, 0, 1)
LIMITS = (2, 3, 3, 4, 6, 7, 8, 9, 10, 10, 10)
MT = 640
FLIGHT = 5
NSEQ = 4
NSH = 8
TOK = 160
ROWS = NSEQ * TOK
HEADS_DEV = 4
MASKED = -1e30
VMEM_LIMIT = 64 * 1024 * 1024 - 1024 * 1024
WIDEN_LIMIT = 64 * 1024 * 1024 - 1024 * 1024
MESH_ID = pl.DeviceIdType.MESH
BF = jnp.bfloat16
F32 = jnp.float32
GATE = 1.702


def dot_nn(left, right):
    return lax.dot_general(left, right, (((1,), (0,)), ((), ())), preferred_element_type=F32)


def dot_nt(left, right):
    return lax.dot_general(left, right, (((1,), (1,)), ((), ())), preferred_element_type=F32)


def dot_tn(left, right):
    return lax.dot_general(left, right, (((0,), (0,)), ((), ())), preferred_element_type=F32)


def layer_kernel(
    inp, cot, kmask, b0, b1, b2, b3, b4, b5, b6, b7, b8, wq_h, wo_h, wu_h, wd_h,
    out_o, dx_o, gq_o, go_o, gu_o, gd_o, sg_o,
    xin, dmin, pack, bias_t, xg, wq, wo, wu, wd, pg, qkv, dqkv, probs, mixt, mixed, part, rc, rx, rc2, rx2,
    hid, cg, act, gate, dmg, dhid, dmix,
    gq, go, gu, gd, ryq, ryo, ryu, ryd, rzq, rzo, rzu, rzd, sgs, sg1, sg2,
    ssem, rsem, lsem,
):
    s = lax.axis_index("seq")
    j = lax.axis_index("shard")
    x, k = s // 2, s % 2
    z, y = j // 2, j % 2
    zs = k * 2 + x
    s_core = x * 2 + (1 - k)
    s_x = (1 - x) * 2 + k
    s_diag = (1 - x) * 2 + (1 - k)
    j_y = z * 2 + (1 - y)
    core = (s_core, j)
    xdev = (s_x, j)
    ydev = (s, j_y)

    def zj(d):
        return lax.rem(z + d, 4) * 2 + y

    ids = {}

    def ix(*key):
        return ids.setdefault(key, len(ids))

    pending = {}
    parts = part

    def send(tag, key, src, dst, dev):
        n = ix(*key)
        copy = pltpu.make_async_remote_copy(
            src_ref=src, dst_ref=dst, send_sem=ssem.at[n], recv_sem=rsem.at[n],
            device_id=dev, device_id_type=MESH_ID)
        copy.start()
        pending.setdefault(tag, []).append(copy)

    def sent(tag):
        for copy in pending.pop(tag, []):
            copy.wait_send()

    def arrived(key, dst, dev):
        n = ix(*key)
        pltpu.make_async_remote_copy(
            src_ref=dst, dst_ref=dst, send_sem=ssem.at[n], recv_sem=rsem.at[n],
            device_id=dev, device_id_type=MESH_ID).wait_recv()

    local = {}

    def load(key, src, dst):
        copy = pltpu.make_async_copy(src, dst, lsem.at[local.setdefault(key, len(local))])
        copy.start()
        return copy

    def rows(block):
        return pl.ds(pl.multiple_of(block * TOK, TOK), TOK)

    def tiles(count, step, body, init=None, unroll=False):
        def inner(t, carry):
            return body(pl.multiple_of(t * step, step), carry)
        return lax.fori_loop(0, count // step, inner, init, unroll=unroll)

    barrier = pltpu.get_barrier_semaphore()
    for d in range(1, NSEQ):
        pl.semaphore_signal(barrier, inc=1, device_id=(lax.rem(s + d, NSEQ), j), device_id_type=MESH_ID)
    for d in range(1, NSH):
        pl.semaphore_signal(barrier, inc=1, device_id=(s, lax.rem(j + d, NSH)), device_id_type=MESH_ID)
    loads_q = [load(("wq", c), wq_h.at[:, pl.ds(pl.multiple_of(1024 * c + 256 * zs, 256), 256)],
                    wq.at[j, :, pl.ds(256 * c, 256)]) for c in range(3)]
    loads_u = [load(("wu", c), wu_h.at[:, pl.ds(pl.multiple_of(512 * c + 128 * s, 128), 128)],
                    wu.at[j, :, pl.ds(128 * c, 128)]) for c in range(8)]
    load_d = load(("wd",), wd_h.at[pl.ds(pl.multiple_of(128 * s, 128), 128)], wd.at[j])
    for row, ref in enumerate((b0, b1, b2, b3, b4, b5, b6, b7)):
        pack[row:row + 1, :] = ref[...].astype(F32)
    own_row = lax.broadcasted_iota(jnp.int32, (NSEQ, 128), 0) == s
    pack[8:9, :] = jnp.sum(jnp.where(own_row, b8[...].astype(F32), 0.0), axis=0, keepdims=True)
    pack[9:16, :] = jnp.zeros((7, 128), F32)
    pg[j] = pack[...]

    tok = inp.shape[0]

    def slots_of(source, i):
        row = lax.broadcasted_iota(jnp.int32, (TOK, 2 * tok), 0)
        col = lax.broadcasted_iota(jnp.int32, (TOK, 2 * tok), 1)
        chosen = (col == 2 * row + i).astype(F32).astype(BF)
        return dot_nn(chosen, source[...].reshape(2 * tok, D))
    for i in range(2):
        xin[i] = slots_of(inp, i).astype(BF)
    n_wo = local.setdefault("wo", len(local))

    @pl.when(z == zs)
    def _():
        pltpu.make_async_copy(wo_h, wo.at[y], lsem.at[n_wo]).start()
    pl.semaphore_wait(barrier, NSEQ - 1 + NSH - 1)

    def ag4_start(key, buf, i, src):
        send(key, (key, "c", i), src, buf.at[i, rows(s)], core)
        send(key, (key, "x", i), src, buf.at[i, rows(s)], xdev)

    def ag4_forward(key, buf, i):
        arrived((key, "x", i), buf.at[i, rows(s_x)], xdev)
        send(key + "f", (key, "d", i), buf.at[i, rows(s_x)], buf.at[i, rows(s_x)], core)

    def ag4_end(key, buf, i):
        arrived((key, "c", i), buf.at[i, rows(s_core)], core)
        arrived((key, "d", i), buf.at[i, rows(s_diag)], core)

    weights = {"wq": wq, "wu": wu, "wd": wd}
    n_oz, n_oy = [ix("wo", d) for d in (1, 2, 3)], ix("wo", "y")

    def out_copy(d):
        return pltpu.make_async_remote_copy(
            src_ref=wo.at[y], dst_ref=wo.at[y], send_sem=ssem.at[n_oz[d - 1]], recv_sem=rsem.at[n_oz[0]],
            device_id=(s, zj(d)), device_id_type=MESH_ID)

    def out_start():
        @pl.when(z == zs)
        def _():
            pltpu.make_async_copy(wo_h, wo.at[y], lsem.at[n_wo]).wait()
            for d in (2, 1, 3):
                out_copy(d).start()

    def out_forward():
        @pl.when(z != zs)
        def _():
            pltpu.make_async_remote_copy(
                src_ref=wo.at[y], dst_ref=wo.at[y], send_sem=ssem.at[n_oz[0]], recv_sem=rsem.at[n_oz[0]],
                device_id=(s, zs * 2 + y), device_id_type=MESH_ID).wait_recv()
        send("wo", ("wo", "y"), wo.at[y], wo.at[y], ydev)

    def block_rows(d):
        return (2, pl.ds(64 * (d - 20), 64)) if d >= 20 else (d, pl.ds(0, 128))

    def gather_start(key, d):
        if key == "wo":
            out_start()
            return
        buf = weights[key]
        if d == 1:
            send(key, (key, "y", 0), buf.at[j], buf.at[j], ydev)
        step, part_rows = block_rows(d)
        mine = buf.at[j, part_rows]
        send(key, (key, "z", d), mine, mine, (s, zj(step)))

    def gather_forward(key, d):
        if key == "wo":
            out_forward()
            return
        buf = weights[key]
        step, part_rows = block_rows(d)
        jf = zj(4 - step)
        block = buf.at[jf, part_rows]
        arrived((key, "z", d), block, (s, jf))
        send(key, (key, "y", d), block, block, ydev)

    issue_order = [("wq", d) for d in STEPS] + [("wo", 0)]
    issue_order += [(key, d) for key in ("wu", "wd") for d in STEPS]
    rounds = list(issue_order)
    at_round, issued = [0], [0]

    def gather_issue(upto):
        while issued[0] < min(upto, len(rounds)):
            gather_start(*issue_order[issued[0]])
            issued[0] += 1

    def pump(place):
        for _step in range(PUMPS[place]):
            n = at_round[0]
            gather_forward(*rounds[n])
            at_round[0] = n + 1
            gather_issue(LIMITS[n + 1])

    def agw_end(key, buf):
        for d in (0,) + STEPS:
            step, part_rows = block_rows(d)
            jf = lax.rem(z + 4 - step, 4) * 2 + (1 - y)
            arrived((key, "y", d), buf.at[jf, part_rows], ydev)

    def rs4_a(key, i, rcb):
        part = act if key == "da" else parts
        send(key, (key, "c0", i), part.at[i, rows(s_core)], rcb.at[i, 0], core)
        send(key, (key, "c1", i), part.at[i, rows(s_diag)], rcb.at[i, 1], core)

    def rs4_b(key, i, rcb, rxb):
        arrived((key, "c1", i), rcb.at[i, 1], core)
        part = act if key == "da" else parts

        def add(r, _):
            here = pl.ds(pl.multiple_of(s_x * TOK + r, 32), 32)
            total = part[i, here, :].astype(F32) + rcb[i, 1, pl.ds(r, 32), :].astype(F32)
            part[i, here, :] = total.astype(BF)
        tiles(TOK, 32, add, unroll=True)
        send(key, (key, "x", i), part.at[i, rows(s_x)], rxb.at[i], xdev)

    def rs4_wait(key, i, rcb, rxb):
        arrived((key, "c0", i), rcb.at[i, 0], core)
        arrived((key, "x", i), rxb.at[i], xdev)

    def rs4_sum(i, r, rcb, rxb, part=None):
        part = parts if part is None else part
        here = pl.ds(pl.multiple_of(s * TOK + r, 32), 32)
        return (part[i, here, :].astype(F32) + rcb[i, 0, pl.ds(r, 32), :].astype(F32)
                + rxb[i, pl.ds(r, 32), :].astype(F32))

    def add_into(g, row, others):
        def add(r, _):
            total = g[row, pl.ds(r, 32), :].astype(F32)
            for ref, at in others:
                total = total + ref[at, pl.ds(r, 32), :].astype(F32)
            g[row, pl.ds(r, 32), :] = total.astype(BF)
        tiles(128, 32, add, unroll=True)

    waiting, flying = [], []

    def reduce_fill():
        while waiting and len(flying) < FLIGHT:
            piece = waiting.pop(0)
            key, d, g, ry, rz = piece
            if key == "o":
                send("go", ("go", "y"), g.at[1 - y], ry, ydev)
            else:
                send(key, (key, "gy", d), g.at[lax.rem(z + d, 4) * 2 + (1 - y)], ry.at[d], ydev)
            flying.append(piece)

    def reduce_add(key, g, ry, rz):
        for d in ((0,) if key == "o" else (2, 1, 3, 0)):
            waiting.append((key, d, g, ry, rz))
        reduce_fill()

    def reduce_step(count=1):
        for _step in range(count):
            key, d, g, ry, rz = flying.pop(0)
            if key == "o":
                arrived(("go", "y"), ry, ydev)
                reduce_fill()
                add_out_block()
                continue
            arrived((key, "gy", d), ry.at[d], ydev)
            reduce_fill()
            add_into(g, zj(d), [(ry, d)])
            if d:
                send(key, (key, "gz", d), g.at[zj(d)], rz.at[d - 1], (s, zj(d)))

    n_gz = [ix("goz", d) for d in range(3)]
    n_gs = ix("gozs")

    def out_grad_copy(slot):
        return pltpu.make_async_remote_copy(
            src_ref=go.at[y], dst_ref=rzo.at[slot], send_sem=ssem.at[n_gs], recv_sem=rsem.at[n_gz[0] + slot],
            device_id=(s, zs * 2 + y), device_id_type=MESH_ID)

    def add_out_block():
        def add_out(r, _):
            total = go[y, pl.ds(r, 32), :].astype(F32) + ryo[pl.ds(r, 32), :].astype(F32)
            go[y, pl.ds(r, 32), :] = total.astype(BF)
        tiles(128, 32, add_out, unroll=True)

        @pl.when(z != zs)
        def _():
            out_grad_copy(lax.rem(z + 3 - zs, 4)).start()

    def rsw_end(key, g, rz, g_o):
        for d in (2, 1, 3):
            arrived((key, "gz", d), rz.at[d - 1], (s, zj(4 - d)))
        add_into(g, j, [(rz, 0), (rz, 1), (rz, 2)])
        copy = load((key, "go"), g.at[j], g_o.at[s])
        send(key, (key, "gc"), g.at[j], g_o.at[s], core)
        send(key, (key, "gx"), g.at[j], g_o.at[s], xdev)
        return copy

    def rsw_forward(key, g_o):
        arrived((key, "gx"), g_o.at[s_x], xdev)
        send(key, (key, "gd"), g_o.at[s_x], g_o.at[s_x], core)

    def rsw_done(key, g_o):
        arrived((key, "gc"), g_o.at[s_core], core)
        arrived((key, "gd"), g_o.at[s_diag], core)

    def param(p):
        return jnp.concatenate([pg[b, pl.ds(p, 1), :] for b in range(NSH)], axis=1)

    def head_param(p):
        return jnp.concatenate([pg[2 * zs, pl.ds(p, 1), :], pg[2 * zs + 1, pl.ds(p, 1), :]], axis=1)

    def normal(value):
        centre = jnp.mean(value, axis=-1, keepdims=True)
        centred = value - centre
        inverse = lax.rsqrt(jnp.mean(centred * centred, axis=-1, keepdims=True) + EPSILON)
        return centred * inverse, inverse

    def normal_back(incoming, scaled, inverse, gain):
        inner = incoming * gain
        return inverse * (inner - jnp.mean(inner, axis=-1, keepdims=True)
                          - scaled * jnp.mean(inner * scaled, axis=-1, keepdims=True))

    def fold(value):
        return value[0:8] + value[8:16] + value[16:24] + value[24:32]

    for d in range(1, NSH):
        send("pk", ("pk", d), pack, pg.at[j], (s, lax.rem(j + d, NSH)))
    for i in range(2):
        ag4_start("xg", xg, i, xin.at[i])
    for copy in loads_q:
        copy.wait()
    gather_issue(LIMITS[0])
    slot = lax.broadcasted_iota(jnp.int32, (ROWS, 1), 0)
    shift = sum(jnp.where(slot >= TOK * b, TOK - tok, 0) for b in range(1, NSEQ))
    used = slot - sum(jnp.where(slot >= TOK * b, TOK, 0) for b in range(1, NSEQ)) < tok
    place_of = jnp.where(used, slot - shift, -1)
    chosen = lax.broadcasted_iota(jnp.int32, (ROWS, kmask.shape[1]), 1) == place_of
    live = dot_nt(chosen.astype(F32).astype(BF), kmask[...].astype(F32).astype(BF))
    bias_t[:, 0:2] = jnp.where(live > 0.5, 0.0, MASKED)
    for i in range(2):
        mask = bias_t[pl.ds(pl.multiple_of(s * TOK, TOK), TOK), i:i + 1]
        dmin[i] = jnp.where(mask == 0.0, slots_of(cot, i), 0.0).astype(BF)
        xg[i, rows(s), :] = xin[i]
        dmg[i, rows(s), :] = dmin[i]
    for copy in loads_u:
        copy.wait()
    load_d.wait()
    pump(0)
    ag4_forward("xg", xg, 0)

    for d in range(1, NSH):
        jf = lax.rem(j + NSH - d, NSH)
        arrived(("pk", d), pg.at[jf], (s, jf))
    attn_gain, attn_shift = param(0), param(1)

    def norm_block(i, block):
        def body(r, _):
            here = pl.ds(pl.multiple_of(block * TOK + r, 32), 32)
            scaled, _inverse = normal(xg[i, here, :].astype(F32))
            xg[i, here, :] = (scaled * attn_gain + attn_shift).astype(BF)
        tiles(TOK, 32, body, unroll=True)

    norm_block(0, s)
    norm_block(1, s)
    pump(1)
    for i in range(2):
        arrived(("xg", "c", i), xg.at[i, rows(s_core)], core)
        norm_block(i, s_core)
    ag4_forward("xg", xg, 1)
    for i in range(2):
        ag4_start("dm", dmg, i, dmin.at[i])
    arrived(("xg", "d", 0), xg.at[0, rows(s_diag)], core)
    norm_block(0, s_diag)
    sent("xgf")
    pump(2)
    norm_block(0, s_x)
    norm_block(1, s_x)
    arrived(("xg", "d", 1), xg.at[1, rows(s_diag)], core)
    norm_block(1, s_diag)
    pump(3)
    agw_end("wq", wq)

    packed_bias = jnp.concatenate([head_param(2), jnp.zeros((1, 256), F32), head_param(3)], axis=1)

    def project_in(i):
        def project(r, _):
            here = pl.ds(r, MT)
            value = dot_nn(xg[i, here, :], wq[...].reshape(D, 768)) + packed_bias
            qkv[i, here, :] = value.astype(BF)
        tiles(ROWS, MT, project)

    def attend(i, first, last):
        if first == 0:
            mixt[...] = qkv[i, :, 512:768].astype(F32).T.astype(BF)
        lane = lax.broadcasted_iota(jnp.int32, (1, 256), 1) // HEAD_DIM

        def one_head(h, _):
            keyed = jnp.where(lane == h, qkv[i, :, 256:512], jnp.zeros((), BF))
            query = qkv[i, :, 0:256] * jnp.asarray(HEAD_DIM ** -0.5, BF)
            scores = dot_nt(keyed, query) + bias_t[:, i:i + 1]
            raised = jnp.exp(scores - jnp.max(scores, axis=0, keepdims=True))
            chances = (raised * (1.0 / jnp.sum(raised, axis=0, keepdims=True))).astype(BF)
            probs[i, h] = chances
            here = pl.ds(pl.multiple_of(h * HEAD_DIM, HEAD_DIM), HEAD_DIM)
            mixt[here, :] = dot_nn(mixt[here, :], chances).astype(BF)
        lax.fori_loop(first, last, one_head, None)
        if last == HEADS_DEV:
            mixed[i] = mixt[...].astype(F32).T.astype(BF)

    def project_out(i):
        def body(r, _):
            here = pl.ds(r, MT)
            part[i, here, :] = dot_nn(mixed[i, here, :], wo[...].reshape(256, D)).astype(BF)
        tiles(ROWS, MT, body)

    project_in(0)
    attend(0, 0, 2)
    pump(14)
    attend(0, 2, 4)
    pump(4)
    project_in(1)
    arrived(("wo", "y"), wo.at[1 - y], ydev)
    project_out(0)
    rs4_a("o", 0, rc)
    pump(5)
    attend(1, 0, 2)
    pump(6)
    attend(1, 2, 4)
    rs4_b("o", 0, rc, rx)
    project_out(1)
    rs4_a("o", 1, rc)
    pump(7)
    rs4_b("o", 1, rc, rx)
    for i in range(2):
        ag4_forward("dm", dmg, i)
    pump(8)

    out_bias, mlp_gain, mlp_shift, down_bias = param(4), param(5), param(6), param(7)
    up_bias = param(8)

    for i in range(2):
        rs4_wait("o", i, rc, rx)

        def middle(r, _, i=i):
            value = xin[i, pl.ds(r, 32), :].astype(F32) + (rs4_sum(i, r, rc, rx) + out_bias)
            hid[i, pl.ds(r, 32), :] = value
            scaled, _inverse = normal(value)
            here = pl.ds(pl.multiple_of(s * TOK + r, 32), 32)
            cg[i, here, :] = (scaled * mlp_gain + mlp_shift).astype(BF)
        tiles(TOK, 32, middle, unroll=True)
        ag4_start("c", cg, i, cg.at[i, rows(s)])
        pump(9 + i)
    for n in range(2):
        ag4_end("dm", dmg, n)
    agw_end("wu", wu)
    for i in range(2):
        ag4_forward("c", cg, i)
        ag4_end("c", cg, i)

        def up(r, _, i=i):
            here = pl.ds(r, MT)
            value = dot_nn(cg[i, here, :], wu[...].reshape(D, D)) + up_bias
            sig = jax.nn.sigmoid(GATE * value)
            act[i, here, :] = (value * sig).astype(BF)
            gate[i, here, :] = (sig + GATE * value * sig * (1.0 - sig)).astype(BF)
        tiles(ROWS, MT, up)
        pump(11 + i)
    sent("o")

    def weight_grad(left, right, g):
        def body(t, _):
            cols = pl.ds(pl.multiple_of(t * 512, 512), 512)
            value = dot_tn(left[:, :, cols].reshape(2 * ROWS, 512), right[...].reshape(2 * ROWS, right.shape[2]))
            g[pl.ds(4 * t, 4)] = value.astype(BF).reshape(4, 128, right.shape[2])
        lax.fori_loop(0, left.shape[2] // 512, body, None)

    weight_grad(act, dmg, gd)
    pump(13)
    reduce_add("d", gd, ryd, rzd)
    agw_end("wd", wd)

    def d_up(i, total):
        def body(r, carry):
            here = pl.ds(r, MT)
            value = dot_nt(dmg[i, here, :], wd[...].reshape(D, D)) * gate[i, here, :].astype(F32)
            value = value.astype(BF)
            gate[i, here, :] = value
            return carry + jnp.sum(value.astype(F32).reshape(MT // 8, 8, D), axis=0)
        return tiles(ROWS, MT, body, total)

    def d_second(i):
        def body(r, _):
            here = pl.ds(r, MT)
            part[i, here, :] = dot_nt(gate[i, here, :], wu[...].reshape(D, D)).astype(BF)
        tiles(ROWS, MT, body)

    sent("dmf")
    sent("dm")
    du_sum = d_up(0, jnp.zeros((8, D), F32))
    d_second(0)
    rs4_a("dc", 0, rc)
    du_sum = d_up(1, du_sum)
    rs4_b("dc", 0, rc, rx)
    d_second(1)
    rs4_a("dc", 1, rc)
    reduce_step()
    rs4_b("dc", 1, rc, rx)
    weight_grad(cg, gate, gu)
    reduce_add("u", gu, ryu, rzu)
    reduce_step()

    zero8 = jnp.zeros((8, D), F32)
    sums = (zero8, zero8, zero8, zero8)
    for i in range(2):
        rs4_wait("dc", i, rc, rx)

        def d_middle(r, carry, i=i):
            mine = pl.ds(r, 32)
            incoming = rs4_sum(i, r, rc, rx)
            scaled, inverse = normal(hid[i, mine, :])
            upstream = dmin[i, mine, :].astype(F32)
            value = upstream + normal_back(incoming, scaled, inverse, mlp_gain)
            dhid[i, mine, :] = value
            low = value.astype(BF)
            dmg[i, pl.ds(pl.multiple_of(s * TOK + r, 32), 32), :] = low
            return (carry[0] + fold(incoming * scaled), carry[1] + fold(incoming),
                    carry[2] + fold(low.astype(F32)), carry[3] + fold(upstream))
        sums = tiles(TOK, 32, d_middle, sums, unroll=True)
        ag4_start("db", dmg, i, dmg.at[i, rows(s)])
        reduce_step()
    sent("dc")

    for i in range(2):
        def down(r, _, i=i):
            here = pl.ds(r, MT)
            part[i, here, :] = dot_nn(act[i, here, :], wd[...].reshape(D, D)).astype(BF)
        tiles(ROWS, MT, down)

    def attend_back(i, first, last):
        if first == 0:
            def d_mixed(r, _):
                here = pl.ds(r, MT)
                dmix[i, here, :] = dot_nt(dmg[i, here, :], wo[...].reshape(256, D)).astype(BF)
            tiles(ROWS, MT, d_mixed)
            mixt[...] = qkv[i, :, 256:512].astype(F32).T.astype(BF)
        lane = lax.broadcasted_iota(jnp.int32, (1, 256), 1) // HEAD_DIM

        def one_head(h, _):
            own = lane == h
            chances = probs[i, h]
            d_value = dot_nn(chances, dmix[i])
            dqkv[i, :, 512:768] = jnp.where(own, d_value.astype(BF), dqkv[i, :, 512:768])
            valued = jnp.where(own, qkv[i, :, 512:768], jnp.zeros((), BF))
            d_chances = dot_nt(valued, dmix[i])
            wide = chances.astype(F32)
            d_scores = wide * (d_chances - jnp.sum(wide * d_chances, axis=0, keepdims=True))
            d_scores = d_scores.astype(BF)
            d_key = dot_nn(d_scores, qkv[i, :, 0:256]) * HEAD_DIM ** -0.5
            dqkv[i, :, 256:512] = jnp.where(own, d_key.astype(BF), dqkv[i, :, 256:512])
            here = pl.ds(pl.multiple_of(h * HEAD_DIM, HEAD_DIM), HEAD_DIM)
            mixt[here, :] = (dot_nn(mixt[here, :], d_scores) * HEAD_DIM ** -0.5).astype(BF)
        lax.fori_loop(first, last, one_head, None)
        if last == HEADS_DEV:
            dqkv[i, :, 0:256] = mixt[...].astype(F32).T.astype(BF)

    def out_presum(i):
        arrived(("y", "c0", i), rc2.at[i, 0], core)
        arrived(("y", "c1", i), rc2.at[i, 1], core)

        def body(r, _):
            mine = pl.ds(r, 32)
            here = pl.ds(pl.multiple_of(s * TOK + r, 32), 32)
            there = pl.ds(pl.multiple_of(s_x * TOK + r, 32), 32)
            total = part[i, here, :].astype(F32) + rc2[i, 0, mine, :].astype(F32)
            hid[i, mine, :] = hid[i, mine, :] + (total + down_bias)
            total = part[i, there, :].astype(F32) + rc2[i, 1, mine, :].astype(F32)
            rc2[i, 1, mine, :] = total.astype(BF)
        tiles(TOK, 32, body, unroll=True)

    def d_normed(i):
        def body(r, _):
            here = pl.ds(r, MT)
            act[i, here, :] = dot_nt(dqkv[i, here, :], wq[...].reshape(D, 768)).astype(BF)
        tiles(ROWS, MT, body)
        rs4_a("da", i, rc)

    ag4_forward("db", dmg, 0)
    ag4_end("db", dmg, 0)
    for i in range(2):
        rs4_a("y", i, rc2)
    attend_back(0, 0, 4)
    reduce_step()
    ag4_forward("db", dmg, 1)
    d_normed(0)
    ag4_end("db", dmg, 1)
    copy_d = rsw_end("d", gd, rzd, gd_o)
    attend_back(1, 0, 2)
    rs4_b("da", 0, rc, rx)
    attend_back(1, 2, 4)
    reduce_step()
    d_normed(1)
    weight_grad(xg, dqkv, gq)
    rs4_b("da", 1, rc, rx)
    value = dot_tn(mixed[...].reshape(2 * ROWS, 256), dmg[...].reshape(2 * ROWS, D))
    go[...] = value.astype(BF).reshape(2, 128, D)
    reduce_add("o", go, ryo, rzo)
    reduce_add("q", gq, ryq, rzq)
    reduce_step()
    for i in range(2):
        out_presum(i)
        send("y", ("y", "x", i), rc2.at[i, 1], rx2.at[i], xdev)
    reduce_step()

    n_gb = [ix("gob", d) for d in range(3)]

    def out_final_copy(d):
        return pltpu.make_async_remote_copy(
            src_ref=go.at[y], dst_ref=go_o, send_sem=ssem.at[n_gb[d - 1]], recv_sem=rsem.at[n_gb[0]],
            device_id=(lax.rem(s + d, 4), j), device_id_type=MESH_ID)
    n_ol = local.setdefault("go", len(local))

    sgs[...] = jnp.zeros_like(sgs)

    def place(row, total):
        for b in range(NSH):
            sgs[b, pl.ds(row, 1), :] = total[:, 128 * b:128 * b + 128]

    def flat(value):
        return jnp.sum(value, axis=0, keepdims=True)
    place(4, flat(sums[2]))
    place(5, flat(sums[0]))
    place(6, flat(sums[1]))
    place(7, flat(sums[3]))
    d_query_sum = jnp.sum(dqkv[0, :, 0:256].astype(F32) + dqkv[1, :, 0:256].astype(F32), axis=0, keepdims=True)
    d_value_sum = jnp.sum(dqkv[0, :, 512:768].astype(F32) + dqkv[1, :, 512:768].astype(F32), axis=0, keepdims=True)
    for b in range(2):
        sgs[2 * zs + b, pl.ds(2, 1), :] = d_query_sum[:, 128 * b:128 * b + 128]
        sgs[2 * zs + b, pl.ds(3, 1), :] = d_value_sum[:, 128 * b:128 * b + 128]
    up_sum = flat(du_sum)
    row_at = lax.broadcasted_iota(jnp.int32, (8, 128), 0)
    for b in range(NSH):
        wide = jnp.broadcast_to(up_sum[:, 128 * b:128 * b + 128], (8, 128))
        sgs[b, 8:16, :] = jnp.where(row_at == s, wide, 0.0)
    sums_a = (zero8, zero8)
    for i in range(2):
        rs4_wait("da", i, rc, rx)

        def d_input(r, carry, i=i):
            mine = pl.ds(r, 32)
            incoming = rs4_sum(i, r, rc, rx, act)
            scaled, inverse = normal(xin[i, mine, :].astype(F32))
            value = dhid[i, mine, :] + normal_back(incoming, scaled, inverse, attn_gain)
            dx_o[i, mine, :] = value.astype(BF)
            return carry[0] + fold(incoming * scaled), carry[1] + fold(incoming)
        sums_a = tiles(TOK, 32, d_input, sums_a, unroll=True)
        if i == 0:
            rsw_forward("d", gd_o)
            reduce_step()

    place(0, flat(sums_a[0]))
    place(1, flat(sums_a[1]))
    for d in range(1, NSH):
        send("sg", ("sg", d), sgs.at[lax.rem(j + d, NSH)], sg1.at[d - 1], (s, lax.rem(j + d, NSH)))

    copy_u = rsw_end("u", gu, rzu, gu_o)
    reduce_step(2)

    @pl.when(z == zs)
    def _():
        for slot in range(3):
            pltpu.make_async_remote_copy(
                src_ref=go.at[y], dst_ref=rzo.at[slot], send_sem=ssem.at[n_gs], recv_sem=rsem.at[n_gz[slot]],
                device_id=(s, zj(1)), device_id_type=MESH_ID).wait_recv()

        def add(r, _):
            total = go[y, pl.ds(r, 32), :].astype(F32)
            for slot in range(3):
                total = total + rzo[slot, pl.ds(r, 32), :].astype(F32)
            go[y, pl.ds(r, 32), :] = total.astype(BF)
        tiles(128, 32, add, unroll=True)
        pltpu.make_async_copy(go.at[y], go_o, lsem.at[n_ol]).start()
        for d in (1, 2, 3):
            out_final_copy(d).start()

    for d in range(1, NSH):
        jf = lax.rem(j + NSH - d, NSH)
        arrived(("sg", d), sg1.at[d - 1], (s, jf))
    total = sgs[j]
    for d in range(1, NSH):
        total = total + sg1[d - 1]
    sg2[0] = total
    for d in range(1, NSEQ):
        send("sg", ("sh", d), sg2.at[0], sg2.at[d], (lax.rem(s + d, NSEQ), j))
    for i in range(2):
        arrived(("y", "x", i), rx2.at[i], xdev)

        def last(r, _, i=i):
            mine = pl.ds(r, 32)
            out_o[i, mine, :] = (hid[i, mine, :] + rx2[i, mine, :].astype(F32)).astype(BF)
        tiles(TOK, 32, last, unroll=True)
    reduce_step(len(flying) + len(waiting))
    assert not waiting and not flying
    rsw_forward("u", gu_o)
    copy_q = rsw_end("q", gq, rzq, gq_o)
    for d in range(1, NSEQ):
        arrived(("sh", d), sg2.at[d], (lax.rem(s + NSEQ - d, NSEQ), j))
    sg_o[...] = sg2[0] + sg2[1] + sg2[2] + sg2[3]
    rsw_forward("q", gq_o)
    rsw_done("d", gd_o)
    rsw_done("u", gu_o)
    rsw_done("q", gq_o)

    @pl.when(z == zs)
    def _():
        for d in (1, 2, 3):
            out_final_copy(d).wait_send()
        pltpu.make_async_copy(go.at[y], go_o, lsem.at[n_ol]).wait()

    @pl.when(z != zs)
    def _():
        out_final_copy(1).wait_recv()
        out_grad_copy(0).wait_send()
    for copy in (copy_d, copy_u, copy_q):
        copy.wait()

    @pl.when(z == zs)
    def _():
        for d in (1, 2, 3):
            out_copy(d).wait_send()
    for tag in list(pending):
        sent(tag)

def widen_kernel(
    result, d_input, gq, go, gu, gd, small,
    output, input_grad, attn_gain, attn_shift, qkv, query, value, out, out_b, mlp_gain, mlp_shift, up, up_b, down, down_b,
):
    tok = output.shape[0]
    for i in range(2):
        output[:, i, :] = result[i, 0:tok, :]
        input_grad[:, i, :] = d_input[i, 0:tok, :]
    for at, ref in enumerate((attn_gain, attn_shift, query, value, out_b, mlp_gain, mlp_shift, down_b)):
        ref[...] = small[at]
    for b in range(NSEQ):
        up_b[128 * b:128 * b + 128] = small[8 + b]
        for c in range(3):
            qkv[:, 1024 * c + 256 * b:1024 * c + 256 * b + 256] = gq[(b % 2) * 2 + b // 2, :, 256 * c:256 * c + 256].astype(F32)
        for c in range(8):
            up[:, 512 * c + 128 * b:512 * c + 128 * b + 128] = gu[b, :, 128 * c:128 * c + 128].astype(F32)
        down[128 * b:128 * b + 128, :] = gd[b].astype(F32)
    out[...] = go[...].astype(F32)


def fused_device(
    inputs, key_mask, cotangent, attn_gain, attn_shift, qkv_weight, query_bias, value_bias,
    out_weight, out_bias, mlp_gain, mlp_shift, up_weight, up_bias, down_weight, down_bias,
):
    tok = inputs.shape[1]
    lines = [
        entry.reshape(1, 128)
        for entry in (attn_gain, attn_shift, query_bias, value_bias, out_bias, mlp_gain, mlp_shift, down_bias)
    ]
    vm = pl.BlockSpec(memory_space=pltpu.VMEM)
    hbm = pl.BlockSpec(memory_space=pl.ANY)

    def shape(dims, dtype=BF):
        return jax.ShapeDtypeStruct(dims, dtype)

    outs = pl.pallas_call(
        layer_kernel,
        out_shape=(
            shape((2, TOK, D)), shape((2, TOK, D)), shape((4, 128, 768)), shape((128, D)),
            shape((4, 128, D)), shape((4, 128, D)), shape((16, 128), F32),
        ),
        in_specs=[vm] * 12 + [hbm] * 4,
        out_specs=(vm, vm, hbm, hbm, hbm, hbm, vm),
        scratch_shapes=[
            pltpu.VMEM((2, TOK, D), BF),
            pltpu.VMEM((2, TOK, D), BF),
            pltpu.VMEM((16, 128), F32),
            pltpu.VMEM((ROWS, 8), F32),
            pltpu.VMEM((2, ROWS, D), BF),
            pltpu.VMEM((8, 128, 768), BF),
            pltpu.VMEM((2, 128, D), BF),
            pltpu.VMEM((8, 128, D), BF),
            pltpu.VMEM((8, 128, D), BF),
            pltpu.VMEM((8, 16, 128), F32),
            pltpu.VMEM((2, ROWS, 768), BF),
            pltpu.VMEM((2, ROWS, 768), BF),
            pltpu.VMEM((2, HEADS_DEV, ROWS, ROWS), BF),
            pltpu.VMEM((256, ROWS), BF),
            pltpu.VMEM((2, ROWS, 256), BF),
            pltpu.VMEM((2, ROWS, D), BF),
            pltpu.VMEM((2, 2, TOK, D), BF),
            pltpu.VMEM((2, TOK, D), BF),
            pltpu.VMEM((2, 2, TOK, D), BF),
            pltpu.VMEM((2, TOK, D), BF),
            pltpu.VMEM((2, TOK, D), F32),
            pltpu.VMEM((2, ROWS, D), BF),
            pltpu.VMEM((2, ROWS, D), BF),
            pltpu.VMEM((2, ROWS, D), BF),
            pltpu.VMEM((2, ROWS, D), BF),
            pltpu.VMEM((2, TOK, D), F32),
            pltpu.VMEM((2, ROWS, 256), BF),
            pltpu.VMEM((8, 128, 768), BF),
            pltpu.VMEM((2, 128, D), BF),
            pltpu.VMEM((8, 128, D), BF),
            pltpu.VMEM((8, 128, D), BF),
            pltpu.VMEM((4, 128, 768), BF),
            pltpu.VMEM((128, D), BF),
            pltpu.VMEM((4, 128, D), BF),
            pltpu.VMEM((4, 128, D), BF),
            pltpu.VMEM((3, 128, 768), BF),
            pltpu.VMEM((3, 128, D), BF),
            pltpu.VMEM((3, 128, D), BF),
            pltpu.VMEM((3, 128, D), BF),
            pltpu.VMEM((8, 16, 128), F32),
            pltpu.VMEM((7, 16, 128), F32),
            pltpu.VMEM((4, 16, 128), F32),
            pltpu.SemaphoreType.DMA((160,)),
            pltpu.SemaphoreType.DMA((160,)),
            pltpu.SemaphoreType.DMA((24,)),
        ],
        compiler_params=pltpu.CompilerParams(
            collective_id=0, has_side_effects=True, vmem_limit_bytes=VMEM_LIMIT
        ),
        cost_estimate=pl.CostEstimate(flops=26_000_000_000, bytes_accessed=30_000_000, transcendentals=8_000_000),
    )(inputs.transpose(1, 0, 2), cotangent.transpose(1, 0, 2), key_mask, *lines, up_bias.reshape(NSEQ, 128), qkv_weight, out_weight, up_weight, down_weight)
    out, d_input, gq, go, gu, gd, small = outs
    line = shape((128,), F32)
    grads = pl.pallas_call(
        widen_kernel,
        out_shape=(
            shape((tok, 2, D)), shape((tok, 2, D)), line, line, shape((128, 3 * D), F32), line, line, shape((128, D), F32), line, line, line,
            shape((128, 4 * D), F32), shape((512,), F32), shape((512, D), F32), line,
        ),
        in_specs=[vm] * 7,
        out_specs=(vm,) * 15,
        compiler_params=pltpu.CompilerParams(vmem_limit_bytes=WIDEN_LIMIT),
    )(out, d_input, gq, go, gu, gd, small)
    return (grads[0].transpose(1, 0, 2), grads[1].transpose(1, 0, 2)) + tuple(grads[2:])


def solution(mesh):
    in_specs = (
        P("shard", "seq", None),
        P("shard", None),
        P("shard", "seq", None),
        P("shard"),
        P("shard"),
        P("shard", None),
        P("shard"),
        P("shard"),
        P("shard", None),
        P("shard"),
        P("shard"),
        P("shard"),
        P("shard", None),
        P("shard"),
        P("shard", None),
        P("shard"),
    )
    out_specs = (
        P("shard", "seq", None),
        P("shard", "seq", None),
        P("shard"),
        P("shard"),
        P("shard", None),
        P("shard"),
        P("shard"),
        P("shard", None),
        P("shard"),
        P("shard"),
        P("shard"),
        P("shard", None),
        P("shard"),
        P("shard", None),
        P("shard"),
    )
    fits = dict(mesh.shape) == {"seq": NSEQ, "shard": NSH}
    return jax.shard_map(
        fused_device if fits else per_device, mesh=mesh, in_specs=in_specs, out_specs=out_specs, check_vma=False
    )
```
